32 devices in a mesh: dp: 4 (over y, core), ctx: 8 (over z, x), tp: 1.
Axes of the slice: x: 2, y: 2, z: 4, core: 2. Of those that a mesh axis runs over, the one named last changes fastest.
Arguments:
- queries: bfloat16 [4, 1024, 4096], P('dp', 'ctx', 'tp'), may hold values from -6 to 6
- keys: bfloat16 [4, 1024, 512], P('dp', 'ctx', 'tp'), may hold values from -6 to 6
- values: bfloat16 [4, 1024, 512], P('dp', 'ctx', 'tp'), may hold values from -6 to 6
- out_grad: bfloat16 [4, 1024, 4096], P('dp', 'ctx', 'tp'), may hold values from -6 to 6
- mixed_grad: bfloat16 [4096, 2048], P(('dp', 'ctx'), 'tp'), may hold values from -6 to 6
- expert_ids: int32 [4096, 8], P(('dp', 'ctx')), may hold values from 0 to 31, all different within a row; in each aligned block of 128 rows (0 to 127, 128 to 255, ...) at most 40 rows name the same one
- combine: bfloat16 [4096, 8], P(('dp', 'ctx')), may hold values from 0.049804688 to 1
- w_down: bfloat16 [32, 1536, 2048], P(('dp', 'ctx'), 'tp'), may hold values from -0.125 to 0.125
Outputs:
- query_grad: bfloat16 [4, 1024, 4096], P('dp', 'ctx', 'tp')
- key_grad: bfloat16 [4, 1024, 512], P('dp', 'ctx', 'tp')
- value_grad: bfloat16 [4, 1024, 512], P('dp', 'ctx', 'tp')
- hidden_grad: bfloat16 [32, 32, 40, 1536], P(('dp', 'ctx'), None, None, 'tp')
The draws below stay inside these ranges and needn't reach their ends.
Inputs may be any that keep to these rules, and one draw needn't show every extreme that they name: `expert_ids`: each row names 8 distinct experts. Within each aligned block of 128 rows no expert is named more than 40 times, a bound that some block reaches.
All inputs are finite; a program needn't handle non-finite values.
Results may differ from the reference program's by a relative error of at most 0.0071.
Values may be sent and summed in bfloat16 or wider, within the bound.
No kernel may reach another device: no remote copies, remote signals or barrier semaphores. Data moves between devices by JAX's collectives and lax.ppermute only.
A program may use at most 128 MiB of HBM per device.

```python
import math
import jax
import jax.numpy as jnp
import numpy as np
from jax import lax

TOK_DEV = 128
HEADS = 32
KV_HEADS = 4
HEAD_DIM = 128
FEAT = 2048
HID = 1536
TOPK = 8
EXPERTS = 32
MOST = 40
SEQS = 4
LEN = 1024
TOKENS = 4096


def draw_queries(key, part):
    key = jax.random.fold_in(key, 11)
    group = HEADS // KV_HEADS
    shape = (SEQS, LEN, KV_HEADS, group, HEAD_DIM)
    drawn = jax.random.truncated_normal(key, -6.0, 6.0, shape, jnp.float32)
    return drawn.reshape(SEQS, LEN, HEADS * HEAD_DIM).astype(jnp.bfloat16)


def draw_keys(key, part):
    key = jax.random.fold_in(key, 23)
    shape = (SEQS, LEN, KV_HEADS, HEAD_DIM)
    drawn = jax.random.truncated_normal(key, -6.0, 6.0, shape, jnp.float32)
    return drawn.reshape(SEQS, LEN, KV_HEADS * HEAD_DIM).astype(jnp.bfloat16)


def block_levels(stream_key, dims, shards, smallest, largest):
    gain, own = 1.0, jax.random.fold_in(stream_key, 6)
    for dim, parts in shards:
        heights = jnp.exp(jax.random.uniform(jax.random.fold_in(own, dim), (parts,), jnp.float32, smallest / len(shards), largest / len(shards)))
        gain = gain * jnp.repeat(heights, dims[dim] // parts).reshape([-1 if axis == dim else 1 for axis in range(len(dims))])
    return gain


def assign_block(key, own, number, rows, count, top, bound, lean):
    ranking = jax.random.permutation(key, count)
    crowded, usual = portions_of(count, rows * top, bound, lean, True), portions_of(count, rows * top, bound, lean, False)
    places = jnp.arange(count)

    def named(tallies, offset_by):
        used = int((tallies > 0).sum())
        fixed = max(1, used // 4)
        passed = fixed + (places - fixed + offset_by * (used - fixed)) % max(1, count - fixed)
        return jnp.zeros((count,), jnp.int32).at[ranking[jnp.where(places < fixed, places, passed)]].set(jnp.asarray(tallies, jnp.int32))

    tallies = jnp.where(number % 4 == 0, named(crowded, number // 4), named(usual, number - number // 4 - 1))
    mixed = jax.random.permutation(jax.random.fold_in(own, 3), count)
    source_of, receiver = mixed[0:count // 2 * 2:2], mixed[1:count // 2 * 2:2]
    slack = jnp.minimum(tallies[source_of] - 1, bound - tallies[receiver]) // 2
    slack = jnp.where((source_of == ranking[0]) | (receiver == ranking[0]) | (tallies[receiver] == 0), 0, jnp.maximum(slack, 0))
    passed = jax.random.randint(jax.random.fold_in(own, 4), (count // 2,), 0, 1 << 20) % (slack + 1)
    tallies = tallies.at[source_of].add(-passed).at[receiver].add(passed)
    labels = jnp.searchsorted(jnp.cumsum(tallies), jnp.arange(rows * top), side="right").astype(jnp.int32)
    listing = labels.reshape(top, rows).T
    listing = listing[jax.random.permutation(jax.random.fold_in(own, 1), rows)]
    offset_by = jax.random.randint(jax.random.fold_in(own, 2), (rows, 1), 0, top)
    return jnp.take_along_axis(listing, (jnp.arange(top)[None, :] + offset_by) % top, axis=1)


def portions_of(number_of, total, reach, slope, full):
    portions = [(1 << 20) // math.isqrt(grade ** slope) + 1 for grade in range(1, number_of + 1)]
    largest = reach if full else min(reach, max(-(-total // number_of), total * portions[0] // sum(portions)))
    least = 1 if total - largest >= number_of - 1 else 0
    given, spare = [largest] + [least] * (number_of - 1), total - largest - least * (number_of - 1)
    while spare > 0:
        candidates = [i for i in range(1, number_of) if given[i] < largest] or [i for i in range(1, number_of) if given[i] < reach]
        pool, remaining = sum([portions[i] for i in candidates]), spare
        for i in candidates:
            addition = min(reach - given[i], max(1, remaining * portions[i] // pool), spare)
            given[i] = given[i] + addition
            spare = spare - addition
    return np.array(given)


def scatter_about(stream_key, shape, deviation, limit, shards=(), held_as=jnp.bfloat16):
    array = jax.random.normal(stream_key, shape, jnp.float32) * deviation
    if len(shards) > 0:
        array = block_levels(stream_key, shape, shards, -0.22, 0.18) * array
    return jnp.clip(array, min=-limit, max=limit).astype(held_as)


def setup_inputs(seed: int = 0) -> dict:
    key_of = jax.random.split(jax.random.key(seed), 9)
    queries = draw_queries(jax.random.fold_in(key_of[8], 71), 0)
    keys = draw_keys(jax.random.fold_in(key_of[8], 71), 0)
    values = scatter_about(key_of[2], (SEQS, LEN, KV_HEADS * HEAD_DIM), 1.0, 6.0, ((0, 4), (1, 8)))
    out_grad = scatter_about(key_of[3], (SEQS, LEN, HEADS * HEAD_DIM), 1.0, 6.0, ((0, 4), (1, 8)))
    mixed_grad = scatter_about(key_of[4], (TOKENS, FEAT), 1.0, 6.0, ((0, 32),))
    expert_ids_keys = jax.random.split(jax.random.fold_in(key_of[5], 1), TOKENS // TOK_DEV)
    expert_ids_turns = jax.random.permutation(jax.random.fold_in(key_of[5], 3), TOKENS // TOK_DEV)
    expert_ids = jax.vmap(lambda own, number: assign_block(jax.random.fold_in(key_of[5], 2), own, number, TOK_DEV, EXPERTS, TOPK, MOST, 2))(expert_ids_keys, expert_ids_turns).reshape((TOKENS, TOPK))
    combine = jnp.clip(jnp.exp(math.log(1.0) - 2.9996462 * jax.random.uniform(key_of[6], (TOKENS, TOPK), jnp.float32) ** block_levels(key_of[6], (TOKENS, TOPK), ((0, 32),), -0.2, 0.2)), 0.049804688, 1.0).astype(jnp.bfloat16)
    w_down = scatter_about(key_of[7], (EXPERTS, HID, FEAT), FEAT ** -0.5, 0.125, ((0, 32),))
    return dict(queries=queries, keys=keys, values=values, out_grad=out_grad, mixed_grad=mixed_grad, expert_ids=expert_ids, combine=combine, w_down=w_down)


def group_backward(operands):
    query_heads, grad_heads, key_rows, value_rows = operands
    score_scale = HEAD_DIM ** -0.5
    places = jnp.arange(LEN, dtype=jnp.int32)
    allowed = places[None, :] <= places[:, None]

    def one_head(carry, pair):
        key_total, value_total = carry
        query_rows, grad_rows = pair
        scores = jnp.dot(query_rows, key_rows.T, preferred_element_type=jnp.float32) * score_scale
        scores = jnp.where(allowed, scores, -jnp.inf)
        log_total = jax.nn.logsumexp(scores, axis=1, keepdims=True)
        probs = jnp.where(allowed, jnp.exp(scores - log_total), 0.0)
        grads = jnp.dot(grad_rows, value_rows.T, preferred_element_type=jnp.float32)
        delta = jnp.sum(probs * grads, axis=1, keepdims=True)
        dscore = probs * (grads - delta)
        probs_low = probs.astype(jnp.bfloat16)
        dscore_low = dscore.astype(jnp.bfloat16)
        query_part = (jnp.dot(dscore_low, key_rows, preferred_element_type=jnp.float32) * score_scale).astype(jnp.bfloat16)
        key_total = key_total + jnp.dot(dscore_low.T, query_rows, preferred_element_type=jnp.float32)
        value_total = value_total + jnp.dot(probs_low.T, grad_rows, preferred_element_type=jnp.float32)
        return (key_total, value_total), query_part

    start_totals = (jnp.zeros((LEN, HEAD_DIM), jnp.float32), jnp.zeros((LEN, HEAD_DIM), jnp.float32))
    (key_total, value_total), query_parts = lax.scan(one_head, start_totals, (query_heads, grad_heads))
    return query_parts, (key_total * score_scale).astype(jnp.bfloat16), value_total.astype(jnp.bfloat16)


def attention_backward(queries, keys, values, out_grad):
    group = HEADS // KV_HEADS
    query_groups = queries.reshape(SEQS, LEN, KV_HEADS, group, HEAD_DIM).transpose(0, 2, 3, 1, 4).reshape(SEQS * KV_HEADS, group, LEN, HEAD_DIM)
    grad_groups = out_grad.reshape(SEQS, LEN, KV_HEADS, group, HEAD_DIM).transpose(0, 2, 3, 1, 4).reshape(SEQS * KV_HEADS, group, LEN, HEAD_DIM)
    key_groups = keys.reshape(SEQS, LEN, KV_HEADS, HEAD_DIM).transpose(0, 2, 1, 3).reshape(SEQS * KV_HEADS, LEN, HEAD_DIM)
    value_groups = values.reshape(SEQS, LEN, KV_HEADS, HEAD_DIM).transpose(0, 2, 1, 3).reshape(SEQS * KV_HEADS, LEN, HEAD_DIM)
    query_parts, key_parts, value_parts = lax.map(group_backward, (query_groups, grad_groups, key_groups, value_groups))
    query_grad = query_parts.reshape(SEQS, KV_HEADS, group, LEN, HEAD_DIM).transpose(0, 3, 1, 2, 4).reshape(SEQS, LEN, HEADS * HEAD_DIM)
    key_grad = key_parts.reshape(SEQS, KV_HEADS, LEN, HEAD_DIM).transpose(0, 2, 1, 3).reshape(SEQS, LEN, KV_HEADS * HEAD_DIM)
    value_grad = value_parts.reshape(SEQS, KV_HEADS, LEN, HEAD_DIM).transpose(0, 2, 1, 3).reshape(SEQS, LEN, KV_HEADS * HEAD_DIM)
    return query_grad, key_grad, value_grad


def expert_backward(mixed_grad, expert_ids, combine, w_down):
    blocks = TOKENS // TOK_DEV
    entries = TOK_DEV * TOPK
    id_blocks = expert_ids.reshape(blocks, entries)
    weight_blocks = combine.reshape(blocks, entries).astype(jnp.float32)
    row_blocks = mixed_grad.reshape(blocks, TOK_DEV, FEAT).astype(jnp.float32)
    slot_places = jnp.arange(MOST, dtype=jnp.int32)

    def one_expert(pair):
        expert, weights = pair
        hits = (id_blocks == expert).astype(jnp.int32)
        ranks = jnp.cumsum(hits, axis=1) - 1
        chosen = ((hits[:, None, :] == 1) & (ranks[:, None, :] == slot_places[None, :, None])).astype(jnp.float32)
        token_pick = chosen.reshape(blocks, MOST, TOK_DEV, TOPK).sum(axis=3)
        rows = jnp.einsum("bct,btf->bcf", token_pick, row_blocks)
        slot_weights = jnp.einsum("bce,be->bc", chosen, weight_blocks)
        hidden = jnp.einsum("bcf,hf->bch", rows, weights.astype(jnp.float32))
        return (hidden * slot_weights[:, :, None]).astype(jnp.bfloat16)

    return lax.map(one_expert, (jnp.arange(EXPERTS, dtype=jnp.int32), w_down))


def reference(queries, keys, values, out_grad, mixed_grad, expert_ids, combine, w_down):
    query_grad, key_grad, value_grad = attention_backward(queries, keys, values, out_grad)
    hidden_grad = expert_backward(mixed_grad, expert_ids, combine, w_down)
    return (query_grad, key_grad, value_grad, hidden_grad)
```

```python
import functools
import math

import jax
import jax.numpy as jnp
from jax import lax
from jax.experimental import pallas as pl
from jax.experimental.pallas import tpu as pltpu
from jax.sharding import PartitionSpec as P

HEADS = 32
KV_HEADS = 4
HEAD_DIM = 128
TOPK = 8

masked_score = -1e30
vmem_limit = 56 * 1024 * 1024


def mul(a, b):
    return jnp.dot(a, b, preferred_element_type=jnp.float32)


def attention_kernel(n_blocks, heads_step, rows, n_parts, place, q_ref, do_ref, *refs):
    kv_refs = refs[:n_blocks]
    n_pairs = n_blocks // 2
    dq_ref, dkv_refs = refs[-11 - n_pairs], refs[-10 - n_pairs : -10]
    kv_s, kt_s, q_s, do_s, qt_s, dot_s, s_s, dp_s, dkv_s, dqt_s = refs[-10:]
    part = pl.program_id(1)
    pair = 2 * rows
    width = heads_step * rows
    z, x = place[0], place[1]
    scale = HEAD_DIM ** (-0.5)
    to_exp2 = scale * math.log2(math.e)
    for i, ref in enumerate(kv_refs):
        kv_s[i * rows : (i + 1) * rows, :] = ref[...]
        kt_s[i // 2, :, (i % 2) * rows : (i % 2 + 1) * rows] = ref[:, :HEAD_DIM].T
    for h in range(heads_step):
        lanes = slice(h * HEAD_DIM, (h + 1) * HEAD_DIM)
        here = slice(h * rows, (h + 1) * rows)
        q_s[here, :] = q_ref[:, lanes]
        do_s[here, :] = do_ref[:, lanes]
        qt_s[:, here] = q_ref[:, lanes].T
        dot_s[:, here] = do_ref[:, lanes].T

    def part_of(k):
        return pl.ds(pl.multiple_of(k * pair, pair), pair)

    def scores(k, top, first):
        s = mul(kv_s[part_of(k), :HEAD_DIM], qt_s[...])
        if first:
            key = lax.broadcasted_iota(jnp.int32, (pair, width), 0)
            query = lax.broadcasted_iota(jnp.int32, (pair, width), 1) & (rows - 1)
            bound = jnp.where(key < rows, query, jnp.where(x == 1, pair, -1))
            s = jnp.where(key <= bound, s, masked_score)
        s_s[part_of(k), :] = s
        return jnp.maximum(top, jnp.max(s, axis=0, keepdims=True))

    top = scores(0, jnp.full((1, width), masked_score, jnp.float32), True)
    top = lax.fori_loop(1, z + 1, functools.partial(scores, first=False), top)

    def sums(k, carry):
        total, accum = carry
        dp = mul(kv_s[part_of(k), HEAD_DIM:], dot_s[...])
        e = jnp.exp2((s_s[part_of(k), :] - top) * to_exp2)
        s_s[part_of(k), :] = e
        dp_s[part_of(k), :] = dp
        return (
            total + jnp.sum(e, axis=0, keepdims=True),
            accum + jnp.sum(e * dp, axis=0, keepdims=True),
        )

    zero = jnp.zeros((1, width), jnp.float32)
    total, accum = lax.fori_loop(0, z + 1, sums, (zero, zero))
    share = 1.0 / total
    delta = accum * share
    dqt_s[...] = jnp.zeros_like(dqt_s)

    def grads(k, carry):
        p = s_s[part_of(k), :] * share
        ds = (p * (dp_s[part_of(k), :] - delta)).astype(jnp.bfloat16)
        p = p.astype(jnp.bfloat16)
        dk = mul(ds, q_s[...]) * scale
        dv = mul(p, do_s[...])
        if n_parts > 1:
            dk = dk + jnp.where(part == 0, 0.0, dkv_s[part_of(k), :HEAD_DIM])
            dv = dv + jnp.where(part == 0, 0.0, dkv_s[part_of(k), HEAD_DIM:])
        dkv_s[part_of(k), :HEAD_DIM] = dk
        dkv_s[part_of(k), HEAD_DIM:] = dv
        dqt_s[...] += mul(kt_s[k], ds)
        return carry

    lax.fori_loop(0, z + 1, grads, 0)
    for h in range(heads_step):
        part_t = dqt_s[:, h * rows : (h + 1) * rows] * scale
        dq_ref[:, h * HEAD_DIM : (h + 1) * HEAD_DIM] = part_t.T.astype(jnp.bfloat16)
    for k, ref in enumerate(dkv_refs):
        held = dkv_s[k * pair : (k + 1) * pair, :]
        ref[...] = jnp.where(k <= z, held, 0.0).astype(jnp.bfloat16)


def attention(place, queries, out_grad, kv_blocks, first, count, query_grad, after=()):
    rows, q_width = queries.shape
    n_blocks = len(kv_blocks)
    group = HEADS // KV_HEADS
    keys = n_blocks * rows
    heads_step = max(1, min(group, 2**20 // (keys * rows)))
    n_parts = group // heads_step
    width = heads_step * rows
    q_spec = pl.BlockSpec(
        (rows, heads_step * HEAD_DIM), lambda g, u: (0, (g + first) * n_parts + u)
    )
    kv_spec = pl.BlockSpec((rows, 2 * HEAD_DIM), lambda g, u: (0, g + first))
    part_spec = pl.BlockSpec((2 * rows, 2 * HEAD_DIM), lambda g, u: (0, g))
    part_shape = jax.ShapeDtypeStruct((2 * rows, count * 2 * HEAD_DIM), jnp.bfloat16)
    held = [] if query_grad is None else [query_grad]
    return pl.pallas_call(
        functools.partial(attention_kernel, n_blocks, heads_step, rows, n_parts),
        grid=(count, n_parts),
        in_specs=[pl.BlockSpec(memory_space=pltpu.SMEM), q_spec, q_spec]
        + [kv_spec] * n_blocks
        + [pl.BlockSpec(memory_space=pl.ANY)] * (len(held) + len(after)),
        out_specs=[q_spec] + [part_spec] * (n_blocks // 2),
        out_shape=[jax.ShapeDtypeStruct((rows, q_width), jnp.bfloat16)]
        + [part_shape] * (n_blocks // 2),
        scratch_shapes=[
            pltpu.VMEM((keys, 2 * HEAD_DIM), jnp.bfloat16),
            pltpu.VMEM((n_blocks // 2, HEAD_DIM, 2 * rows), jnp.bfloat16),
            pltpu.VMEM((width, HEAD_DIM), jnp.bfloat16),
            pltpu.VMEM((width, HEAD_DIM), jnp.bfloat16),
            pltpu.VMEM((HEAD_DIM, width), jnp.bfloat16),
            pltpu.VMEM((HEAD_DIM, width), jnp.bfloat16),
            pltpu.VMEM((keys, width), jnp.float32),
            pltpu.VMEM((keys, width), jnp.float32),
            pltpu.VMEM((keys, 2 * HEAD_DIM), jnp.float32),
            pltpu.VMEM((HEAD_DIM, width), jnp.float32),
        ],
        input_output_aliases={3 + n_blocks: 0} if held else {},
        compiler_params=pltpu.CompilerParams(
            vmem_limit_bytes=vmem_limit, dimension_semantics=("arbitrary", "arbitrary")
        ),
        cost_estimate=pl.CostEstimate(
            flops=10 * rows * keys * group * count * HEAD_DIM,
            bytes_accessed=6 * rows * group * count * HEAD_DIM + 8 * keys * count * HEAD_DIM,
            transcendentals=rows * keys * group * count,
        ),
        name="attention_backward",
    )(place, queries, out_grad, *kv_blocks, *held, *after)


def fold_kernel(n_z, groups, rows, *refs):
    own_ref, other_ref = refs[-2:]
    first = 0
    for i in range(groups):
        parts = refs[i * n_z : (i + 1) * n_z]
        total = parts[0][...].astype(jnp.float32)
        for ref in parts[1:]:
            total = total + ref[...].astype(jnp.float32)
        lanes = slice(first, first + total.shape[1])
        own_ref[:, lanes] = total[:rows]
        other_ref[:, lanes] = total[rows:].astype(jnp.bfloat16)
        first += total.shape[1]


def fold(parts, rows, after=()):
    width = sum(group[0].shape[1] for group in parts)
    return pl.pallas_call(
        functools.partial(fold_kernel, len(parts[0]), len(parts), rows),
        in_specs=[pl.BlockSpec(memory_space=pltpu.VMEM)] * (len(parts) * len(parts[0]))
        + [pl.BlockSpec(memory_space=pl.ANY)] * len(after),
        out_shape=[
            jax.ShapeDtypeStruct((rows, width), jnp.float32),
            jax.ShapeDtypeStruct((rows, width), jnp.bfloat16),
        ],
        compiler_params=pltpu.CompilerParams(vmem_limit_bytes=vmem_limit),
        name="fold",
    )(*[part for group in parts for part in group], *after)


def finish_kernel(own_ref, got_ref, key_ref, value_ref):
    total = (own_ref[...] + got_ref[...].astype(jnp.float32)).astype(jnp.bfloat16)
    for g in range(total.shape[1] // (2 * HEAD_DIM)):
        lanes = slice(g * HEAD_DIM, (g + 1) * HEAD_DIM)
        key_ref[0, :, lanes] = total[:, 2 * g * HEAD_DIM : (2 * g + 1) * HEAD_DIM]
        value_ref[0, :, lanes] = total[:, (2 * g + 1) * HEAD_DIM : (2 * g + 2) * HEAD_DIM]


def finish(own, got):
    shape = jax.ShapeDtypeStruct((1, own.shape[0], own.shape[1] // 2), jnp.bfloat16)
    return pl.pallas_call(
        finish_kernel,
        out_shape=[shape, shape],
        compiler_params=pltpu.CompilerParams(vmem_limit_bytes=vmem_limit),
        name="finish",
    )(own, got)


def join_kernel(
    n_z, n_dp, key_ref, value_ref, rows_ref, ids_ref, combine_ref, kv_ref, ext_ref
):
    for g in range(kv_ref.shape[1] // (2 * HEAD_DIM)):
        lanes = slice(g * HEAD_DIM, (g + 1) * HEAD_DIM)
        kv_ref[:, 2 * g * HEAD_DIM : (2 * g + 1) * HEAD_DIM] = key_ref[0, :, lanes]
        kv_ref[:, (2 * g + 1) * HEAD_DIM : (2 * g + 2) * HEAD_DIM] = value_ref[0, :, lanes]
    tokens, feat = rows_ref.shape
    lines = 4 * n_dp
    line = lax.broadcasted_iota(jnp.int32, (n_z * lines, tokens), 0)
    kind = line % lines
    member = kind % (2 * n_dp)
    expert = (member // 2) * (2 * n_z) + line // lines * 2 + member % 2
    hits = jnp.zeros((n_z * lines, tokens), jnp.float32)
    weights = jnp.zeros((n_z * lines, tokens), jnp.float32)
    combine = combine_ref[...].astype(jnp.float32)
    for k in range(TOPK):
        hit = ids_ref[k : k + 1, :] == expert
        hits = hits + jnp.where(hit, 1.0, 0.0)
        weights = weights + jnp.where(hit, combine[k : k + 1, :], 0.0)
    before = lax.broadcasted_iota(jnp.int32, (tokens, tokens), 0) < lax.broadcasted_iota(
        jnp.int32, (tokens, tokens), 1
    )
    ranks = mul(hits.astype(jnp.bfloat16), jnp.where(before, 1.0, 0.0).astype(jnp.bfloat16))
    table = jnp.where(kind < 2 * n_dp, jnp.where(hits > 0.0, ranks, -1.0), weights)
    ext_ref[:tokens, :] = rows_ref[...]
    squares = [table[i * lines : (i + 1) * lines] for i in range(n_z)]
    squares += [jnp.zeros((lines, tokens), jnp.float32)] * (feat // tokens - n_z)
    ext_ref[tokens:, :] = jnp.concatenate(squares, axis=1).astype(jnp.bfloat16)


def join(keys, values, full_rows, ids, combine, n_z, n_dp):
    rows, width = keys.shape[1:]
    tokens, feat = full_rows.shape
    return pl.pallas_call(
        functools.partial(join_kernel, n_z, n_dp),
        out_shape=[
            jax.ShapeDtypeStruct((rows, 2 * width), jnp.bfloat16),
            jax.ShapeDtypeStruct((tokens + 4 * n_dp, feat), jnp.bfloat16),
        ],
        compiler_params=pltpu.CompilerParams(vmem_limit_bytes=vmem_limit),
        name="join",
    )(keys, values, full_rows, ids.T, combine.T)


def pick_kernel(sizes, n_dp, capacity, place, *refs):
    pieces = sum(sizes)
    out_ref, pick_s = refs[-2:]
    bounds = [sum(sizes[:i]) for i in range(len(sizes) + 1)]

    def added(group, i):
        total = group[bounds[i]][...]
        for ref in group[bounds[i] + 1 : bounds[i + 1]]:
            total = total + ref[...]
        return total

    @pl.when(pl.program_id(0) == 0)
    def _():
        for i in range(len(sizes)):
            tokens = refs[pieces].shape[0]
            table = refs[bounds[i]][:, pl.ds(pl.multiple_of(place[0] * tokens, tokens), tokens)]
            for ref in refs[bounds[i] + 1 : bounds[i + 1]]:
                table = table + ref[:, pl.ds(pl.multiple_of(place[0] * tokens, tokens), tokens)]
            table = table.astype(jnp.float32)
            slot = lax.broadcasted_iota(jnp.int32, (capacity, tokens), 0).astype(jnp.float32)
            picks = [
                jnp.where(
                    slot == table[q : q + 1, :], table[2 * n_dp + q : 2 * n_dp + q + 1, :], 0.0
                )
                for q in range(2 * n_dp)
            ]
            pick_s[i] = jnp.concatenate(picks, axis=0).astype(jnp.bfloat16)

    results = [mul(pick_s[i], added(refs[pieces : 2 * pieces], i)) for i in range(len(sizes))]
    for q in range(2 * n_dp):
        here = slice(q * capacity, (q + 1) * capacity)
        total = jnp.concatenate([part[here] for part in results], axis=0)
        size = len(sizes) * capacity
        out_ref[q * size : (q + 1) * size, :] = total.astype(jnp.bfloat16)


def pick_rows(place, blocks, n_dp, capacity, after=()):
    arrays = [array for block in blocks for array in block]
    sizes = [len(block) for block in blocks]
    lines, feat = 4 * n_dp, arrays[0].shape[1]
    tokens = arrays[0].shape[0] - lines
    step = math.gcd(feat, 1024)
    out_rows = len(blocks) * 2 * n_dp * capacity
    return pl.pallas_call(
        functools.partial(pick_kernel, sizes, n_dp, capacity),
        grid=(feat // step,),
        in_specs=[pl.BlockSpec(memory_space=pltpu.SMEM)]
        + [pl.BlockSpec((lines, feat), lambda f: (tokens // lines, 0))] * len(arrays)
        + [pl.BlockSpec((tokens, step), lambda f: (0, f))] * len(arrays)
        + [pl.BlockSpec(memory_space=pl.ANY)] * len(after),
        out_specs=pl.BlockSpec((out_rows, step), lambda f: (0, f)),
        out_shape=jax.ShapeDtypeStruct((out_rows, feat), jnp.bfloat16),
        scratch_shapes=[pltpu.VMEM((len(blocks), 2 * n_dp * capacity, tokens), jnp.bfloat16)],
        compiler_params=pltpu.CompilerParams(vmem_limit_bytes=vmem_limit),
        cost_estimate=pl.CostEstimate(
            flops=2 * out_rows * tokens * feat,
            bytes_accessed=2 * (out_rows + len(arrays) * tokens) * feat,
            transcendentals=0,
        ),
        name="pick_rows",
    )(place, *arrays, *arrays, *after)


def expert_kernel(ks, n_z, n_dp, capacity, slots, place, rows_ref, w_ref, *refs):
    out_ref, out_s, sem = refs[-3:]
    step, steps = pl.program_id(0), out_s.shape[0]
    width = out_s.shape[-1]
    blocks = [(q, k) for q in range(2 * n_dp) for k in ks]
    result = lax.dot_general(
        rows_ref[...], w_ref[0], (((1,), (1,)), ((), ())), preferred_element_type=jnp.float32
    )
    for i in range(len(blocks)):
        out_s[step, i] = result[i * capacity : i * capacity + slots].astype(jnp.bfloat16)

    def copies(at):
        z = place[0]
        for i, (q, k) in enumerate(blocks):
            source = (q // 2) * (2 * n_z) + (z ^ k) * 2 + q % 2
            lanes = pl.ds(pl.multiple_of(at * width, width), width)
            yield pltpu.make_async_copy(
                out_s.at[at, i], out_ref.at[0, source, :, lanes], sem.at[at, i]
            )

    for copy in copies(step):
        copy.start()

    @pl.when(step == steps - 1)
    def _():
        for at in range(steps):
            for copy in copies(at):
                copy.wait()


def expert_rows(place, rows, ks, w_down, n_z, n_dp, capacity, slots, hidden_grad, after=()):
    hid, feat = w_down.shape[1:]
    step = math.gcd(hid, 512)
    held = [] if hidden_grad is None else [hidden_grad]
    return pl.pallas_call(
        functools.partial(expert_kernel, ks, n_z, n_dp, capacity, slots),
        grid=(hid // step,),
        in_specs=[
            pl.BlockSpec(memory_space=pltpu.SMEM),
            pl.BlockSpec(rows.shape, lambda n: (0, 0)),
            pl.BlockSpec((1, step, feat), lambda n: (0, n, 0)),
        ]
        + [pl.BlockSpec(memory_space=pl.ANY)] * (len(held) + len(after)),
        out_specs=pl.BlockSpec(memory_space=pl.ANY),
        out_shape=jax.ShapeDtypeStruct((1, n_dp * 2 * n_z, slots, hid), jnp.bfloat16),
        scratch_shapes=[
            pltpu.VMEM((hid // step, rows.shape[0] // capacity, slots, step), jnp.bfloat16),
            pltpu.SemaphoreType.DMA((hid // step, rows.shape[0] // capacity)),
        ],
        input_output_aliases={3: 0} if held else {},
        compiler_params=pltpu.CompilerParams(vmem_limit_bytes=vmem_limit),
        cost_estimate=pl.CostEstimate(
            flops=2 * rows.shape[0] * feat * hid,
            bytes_accessed=2 * hid * feat + 2 * rows.shape[0] * (feat + hid),
            transcendentals=0,
        ),
        name="expert_rows",
    )(place, rows, w_down, *held, *after)


def per_device(queries, keys, values, out_grad, mixed_grad, expert_ids, combine, w_down):
    rows_dev = queries.shape[1]
    kv_local = keys.shape[2] // HEAD_DIM
    n_ctx, n_dp = lax.axis_size("ctx"), lax.axis_size("dp")
    n_z = n_ctx // 2
    position = lax.axis_index("ctx")
    place = jnp.stack([position >> 1, position & 1]).astype(jnp.int32)
    token_rows = expert_ids.shape[0]
    experts_all = n_dp * n_ctx
    slots = min(
        token_rows,
        max(
            2,
            token_rows * TOPK * 5 // (4 * experts_all),
            (token_rows * TOPK + experts_all - 1) // experts_all,
        ),
    )
    capacity = -(-slots // 8) * 8
    full_rows = mixed_grad
    if lax.axis_size("tp") > 1:
        full_rows = lax.all_gather(mixed_grad, "tp", axis=1, tiled=True)
    own, own_rows = join(keys, values, full_rows, expert_ids, combine, n_z, n_dp)

    columns = [own] + [
        lax.ppermute(own, "ctx", [(i, i + 2 * k) for i in range(n_ctx - 2 * k)])
        for k in range(1, n_z)
    ]
    blocks = []
    for k, column in enumerate(columns):
        pairs = [(i, i ^ 1) for i in range(2 * k, n_ctx) if k > 0 or i % 2 == 0]
        blocks += [column, lax.ppermute(column, "ctx", pairs)]

    plane_groups = [
        [d * n_ctx + 2 * i + j for d in range(n_dp) for j in range(2)] for i in range(n_z)
    ]
    def along_z(array, targets):
        pairs = [(2 * i + x, 2 * j + x) for i, j in targets for x in range(2)]
        return lax.ppermute(array, "ctx", pairs)

    near = along_z(own_rows, [(i, i ^ 1) for i in range(n_z)])
    if n_z == 4:
        across = along_z(own_rows, [(1, 2), (2, 1)])
        across_near = along_z(near, [(1, 2), (2, 1)])
        outward = along_z(across, [(1, 0), (2, 3)])
        outward_near = along_z(across_near, [(1, 0), (2, 3)])
        far = [(across_near, outward), (across, outward_near)]
        early, late = (across,), (across_near, outward)
    else:
        far = [(along_z(own_rows, [(i, i ^ k) for i in range(n_z)]),) for k in range(2, n_z)]
        early, late = (), ()

    def exchange(arrays, after):
        picked = pick_rows(place, arrays, n_dp, capacity, after)
        return picked, lax.all_to_all(
            picked,
            ("dp", "ctx"),
            split_axis=0,
            concat_axis=0,
            tiled=True,
            axis_index_groups=plane_groups,
        )

    picked, got_near = exchange([(own_rows,), (near,)], (*blocks, *early))

    counts = [1] if kv_local == 1 else [kv_local // 2, kv_local - kv_local // 2]
    query_grad, gathered, first = None, [], 0
    for count in counts:
        after = (picked,) if first == 0 else late
        query_grad, *parts = attention(
            place, queries[0], out_grad[0], blocks, first, count, query_grad, after
        )
        first += count
        gathered.append(
            [parts[0]]
            + [
                lax.ppermute(parts[k], "ctx", [(i, i - 2 * k) for i in range(2 * k, n_ctx)])
                for k in range(1, n_z)
            ]
        )
    picked, got_far = exchange(far, (query_grad, *(gathered[0] if len(counts) > 1 else ())))
    sizes = (n_z, n_dp, capacity, slots)
    hidden_grad = expert_rows(place, got_near, (0, 1), w_down, *sizes, None, (picked,))
    total, other = fold(gathered, rows_dev, (hidden_grad,))
    got = lax.ppermute(other, "ctx", [(i, i ^ 1) for i in range(n_ctx)])
    key_grad, value_grad = finish(total, got)
    hidden_grad = expert_rows(
        place, got_far, tuple(range(2, n_z)), w_down, *sizes, hidden_grad, (key_grad,)
    )
    return (query_grad[None], key_grad, value_grad, hidden_grad)


def solution(mesh):
    placed = (
        P("dp", "ctx", "tp"),
        P("dp", "ctx", "tp"),
        P("dp", "ctx", "tp"),
        P("dp", "ctx", "tp"),
        P(("dp", "ctx"), "tp"),
        P(("dp", "ctx"), None),
        P(("dp", "ctx"), None),
        P(("dp", "ctx"), "tp", None),
    )
    return jax.shard_map(
        per_device,
        mesh=mesh,
        in_specs=placed,
        out_specs=(
            P("dp", "ctx", "tp"),
            P("dp", "ctx", "tp"),
            P("dp", "ctx", "tp"),
            P(("dp", "ctx"), None, None, "tp"),
        ),
        check_vma=False,
    )
```

```python
import functools
import math

import jax
import jax.numpy as jnp
from jax import lax
from jax.experimental import pallas as pl
from jax.experimental.pallas import tpu as pltpu
from jax.sharding import PartitionSpec as P

HEADS = 32
KV_HEADS = 4
HEAD_DIM = 128
TOPK = 8

masked_score = -1e30
mib = 1024 * 1024


def mul(a, b):
    return jnp.dot(a, b, preferred_element_type=jnp.float32)


def attention_kernel(n_blocks, heads_step, rows, n_parts, place, q_ref, do_ref, *refs):
    kv_refs = refs[:n_blocks]
    n_pairs = n_blocks // 2
    dq_ref, dkv_refs = refs[-11 - n_pairs], refs[-10 - n_pairs : -10]
    kv_s, kt_s, q_s, do_s, qt_s, dot_s, s_s, dp_s, dkv_s, dqt_s = refs[-10:]
    part = pl.program_id(1)
    pair = 2 * rows
    width = heads_step * rows
    z, x = place[0], place[1]
    scale = HEAD_DIM ** (-0.5)
    to_exp2 = scale * math.log2(math.e)
    for i, ref in enumerate(kv_refs):
        kv_s[i * rows : (i + 1) * rows, :] = ref[...]
        kt_s[i // 2, :, (i % 2) * rows : (i % 2 + 1) * rows] = ref[:, :HEAD_DIM].T
    for h in range(heads_step):
        lanes = slice(h * HEAD_DIM, (h + 1) * HEAD_DIM)
        here = slice(h * rows, (h + 1) * rows)
        q_s[here, :] = q_ref[:, lanes]
        do_s[here, :] = do_ref[:, lanes]
        qt_s[:, here] = q_ref[:, lanes].T
        dot_s[:, here] = do_ref[:, lanes].T

    def part_of(k):
        return pl.ds(pl.multiple_of(k * pair, pair), pair)

    def scores(k, top, first):
        s = mul(kv_s[part_of(k), :HEAD_DIM], qt_s[...])
        if first:
            key = lax.broadcasted_iota(jnp.int32, (pair, width), 0)
            query = lax.broadcasted_iota(jnp.int32, (pair, width), 1) & (rows - 1)
            bound = jnp.where(key < rows, query, jnp.where(x == 1, pair, -1))
            s = jnp.where(key <= bound, s, masked_score)
        s_s[part_of(k), :] = s
        return jnp.maximum(top, jnp.max(s, axis=0, keepdims=True))

    top = scores(0, jnp.full((1, width), masked_score, jnp.float32), True)
    top = lax.fori_loop(1, z + 1, functools.partial(scores, first=False), top)

    def sums(k, carry):
        total, accum = carry
        dp = mul(kv_s[part_of(k), HEAD_DIM:], dot_s[...])
        e = jnp.exp2((s_s[part_of(k), :] - top) * to_exp2)
        s_s[part_of(k), :] = e
        dp_s[part_of(k), :] = dp
        return (
            total + jnp.sum(e, axis=0, keepdims=True),
            accum + jnp.sum(e * dp, axis=0, keepdims=True),
        )

    zero = jnp.zeros((1, width), jnp.float32)
    total, accum = lax.fori_loop(0, z + 1, sums, (zero, zero))
    share = 1.0 / total
    delta = accum * share
    dqt_s[...] = jnp.zeros_like(dqt_s)

    def grads(k, carry):
        p = s_s[part_of(k), :] * share
        ds = (p * (dp_s[part_of(k), :] - delta)).astype(jnp.bfloat16)
        p = p.astype(jnp.bfloat16)
        dk = mul(ds, q_s[...]) * scale
        dv = mul(p, do_s[...])
        if n_parts > 1:
            dk = dk + jnp.where(part == 0, 0.0, dkv_s[part_of(k), :HEAD_DIM])
            dv = dv + jnp.where(part == 0, 0.0, dkv_s[part_of(k), HEAD_DIM:])
        dkv_s[part_of(k), :HEAD_DIM] = dk
        dkv_s[part_of(k), HEAD_DIM:] = dv
        dqt_s[...] += mul(kt_s[k], ds)
        return carry

    lax.fori_loop(0, z + 1, grads, 0)
    for h in range(heads_step):
        part_t = dqt_s[:, h * rows : (h + 1) * rows] * scale
        dq_ref[:, h * HEAD_DIM : (h + 1) * HEAD_DIM] = part_t.T.astype(jnp.bfloat16)
    for k, ref in enumerate(dkv_refs):
        held = dkv_s[k * pair : (k + 1) * pair, :]
        ref[...] = jnp.where(k <= z, held, 0.0).astype(jnp.bfloat16)


def attention(place, queries, out_grad, kv_blocks, first, count, query_grad, after=()):
    rows, q_width = queries.shape
    n_blocks = len(kv_blocks)
    group = HEADS // KV_HEADS
    keys = n_blocks * rows
    heads_step = max(1, min(group, 2**20 // (keys * rows)))
    n_parts = group // heads_step
    width = heads_step * rows
    q_spec = pl.BlockSpec(
        (rows, heads_step * HEAD_DIM), lambda g, u: (0, (g + first) * n_parts + u)
    )
    kv_spec = pl.BlockSpec((rows, 2 * HEAD_DIM), lambda g, u: (0, g + first))
    part_spec = pl.BlockSpec((2 * rows, 2 * HEAD_DIM), lambda g, u: (0, g))
    part_shape = jax.ShapeDtypeStruct((2 * rows, count * 2 * HEAD_DIM), jnp.bfloat16)
    held = [] if query_grad is None else [query_grad]
    return pl.pallas_call(
        functools.partial(attention_kernel, n_blocks, heads_step, rows, n_parts),
        grid=(count, n_parts),
        in_specs=[pl.BlockSpec(memory_space=pltpu.SMEM), q_spec, q_spec]
        + [kv_spec] * n_blocks
        + [pl.BlockSpec(memory_space=pl.ANY)] * (len(held) + len(after)),
        out_specs=[q_spec] + [part_spec] * (n_blocks // 2),
        out_shape=[jax.ShapeDtypeStruct((rows, q_width), jnp.bfloat16)]
        + [part_shape] * (n_blocks // 2),
        scratch_shapes=[
            pltpu.VMEM((keys, 2 * HEAD_DIM), jnp.bfloat16),
            pltpu.VMEM((n_blocks // 2, HEAD_DIM, 2 * rows), jnp.bfloat16),
            pltpu.VMEM((width, HEAD_DIM), jnp.bfloat16),
            pltpu.VMEM((width, HEAD_DIM), jnp.bfloat16),
            pltpu.VMEM((HEAD_DIM, width), jnp.bfloat16),
            pltpu.VMEM((HEAD_DIM, width), jnp.bfloat16),
            pltpu.VMEM((keys, width), jnp.float32),
            pltpu.VMEM((keys, width), jnp.float32),
            pltpu.VMEM((keys, 2 * HEAD_DIM), jnp.float32),
            pltpu.VMEM((HEAD_DIM, width), jnp.float32),
        ],
        input_output_aliases={3 + n_blocks: 0} if held else {},
        compiler_params=pltpu.CompilerParams(
            vmem_limit_bytes=24 * mib, dimension_semantics=("arbitrary", "arbitrary")
        ),
        cost_estimate=pl.CostEstimate(
            flops=10 * rows * keys * group * count * HEAD_DIM,
            bytes_accessed=6 * rows * group * count * HEAD_DIM + 8 * keys * count * HEAD_DIM,
            transcendentals=rows * keys * group * count,
        ),
        name="attention_backward",
    )(place, queries, out_grad, *kv_blocks, *held, *after)


def fold_kernel(n_z, groups, rows, *refs):
    own_ref, other_ref = refs[-2:]
    first = 0
    for i in range(groups):
        parts = refs[i * n_z : (i + 1) * n_z]
        total = parts[0][...].astype(jnp.float32)
        for ref in parts[1:]:
            total = total + ref[...].astype(jnp.float32)
        lanes = slice(first, first + total.shape[1])
        own_ref[:, lanes] = total[:rows]
        other_ref[:, lanes] = total[rows:].astype(jnp.bfloat16)
        first += total.shape[1]


def fold(parts, rows, after=()):
    width = sum(group[0].shape[1] for group in parts)
    return pl.pallas_call(
        functools.partial(fold_kernel, len(parts[0]), len(parts), rows),
        in_specs=[pl.BlockSpec(memory_space=pltpu.VMEM)] * (len(parts) * len(parts[0]))
        + [pl.BlockSpec(memory_space=pl.ANY)] * len(after),
        out_shape=[
            jax.ShapeDtypeStruct((rows, width), jnp.float32),
            jax.ShapeDtypeStruct((rows, width), jnp.bfloat16),
        ],
        compiler_params=pltpu.CompilerParams(vmem_limit_bytes=12 * mib),
        name="fold",
    )(*[part for group in parts for part in group], *after)


def finish_kernel(own_ref, got_ref, key_ref, value_ref):
    total = (own_ref[...] + got_ref[...].astype(jnp.float32)).astype(jnp.bfloat16)
    for g in range(total.shape[1] // (2 * HEAD_DIM)):
        lanes = slice(g * HEAD_DIM, (g + 1) * HEAD_DIM)
        key_ref[0, :, lanes] = total[:, 2 * g * HEAD_DIM : (2 * g + 1) * HEAD_DIM]
        value_ref[0, :, lanes] = total[:, (2 * g + 1) * HEAD_DIM : (2 * g + 2) * HEAD_DIM]


def finish(own, got):
    shape = jax.ShapeDtypeStruct((1, own.shape[0], own.shape[1] // 2), jnp.bfloat16)
    return pl.pallas_call(
        finish_kernel,
        out_shape=[shape, shape],
        compiler_params=pltpu.CompilerParams(vmem_limit_bytes=8 * mib),
        name="finish",
    )(own, got)


def join_kernel(
    n_z, n_dp, key_ref, value_ref, rows_ref, ids_ref, combine_ref, kv_ref, ext_ref
):
    for g in range(kv_ref.shape[1] // (2 * HEAD_DIM)):
        lanes = slice(g * HEAD_DIM, (g + 1) * HEAD_DIM)
        kv_ref[:, 2 * g * HEAD_DIM : (2 * g + 1) * HEAD_DIM] = key_ref[0, :, lanes]
        kv_ref[:, (2 * g + 1) * HEAD_DIM : (2 * g + 2) * HEAD_DIM] = value_ref[0, :, lanes]
    tokens, feat = rows_ref.shape
    lines = 4 * n_dp
    line = lax.broadcasted_iota(jnp.int32, (n_z * lines, tokens), 0)
    kind = line % lines
    member = kind % (2 * n_dp)
    expert = (member // 2) * (2 * n_z) + line // lines * 2 + member % 2
    hits = jnp.zeros((n_z * lines, tokens), jnp.float32)
    weights = jnp.zeros((n_z * lines, tokens), jnp.float32)
    combine = combine_ref[...].astype(jnp.float32)
    for k in range(TOPK):
        hit = ids_ref[k : k + 1, :] == expert
        hits = hits + jnp.where(hit, 1.0, 0.0)
        weights = weights + jnp.where(hit, combine[k : k + 1, :], 0.0)
    before = lax.broadcasted_iota(jnp.int32, (tokens, tokens), 0) < lax.broadcasted_iota(
        jnp.int32, (tokens, tokens), 1
    )
    ranks = mul(hits.astype(jnp.bfloat16), jnp.where(before, 1.0, 0.0).astype(jnp.bfloat16))
    table = jnp.where(kind < 2 * n_dp, jnp.where(hits > 0.0, ranks, -1.0), weights)
    ext_ref[:tokens, :] = rows_ref[...]
    squares = [table[i * lines : (i + 1) * lines] for i in range(n_z)]
    squares += [jnp.zeros((lines, tokens), jnp.float32)] * (feat // tokens - n_z)
    ext_ref[tokens:, :] = jnp.concatenate(squares, axis=1).astype(jnp.bfloat16)


def join(keys, values, full_rows, ids, combine, n_z, n_dp):
    rows, width = keys.shape[1:]
    tokens, feat = full_rows.shape
    return pl.pallas_call(
        functools.partial(join_kernel, n_z, n_dp),
        out_shape=[
            jax.ShapeDtypeStruct((rows, 2 * width), jnp.bfloat16),
            jax.ShapeDtypeStruct((tokens + 4 * n_dp, feat), jnp.bfloat16),
        ],
        compiler_params=pltpu.CompilerParams(vmem_limit_bytes=8 * mib),
        name="join",
    )(keys, values, full_rows, ids.T, combine.T)


def pick_kernel(sizes, n_dp, capacity, place, *refs):
    pieces = sum(sizes)
    out_ref, pick_s = refs[-2:]
    bounds = [sum(sizes[:i]) for i in range(len(sizes) + 1)]

    def added(group, i):
        total = group[bounds[i]][...]
        for ref in group[bounds[i] + 1 : bounds[i + 1]]:
            total = total + ref[...]
        return total

    @pl.when(pl.program_id(0) == 0)
    def _():
        for i in range(len(sizes)):
            tokens = refs[pieces].shape[0]
            table = refs[bounds[i]][:, pl.ds(pl.multiple_of(place[0] * tokens, tokens), tokens)]
            for ref in refs[bounds[i] + 1 : bounds[i + 1]]:
                table = table + ref[:, pl.ds(pl.multiple_of(place[0] * tokens, tokens), tokens)]
            table = table.astype(jnp.float32)
            slot = lax.broadcasted_iota(jnp.int32, (capacity, tokens), 0).astype(jnp.float32)
            picks = [
                jnp.where(
                    slot == table[q : q + 1, :], table[2 * n_dp + q : 2 * n_dp + q + 1, :], 0.0
                )
                for q in range(2 * n_dp)
            ]
            pick_s[i] = jnp.concatenate(picks, axis=0).astype(jnp.bfloat16)

    results = [mul(pick_s[i], added(refs[pieces : 2 * pieces], i)) for i in range(len(sizes))]
    for q in range(2 * n_dp):
        here = slice(q * capacity, (q + 1) * capacity)
        total = jnp.concatenate([part[here] for part in results], axis=0)
        size = len(sizes) * capacity
        out_ref[q * size : (q + 1) * size, :] = total.astype(jnp.bfloat16)


def pick_rows(place, blocks, n_dp, capacity, after=()):
    arrays = [array for block in blocks for array in block]
    sizes = [len(block) for block in blocks]
    lines, feat = 4 * n_dp, arrays[0].shape[1]
    tokens = arrays[0].shape[0] - lines
    step = math.gcd(feat, 1024)
    out_rows = len(blocks) * 2 * n_dp * capacity
    return pl.pallas_call(
        functools.partial(pick_kernel, sizes, n_dp, capacity),
        grid=(feat // step,),
        in_specs=[pl.BlockSpec(memory_space=pltpu.SMEM)]
        + [pl.BlockSpec((lines, feat), lambda f: (tokens // lines, 0))] * len(arrays)
        + [pl.BlockSpec((tokens, step), lambda f: (0, f))] * len(arrays)
        + [pl.BlockSpec(memory_space=pl.ANY)] * len(after),
        out_specs=pl.BlockSpec((out_rows, step), lambda f: (0, f)),
        out_shape=jax.ShapeDtypeStruct((out_rows, feat), jnp.bfloat16),
        scratch_shapes=[pltpu.VMEM((len(blocks), 2 * n_dp * capacity, tokens), jnp.bfloat16)],
        compiler_params=pltpu.CompilerParams(vmem_limit_bytes=(12 + 3 * len(blocks)) * mib),
        cost_estimate=pl.CostEstimate(flops=10**6, bytes_accessed=10**5, transcendentals=0),
        name="pick_rows",
    )(place, *arrays, *arrays, *after)


def expert_kernel(ks, n_z, n_dp, capacity, slots, place, rows_ref, w_ref, *refs):
    out_ref, out_s, sem = refs[-3:]
    step, steps = pl.program_id(0), out_s.shape[0]
    width = out_s.shape[-1]
    blocks = [(q, k) for q in range(2 * n_dp) for k in ks]
    result = lax.dot_general(
        rows_ref[...], w_ref[0], (((1,), (1,)), ((), ())), preferred_element_type=jnp.float32
    )
    for i in range(len(blocks)):
        out_s[step, i] = result[i * capacity : i * capacity + slots].astype(jnp.bfloat16)

    def copies(at):
        z = place[0]
        for i, (q, k) in enumerate(blocks):
            source = (q // 2) * (2 * n_z) + (z ^ k) * 2 + q % 2
            lanes = pl.ds(pl.multiple_of(at * width, width), width)
            yield pltpu.make_async_copy(
                out_s.at[at, i], out_ref.at[0, source, :, lanes], sem.at[at, i]
            )

    for copy in copies(step):
        copy.start()

    @pl.when(step == steps - 1)
    def _():
        for at in range(steps):
            for copy in copies(at):
                copy.wait()


def expert_rows(place, rows, ks, w_down, n_z, n_dp, capacity, slots, hidden_grad, after=()):
    hid, feat = w_down.shape[1:]
    step = math.gcd(hid, 512)
    held = [] if hidden_grad is None else [hidden_grad]
    return pl.pallas_call(
        functools.partial(expert_kernel, ks, n_z, n_dp, capacity, slots),
        grid=(hid // step,),
        in_specs=[
            pl.BlockSpec(memory_space=pltpu.SMEM),
            pl.BlockSpec(rows.shape, lambda n: (0, 0)),
            pl.BlockSpec((1, step, feat), lambda n: (0, n, 0)),
        ]
        + [pl.BlockSpec(memory_space=pl.ANY)] * (len(held) + len(after)),
        out_specs=pl.BlockSpec(memory_space=pl.ANY),
        out_shape=jax.ShapeDtypeStruct((1, n_dp * 2 * n_z, slots, hid), jnp.bfloat16),
        scratch_shapes=[
            pltpu.VMEM((hid // step, rows.shape[0] // capacity, slots, step), jnp.bfloat16),
            pltpu.SemaphoreType.DMA((hid // step, rows.shape[0] // capacity)),
        ],
        input_output_aliases={3: 0} if held else {},
        compiler_params=pltpu.CompilerParams(vmem_limit_bytes=(12 + rows.size // 2**17) * mib),
        cost_estimate=pl.CostEstimate(flops=10**6, bytes_accessed=10**5, transcendentals=0),
        name="expert_rows",
    )(place, rows, w_down, *held, *after)


def per_device(queries, keys, values, out_grad, mixed_grad, expert_ids, combine, w_down):
    rows_dev = queries.shape[1]
    kv_local = keys.shape[2] // HEAD_DIM
    n_ctx, n_dp = lax.axis_size("ctx"), lax.axis_size("dp")
    n_z = n_ctx // 2
    position = lax.axis_index("ctx")
    place = jnp.stack([position >> 1, position & 1]).astype(jnp.int32)
    token_rows = expert_ids.shape[0]
    experts_all = n_dp * n_ctx
    slots = min(
        token_rows,
        max(
            2,
            token_rows * TOPK * 5 // (4 * experts_all),
            (token_rows * TOPK + experts_all - 1) // experts_all,
        ),
    )
    capacity = -(-slots // 8) * 8
    full_rows = mixed_grad
    if lax.axis_size("tp") > 1:
        full_rows = lax.all_gather(mixed_grad, "tp", axis=1, tiled=True)
    own, own_rows = join(keys, values, full_rows, expert_ids, combine, n_z, n_dp)

    def along_z(array, targets):
        pairs = [(2 * i + x, 2 * j + x) for i, j in targets for x in range(2)]
        return lax.ppermute(array, "ctx", pairs)

    columns = [own]
    for k in range(1, n_z):
        columns.append(along_z(columns[-1], [(i, i + 1) for i in range(k - 1, n_z - 1)]))
    blocks = []
    for k, column in enumerate(columns):
        pairs = [(i, i ^ 1) for i in range(2 * k, n_ctx) if k > 0 or i % 2 == 0]
        blocks += [column, lax.ppermute(column, "ctx", pairs)]

    plane_groups = [
        [d * n_ctx + 2 * i + j for d in range(n_dp) for j in range(2)] for i in range(n_z)
    ]
    first_rows, columns[1] = lax.optimization_barrier((own_rows, columns[1]))
    near = along_z(first_rows, [(i, i ^ 1) for i in range(n_z)])
    if n_z == 4:
        second_rows, columns[2] = lax.optimization_barrier((own_rows, columns[2]))
        across = along_z(second_rows, [(1, 2), (2, 1)])
        across_near = along_z(near, [(1, 2), (2, 1)])
        outward = along_z(across, [(1, 0), (2, 3)])

    def exchange(arrays, after):
        picked = pick_rows(place, arrays, n_dp, capacity, after)
        return picked, lax.all_to_all(
            picked,
            ("dp", "ctx"),
            split_axis=0,
            concat_axis=0,
            tiled=True,
            axis_index_groups=plane_groups,
        )

    picked, got_near = exchange([(own_rows,), (near,)], tuple(blocks))

    counts = [1] if kv_local == 1 else [kv_local // 2, kv_local - kv_local // 2]
    query_grad, gathered, first = None, [], 0
    for count in counts:
        query_grad, *parts = attention(
            place, queries[0], out_grad[0], blocks, first, count, query_grad, (picked,)
        )
        if n_z == 4 and first == 0:
            across_near, query_grad = lax.optimization_barrier((across_near, query_grad))
            outward_near = along_z(across_near, [(1, 0), (2, 3)])
        first += count
        gathered.append(
            [parts[0]]
            + [
                lax.ppermute(parts[k], "ctx", [(i, i - 2 * k) for i in range(2 * k, n_ctx)])
                for k in range(1, n_z)
            ]
        )
    if n_z == 4:
        far = [(across_near, outward), (across, outward_near)]
    else:
        far = [(along_z(own_rows, [(i, i ^ k) for i in range(n_z)]),) for k in range(2, n_z)]
    picked, got_far = exchange(far, (query_grad,))
    sizes = (n_z, n_dp, capacity, slots)
    hidden_grad = expert_rows(place, got_near, (0, 1), w_down, *sizes, None, (picked,))
    total, other = fold(gathered, rows_dev, (hidden_grad,))
    got = lax.ppermute(other, "ctx", [(i, i ^ 1) for i in range(n_ctx)])
    key_grad, value_grad = finish(total, got)
    hidden_grad = expert_rows(place, got_far, tuple(range(2, n_z)), w_down, *sizes, hidden_grad)
    return (query_grad[None], key_grad, value_grad, hidden_grad)


def solution(mesh):
    placed = (
        P("dp", "ctx", "tp"),
        P("dp", "ctx", "tp"),
        P("dp", "ctx", "tp"),
        P("dp", "ctx", "tp"),
        P(("dp", "ctx"), "tp"),
        P(("dp", "ctx"), None),
        P(("dp", "ctx"), None),
        P(("dp", "ctx"), "tp", None),
    )
    return jax.shard_map(
        per_device,
        mesh=mesh,
        in_specs=placed,
        out_specs=(
            P("dp", "ctx", "tp"),
            P("dp", "ctx", "tp"),
            P("dp", "ctx", "tp"),
            P(("dp", "ctx"), None, None, "tp"),
        ),
        check_vma=False,
    )
```

```python
import functools
import math

import jax
import jax.numpy as jnp
from jax import lax
from jax.experimental import pallas as pl
from jax.experimental.pallas import tpu as pltpu
from jax.sharding import PartitionSpec as P

HEADS = 32
KV_HEADS = 4
HEAD_DIM = 128
TOPK = 8

masked_score = -1e30
vmem_limit = 56 * 1024 * 1024
small_cost = pl.CostEstimate(flops=1, bytes_accessed=1, transcendentals=0)


def mul(a, b):
    return jnp.dot(a, b, preferred_element_type=jnp.float32)


def attention_kernel(n_blocks, heads_step, rows, n_parts, place, q_ref, do_ref, *refs):
    kv_refs = refs[:n_blocks]
    dq_ref, mine_ref, other_ref = refs[-13:-10]
    kv_s, kt_s, q_s, do_s, qt_s, dot_s, s_s, dp_s, dkv_s, dqt_s = refs[-10:]
    part = pl.program_id(1)
    pair = 2 * rows
    width = heads_step * rows
    z, x = place[0], place[1]
    scale = HEAD_DIM ** (-0.5)
    to_exp2 = scale * math.log2(math.e)
    for i, ref in enumerate(kv_refs):
        kv_s[i * rows : (i + 1) * rows, :] = ref[...]
        kt_s[i // 2, :, (i % 2) * rows : (i % 2 + 1) * rows] = ref[:, :HEAD_DIM].T
    for h in range(heads_step):
        lanes = slice(h * HEAD_DIM, (h + 1) * HEAD_DIM)
        here = slice(h * rows, (h + 1) * rows)
        q_s[here, :] = q_ref[:, lanes]
        do_s[here, :] = do_ref[:, lanes]
        qt_s[:, here] = q_ref[:, lanes].T
        dot_s[:, here] = do_ref[:, lanes].T

    def part_of(k):
        return pl.ds(pl.multiple_of(k * pair, pair), pair)

    cut = math.gcd(width, 256)
    slices = [slice(i, i + cut) for i in range(0, width, cut)]

    def scores(k, tops, first):
        results = []
        for here, top in zip(slices, tops):
            s = mul(kv_s[part_of(k), :HEAD_DIM], qt_s[:, here])
            if first:
                key = lax.broadcasted_iota(jnp.int32, (pair, cut), 0)
                query = lax.broadcasted_iota(jnp.int32, (pair, cut), 1) & (rows - 1)
                bound = jnp.where(key < rows, query, jnp.where(x == 1, pair, -1))
                s = jnp.where(key <= bound, s, masked_score)
            s_s[part_of(k), here] = s
            results.append(jnp.maximum(top, jnp.max(s, axis=0, keepdims=True)))
        return tuple(results)

    tops = scores(0, tuple(jnp.full((1, cut), masked_score, jnp.float32) for _ in slices), True)
    tops = lax.fori_loop(1, z + 1, functools.partial(scores, first=False), tops)

    def sums(k, carry):
        results = []
        for here, top, (total, accum) in zip(slices, tops, carry):
            dp = mul(kv_s[part_of(k), HEAD_DIM:], dot_s[:, here])
            e = jnp.exp2((s_s[part_of(k), here] - top) * to_exp2)
            s_s[part_of(k), here] = e
            dp_s[part_of(k), here] = dp
            results.append(
                (
                    total + jnp.sum(e, axis=0, keepdims=True),
                    accum + jnp.sum(e * dp, axis=0, keepdims=True),
                )
            )
        return tuple(results)

    zero = jnp.zeros((1, cut), jnp.float32)
    stats = lax.fori_loop(0, z + 1, sums, tuple((zero, zero) for _ in slices))
    shares = [1.0 / total for total, _ in stats]
    deltas = [accum * share for (_, accum), share in zip(stats, shares)]
    dqt_s[...] = jnp.zeros_like(dqt_s)

    def grads(k, carry):
        dk = jnp.zeros((pair, HEAD_DIM), jnp.float32)
        dv = jnp.zeros((pair, HEAD_DIM), jnp.float32)
        for here, share, delta in zip(slices, shares, deltas):
            p = s_s[part_of(k), here] * share
            ds = (p * (dp_s[part_of(k), here] - delta)).astype(jnp.bfloat16)
            dv = dv + mul(p.astype(jnp.bfloat16), do_s[here, :])
            dk = dk + mul(ds, q_s[here, :])
            dqt_s[:, here] += mul(kt_s[k], ds)
        dk = dk * scale
        if n_parts > 1:
            dk = dk + jnp.where(part == 0, 0.0, dkv_s[part_of(k), :HEAD_DIM])
            dv = dv + jnp.where(part == 0, 0.0, dkv_s[part_of(k), HEAD_DIM:])
        dkv_s[part_of(k), :HEAD_DIM] = dk
        dkv_s[part_of(k), HEAD_DIM:] = dv
        return carry

    lax.fori_loop(0, z + 1, grads, 0)
    for h in range(heads_step):
        part_t = dqt_s[:, h * rows : (h + 1) * rows] * scale
        dq_ref[:, h * HEAD_DIM : (h + 1) * HEAD_DIM] = part_t.T.astype(jnp.bfloat16)
    for i in range(n_blocks):
        held = dkv_s[i * rows : (i + 1) * rows, :]
        ref = mine_ref if i % 2 == 0 else other_ref
        here = slice(i // 2 * rows, (i // 2 + 1) * rows)
        ref[here, :] = jnp.where(i // 2 <= z, held, 0.0).astype(jnp.bfloat16)


def attention(place, queries, out_grad, kv_blocks, first, count, query_grad, after=()):
    rows, q_width = queries.shape
    n_blocks = len(kv_blocks)
    group = HEADS // KV_HEADS
    keys = n_blocks * rows
    heads_step = max(1, min(group, 2**20 // (keys * rows)))
    n_parts = group // heads_step
    width = heads_step * rows
    q_spec = pl.BlockSpec(
        (rows, heads_step * HEAD_DIM), lambda g, u: (0, (g + first) * n_parts + u)
    )
    kv_spec = pl.BlockSpec((rows, 2 * HEAD_DIM), lambda g, u: (0, g + first))
    part_spec = pl.BlockSpec((keys // 2, 2 * HEAD_DIM), lambda g, u: (0, g))
    part_shape = jax.ShapeDtypeStruct((keys // 2, count * 2 * HEAD_DIM), jnp.bfloat16)
    held = [] if query_grad is None else [query_grad]
    return pl.pallas_call(
        functools.partial(attention_kernel, n_blocks, heads_step, rows, n_parts),
        grid=(count, n_parts),
        in_specs=[pl.BlockSpec(memory_space=pltpu.SMEM), q_spec, q_spec]
        + [kv_spec] * n_blocks
        + [pl.BlockSpec(memory_space=pl.ANY)] * (len(held) + len(after)),
        out_specs=[q_spec, part_spec, part_spec],
        out_shape=[jax.ShapeDtypeStruct((rows, q_width), jnp.bfloat16), part_shape, part_shape],
        scratch_shapes=[
            pltpu.VMEM((keys, 2 * HEAD_DIM), jnp.bfloat16),
            pltpu.VMEM((n_blocks // 2, HEAD_DIM, 2 * rows), jnp.bfloat16),
            pltpu.VMEM((width, HEAD_DIM), jnp.bfloat16),
            pltpu.VMEM((width, HEAD_DIM), jnp.bfloat16),
            pltpu.VMEM((HEAD_DIM, width), jnp.bfloat16),
            pltpu.VMEM((HEAD_DIM, width), jnp.bfloat16),
            pltpu.VMEM((keys, width), jnp.float32),
            pltpu.VMEM((keys, width), jnp.float32),
            pltpu.VMEM((keys, 2 * HEAD_DIM), jnp.float32),
            pltpu.VMEM((HEAD_DIM, width), jnp.float32),
        ],
        input_output_aliases={3 + n_blocks: 0} if held else {},
        compiler_params=pltpu.CompilerParams(
            vmem_limit_bytes=vmem_limit, dimension_semantics=("arbitrary", "arbitrary")
        ),
        cost_estimate=small_cost
        if held
        else pl.CostEstimate(
            flops=10 * rows * keys * group * count * HEAD_DIM,
            bytes_accessed=8 * (rows * group + keys) * count * HEAD_DIM,
            transcendentals=rows * keys * group * count,
        ),
        name="attention_backward",
    )(place, queries, out_grad, *kv_blocks, *held, *after)


def fold_kernel(rows, mine_ref, got_ref, *refs):
    for k, ref in enumerate(refs[-(mine_ref.shape[0] // rows) :]):
        here = slice(k * rows, (k + 1) * rows)
        total = mine_ref[here, :].astype(jnp.float32) + got_ref[here, :].astype(jnp.float32)
        ref[...] = total.astype(ref.dtype)


def fold(mine, got, rows, after=()):
    n_z, width = mine.shape[0] // rows, mine.shape[1]
    return pl.pallas_call(
        functools.partial(fold_kernel, rows),
        in_specs=[pl.BlockSpec(memory_space=pltpu.VMEM)] * 2
        + [pl.BlockSpec(memory_space=pl.ANY)] * len(after),
        out_shape=[jax.ShapeDtypeStruct((rows, width), jnp.float32)]
        + [jax.ShapeDtypeStruct((rows, width), jnp.bfloat16)] * (n_z - 1),
        compiler_params=pltpu.CompilerParams(vmem_limit_bytes=vmem_limit),
        cost_estimate=small_cost,
        name="fold",
    )(mine, got, *after)


def finish_kernel(n_z, counts, *refs):
    key_ref, value_ref = refs[-2:]
    first = 0
    for i, count in enumerate(counts):
        parts = refs[i * n_z : (i + 1) * n_z]
        total = parts[0][...]
        for ref in parts[1:]:
            total = total + ref[...].astype(jnp.float32)
        total = total.astype(jnp.bfloat16)
        for g in range(count):
            lanes = slice((first + g) * HEAD_DIM, (first + g + 1) * HEAD_DIM)
            key_ref[0, :, lanes] = total[:, 2 * g * HEAD_DIM : (2 * g + 1) * HEAD_DIM]
            value_ref[0, :, lanes] = total[:, (2 * g + 1) * HEAD_DIM : (2 * g + 2) * HEAD_DIM]
        first += count


def finish(parts, counts, rows, after):
    shape = jax.ShapeDtypeStruct((1, rows, sum(counts) * HEAD_DIM), jnp.bfloat16)
    return pl.pallas_call(
        functools.partial(finish_kernel, len(parts[0]), counts),
        in_specs=[pl.BlockSpec(memory_space=pltpu.VMEM)] * (len(parts) * len(parts[0]))
        + [pl.BlockSpec(memory_space=pl.ANY)],
        out_shape=[shape, shape],
        compiler_params=pltpu.CompilerParams(vmem_limit_bytes=vmem_limit),
        cost_estimate=small_cost,
        name="finish",
    )(*[part for group in parts for part in group], after)


def join_kernel(
    n_z, n_dp, key_ref, value_ref, rows_ref, ids_ref, combine_ref, kv_ref, ext_ref
):
    for g in range(kv_ref.shape[1] // (2 * HEAD_DIM)):
        lanes = slice(g * HEAD_DIM, (g + 1) * HEAD_DIM)
        kv_ref[:, 2 * g * HEAD_DIM : (2 * g + 1) * HEAD_DIM] = key_ref[0, :, lanes]
        kv_ref[:, (2 * g + 1) * HEAD_DIM : (2 * g + 2) * HEAD_DIM] = value_ref[0, :, lanes]
    tokens, feat = rows_ref.shape
    lines = 4 * n_dp
    line = lax.broadcasted_iota(jnp.int32, (n_z * lines, tokens), 0)
    kind = line % lines
    member = kind % (2 * n_dp)
    expert = (member // 2) * (2 * n_z) + line // lines * 2 + member % 2
    hits = jnp.zeros((n_z * lines, tokens), jnp.float32)
    weights = jnp.zeros((n_z * lines, tokens), jnp.float32)
    combine = combine_ref[...].astype(jnp.float32)
    for k in range(TOPK):
        hit = ids_ref[k : k + 1, :] == expert
        hits = hits + jnp.where(hit, 1.0, 0.0)
        weights = weights + jnp.where(hit, combine[k : k + 1, :], 0.0)
    before = lax.broadcasted_iota(jnp.int32, (tokens, tokens), 0) < lax.broadcasted_iota(
        jnp.int32, (tokens, tokens), 1
    )
    ranks = mul(hits.astype(jnp.bfloat16), jnp.where(before, 1.0, 0.0).astype(jnp.bfloat16))
    table = jnp.where(kind < 2 * n_dp, jnp.where(hits > 0.0, ranks, -1.0), weights)
    ext_ref[:tokens, :] = rows_ref[...]
    squares = [table[i * lines : (i + 1) * lines] for i in range(n_z)]
    squares += [jnp.zeros((lines, tokens), jnp.float32)] * (feat // tokens - n_z)
    ext_ref[tokens:, :] = jnp.concatenate(squares, axis=1).astype(jnp.bfloat16)


def join(keys, values, full_rows, ids, combine, n_z, n_dp):
    rows, width = keys.shape[1:]
    tokens, feat = full_rows.shape
    return pl.pallas_call(
        functools.partial(join_kernel, n_z, n_dp),
        out_shape=[
            jax.ShapeDtypeStruct((rows, 2 * width), jnp.bfloat16),
            jax.ShapeDtypeStruct((tokens + 4 * n_dp, feat), jnp.bfloat16),
        ],
        compiler_params=pltpu.CompilerParams(vmem_limit_bytes=vmem_limit),
        cost_estimate=small_cost,
        name="join",
    )(keys, values, full_rows, ids.T, combine.T)


def pick_kernel(count, n_dp, capacity, place, *refs):
    table_refs, row_refs = refs[:count], refs[count : 2 * count]
    out_ref, pick_s = refs[-2:]
    tokens = pick_s.shape[2]

    @pl.when(pl.program_id(0) == 0)
    def _():
        for i, ref in enumerate(table_refs):
            table = ref[:, pl.ds(pl.multiple_of(place[0] * tokens, tokens), tokens)]
            table = table.astype(jnp.float32)
            slot = lax.broadcasted_iota(jnp.int32, (capacity, tokens), 0).astype(jnp.float32)
            picks = [
                jnp.where(
                    slot == table[q : q + 1, :], table[2 * n_dp + q : 2 * n_dp + q + 1, :], 0.0
                )
                for q in range(2 * n_dp)
            ]
            pick_s[i] = jnp.concatenate(picks, axis=0).astype(jnp.bfloat16)

    results = [mul(pick_s[i], ref[:tokens, :]) for i, ref in enumerate(row_refs)]
    for q in range(2 * n_dp):
        here = slice(q * capacity, (q + 1) * capacity)
        total = jnp.concatenate([part[here] for part in results], axis=0)
        size = count * capacity
        out_ref[q * size : (q + 1) * size, :] = total.astype(jnp.bfloat16)


def pick_rows(place, array, ks, tokens, n_dp, capacity, after=()):
    lines, feat = 4 * n_dp, array.shape[1]
    block = tokens + lines
    step = math.gcd(feat, 512)
    out_rows = len(ks) * 2 * n_dp * capacity

    def at(place, k):
        return place[0] ^ k if array.shape[0] > block else 0

    def table_spec(k):
        per_block = block // lines
        return pl.BlockSpec(
            (lines, feat), lambda f, place: (at(place, k) * per_block + per_block - 1, 0)
        )

    def rows_spec(k):
        return pl.BlockSpec((block, step), lambda f, place: (at(place, k), f))

    return pl.pallas_call(
        functools.partial(pick_kernel, len(ks), n_dp, capacity),
        grid_spec=pltpu.PrefetchScalarGridSpec(
            num_scalar_prefetch=1,
            grid=(feat // step,),
            in_specs=[table_spec(k) for k in ks]
            + [rows_spec(k) for k in ks]
            + [pl.BlockSpec(memory_space=pl.ANY)] * len(after),
            out_specs=pl.BlockSpec((out_rows, step), lambda f, place: (0, f)),
            scratch_shapes=[pltpu.VMEM((len(ks), 2 * n_dp * capacity, tokens), jnp.bfloat16)],
        ),
        out_shape=jax.ShapeDtypeStruct((out_rows, feat), jnp.bfloat16),
        compiler_params=pltpu.CompilerParams(vmem_limit_bytes=vmem_limit),
        cost_estimate=small_cost,
        name="pick_rows",
    )(place, *[array] * (2 * len(ks)), *after)


def expert_kernel(chunks, n_z, n_dp, capacity, slots, place, *refs):
    row_refs, w_ref = refs[: len(chunks)], refs[len(chunks)]
    out_ref, out_s, sem = refs[-3:]
    step, steps = pl.program_id(0), out_s.shape[0]
    width = out_s.shape[-1]
    blocks = [(q, k) for ks in chunks for q in range(2 * n_dp) for k in ks]
    first = 0
    for rows_ref in row_refs:
        result = lax.dot_general(
            rows_ref[...], w_ref[0], (((1,), (1,)), ((), ())), preferred_element_type=jnp.float32
        )
        count = rows_ref.shape[0] // capacity
        for i in range(count):
            out_s[step, first + i] = result[i * capacity : i * capacity + slots].astype(jnp.bfloat16)
        first += count

    def copies(at):
        z = place[0]
        for i, (q, k) in enumerate(blocks):
            source = (q // 2) * (2 * n_z) + (z ^ k) * 2 + q % 2
            lanes = pl.ds(pl.multiple_of(at * width, width), width)
            yield pltpu.make_async_copy(
                out_s.at[at, i], out_ref.at[0, source, :, lanes], sem.at[at, i]
            )

    for copy in copies(step):
        copy.start()

    @pl.when(step == steps - 1)
    def _():
        for at in range(steps):
            for copy in copies(at):
                copy.wait()


def expert_rows(place, arrays, chunks, w_down, n_z, n_dp, capacity, slots, hidden_grad, after=()):
    hid, feat = w_down.shape[1:]
    step = math.gcd(hid, 512)
    count = sum(array.shape[0] for array in arrays) // capacity
    held = [] if hidden_grad is None else [hidden_grad]
    return pl.pallas_call(
        functools.partial(expert_kernel, chunks, n_z, n_dp, capacity, slots),
        grid=(hid // step,),
        in_specs=[pl.BlockSpec(memory_space=pltpu.SMEM)]
        + [pl.BlockSpec(array.shape, lambda n: (0, 0)) for array in arrays]
        + [pl.BlockSpec((1, step, feat), lambda n: (0, n, 0))]
        + [pl.BlockSpec(memory_space=pl.ANY)] * (len(held) + len(after)),
        out_specs=pl.BlockSpec(memory_space=pl.ANY),
        out_shape=jax.ShapeDtypeStruct((1, n_dp * 2 * n_z, slots, hid), jnp.bfloat16),
        scratch_shapes=[
            pltpu.VMEM((hid // step, count, slots, step), jnp.bfloat16),
            pltpu.SemaphoreType.DMA((hid // step, count)),
        ],
        input_output_aliases={2 + len(arrays): 0} if held else {},
        compiler_params=pltpu.CompilerParams(vmem_limit_bytes=vmem_limit),
        cost_estimate=small_cost,
        name="expert_rows",
    )(place, *arrays, w_down, *held, *after)


def per_device(queries, keys, values, out_grad, mixed_grad, expert_ids, combine, w_down):
    rows_dev = queries.shape[1]
    kv_local = keys.shape[2] // HEAD_DIM
    n_ctx, n_dp = lax.axis_size("ctx"), lax.axis_size("dp")
    n_z = n_ctx // 2
    position = lax.axis_index("ctx")
    place = jnp.stack([position >> 1, position & 1]).astype(jnp.int32)
    token_rows = expert_ids.shape[0]
    experts_all = n_dp * n_ctx
    slots = min(
        token_rows,
        max(
            2,
            token_rows * TOPK * 5 // (4 * experts_all),
            (token_rows * TOPK + experts_all - 1) // experts_all,
        ),
    )
    capacity = -(-slots // 8) * 8
    full_rows = mixed_grad
    if lax.axis_size("tp") > 1:
        full_rows = lax.all_gather(mixed_grad, "tp", axis=1, tiled=True)
    own, own_rows = join(keys, values, full_rows, expert_ids, combine, n_z, n_dp)

    def along_z(array, targets):
        pairs = [(2 * i + x, 2 * j + x) for i, j in targets for x in range(2)]
        return lax.ppermute(array, "ctx", pairs)

    def across_x(k):
        pairs = [(i, i ^ 1) for i in range(2 * k, n_ctx) if k > 0 or i % 2 == 0]
        return lax.ppermute(columns[k], "ctx", pairs)

    columns, others = [own], []
    for k in range(1, n_z):
        others.append(across_x(k - 1))
        if k > 2:
            columns[-1], others[k - 3] = lax.optimization_barrier((columns[-1], others[k - 3]))
        columns.append(along_z(columns[-1], [(i, i + 1) for i in range(k - 1, n_z - 1)]))
    columns[-1], *others[-2:] = lax.optimization_barrier((columns[-1], *others[-2:]))
    others.append(across_x(n_z - 1))
    blocks = [block for pair in zip(columns, others) for block in pair]

    plane_groups = [
        [d * n_ctx + 2 * i + j for d in range(n_dp) for j in range(2)] for i in range(n_z)
    ]
    line_groups = [[2 * i + x for i in range(n_z)] for x in range(2)]
    gathered_rows = lax.all_gather(
        own_rows, "ctx", axis=0, tiled=True, axis_index_groups=line_groups
    )

    def exchange(array, ks, after):
        picked = pick_rows(place, array, ks, token_rows, n_dp, capacity, after)
        return picked, lax.all_to_all(
            picked,
            ("dp", "ctx"),
            split_axis=0,
            concat_axis=0,
            tiled=True,
            axis_index_groups=plane_groups,
        )

    counts = [1] if kv_local == 1 else [kv_local - 1, 1]
    gathered = []

    def down(mine, other, after=()):
        got = lax.ppermute(other, "ctx", [(i, i ^ 1) for i in range(n_ctx)])
        parts = fold(mine, got, rows_dev, after)
        gathered.append(
            [parts[0]]
            + [
                lax.ppermute(parts[k], "ctx", [(i, i - 2 * k) for i in range(2 * k, n_ctx)])
                for k in range(1, n_z)
            ]
        )
        return got, parts[0]

    chunks = [(0,), tuple(range(1, n_z))]
    picked, got_own = exchange(own_rows, chunks[0], (columns[n_z - 1],))
    query_grad, mine, other = attention(
        place, queries[0], out_grad[0], blocks, 0, counts[0], None, (picked,)
    )
    got, folded = down(mine, other)
    picked, got_rest = exchange(gathered_rows, chunks[1], (got,))
    if len(counts) > 1:
        query_grad, mine, other = attention(
            place, queries[0], out_grad[0], blocks, counts[0], counts[1], query_grad, (picked,)
        )
        got, folded = down(mine, other)
    sizes = (n_z, n_dp, capacity, slots)
    hidden_grad = expert_rows(place, (got_own,), chunks[:1], w_down, *sizes, None, (folded,))
    key_grad, value_grad = finish(gathered, counts, rows_dev, hidden_grad)
    hidden_grad = expert_rows(place, (got_rest,), chunks[1:], w_down, *sizes, hidden_grad)
    return (query_grad[None], key_grad, value_grad, hidden_grad)


def solution(mesh):
    placed = (
        P("dp", "ctx", "tp"),
        P("dp", "ctx", "tp"),
        P("dp", "ctx", "tp"),
        P("dp", "ctx", "tp"),
        P(("dp", "ctx"), "tp"),
        P(("dp", "ctx"), None),
        P(("dp", "ctx"), None),
        P(("dp", "ctx"), "tp", None),
    )
    return jax.shard_map(
        per_device,
        mesh=mesh,
        in_specs=placed,
        out_specs=(
            P("dp", "ctx", "tp"),
            P("dp", "ctx", "tp"),
            P("dp", "ctx", "tp"),
            P(("dp", "ctx"), None, None, "tp"),
        ),
        check_vma=False,
    )
```

```python
import functools
import math

import jax
import jax.numpy as jnp
from jax import lax
from jax.experimental import pallas as pl
from jax.experimental.pallas import tpu as pltpu
from jax.sharding import PartitionSpec as P

HEADS = 32
KV_HEADS = 4
HEAD_DIM = 128
TOPK = 8

masked_score = -1e30
vmem_limit = 56 * 1024 * 1024
small_cost = pl.CostEstimate(flops=1, bytes_accessed=1, transcendentals=0)


def mul(a, b):
    return jnp.dot(a, b, preferred_element_type=jnp.float32)


def attention_kernel(n_blocks, heads_step, rows, n_parts, place, q_ref, do_ref, *refs):
    kv_refs = refs[:n_blocks]
    dq_ref, mine_ref, other_ref = refs[-13:-10]
    kv_s, kt_s, q_s, do_s, qt_s, dot_s, s_s, dp_s, dkv_s, dqt_s = refs[-10:]
    part = pl.program_id(1)
    pair = 2 * rows
    width = heads_step * rows
    z, x = place[0], place[1]
    scale = HEAD_DIM ** (-0.5)
    to_exp2 = scale * math.log2(math.e)
    for i, ref in enumerate(kv_refs):
        kv_s[i * rows : (i + 1) * rows, :] = ref[...]
        kt_s[i // 2, :, (i % 2) * rows : (i % 2 + 1) * rows] = ref[:, :HEAD_DIM].T
    for h in range(heads_step):
        lanes = slice(h * HEAD_DIM, (h + 1) * HEAD_DIM)
        here = slice(h * rows, (h + 1) * rows)
        q_s[here, :] = q_ref[:, lanes]
        do_s[here, :] = do_ref[:, lanes]
        qt_s[:, here] = q_ref[:, lanes].T
        dot_s[:, here] = do_ref[:, lanes].T

    def part_of(k):
        return pl.ds(pl.multiple_of(k * pair, pair), pair)

    cut = math.gcd(width, 256)
    slices = [slice(i, i + cut) for i in range(0, width, cut)]

    def scores(k, tops, first):
        results = []
        for here, top in zip(slices, tops):
            s = mul(kv_s[part_of(k), :HEAD_DIM], qt_s[:, here])
            if first:
                key = lax.broadcasted_iota(jnp.int32, (pair, cut), 0)
                query = lax.broadcasted_iota(jnp.int32, (pair, cut), 1) & (rows - 1)
                bound = jnp.where(key < rows, query, jnp.where(x == 1, pair, -1))
                s = jnp.where(key <= bound, s, masked_score)
            s_s[part_of(k), here] = s
            results.append(jnp.maximum(top, jnp.max(s, axis=0, keepdims=True)))
        return tuple(results)

    tops = scores(0, tuple(jnp.full((1, cut), masked_score, jnp.float32) for _ in slices), True)
    tops = lax.fori_loop(1, z + 1, functools.partial(scores, first=False), tops)

    def sums(k, carry):
        results = []
        for here, top, (total, accum) in zip(slices, tops, carry):
            dp = mul(kv_s[part_of(k), HEAD_DIM:], dot_s[:, here])
            e = jnp.exp2((s_s[part_of(k), here] - top) * to_exp2)
            s_s[part_of(k), here] = e
            dp_s[part_of(k), here] = dp
            results.append(
                (
                    total + jnp.sum(e, axis=0, keepdims=True),
                    accum + jnp.sum(e * dp, axis=0, keepdims=True),
                )
            )
        return tuple(results)

    zero = jnp.zeros((1, cut), jnp.float32)
    stats = lax.fori_loop(0, z + 1, sums, tuple((zero, zero) for _ in slices))
    shares = [1.0 / total for total, _ in stats]
    deltas = [accum * share for (_, accum), share in zip(stats, shares)]
    dqt_s[...] = jnp.zeros_like(dqt_s)

    def grads(k, carry):
        dk = jnp.zeros((pair, HEAD_DIM), jnp.float32)
        dv = jnp.zeros((pair, HEAD_DIM), jnp.float32)
        for here, share, delta in zip(slices, shares, deltas):
            p = s_s[part_of(k), here] * share
            ds = (p * (dp_s[part_of(k), here] - delta)).astype(jnp.bfloat16)
            dv = dv + mul(p.astype(jnp.bfloat16), do_s[here, :])
            dk = dk + mul(ds, q_s[here, :])
            dqt_s[:, here] += mul(kt_s[k], ds)
        dk = dk * scale
        if n_parts > 1:
            dk = dk + jnp.where(part == 0, 0.0, dkv_s[part_of(k), :HEAD_DIM])
            dv = dv + jnp.where(part == 0, 0.0, dkv_s[part_of(k), HEAD_DIM:])
        dkv_s[part_of(k), :HEAD_DIM] = dk
        dkv_s[part_of(k), HEAD_DIM:] = dv
        return carry

    lax.fori_loop(0, z + 1, grads, 0)
    for h in range(heads_step):
        part_t = dqt_s[:, h * rows : (h + 1) * rows] * scale
        dq_ref[:, h * HEAD_DIM : (h + 1) * HEAD_DIM] = part_t.T.astype(jnp.bfloat16)
    for i in range(n_blocks):
        held = dkv_s[i * rows : (i + 1) * rows, :]
        ref = mine_ref if i % 2 == 0 else other_ref
        at = lax.rem(z - i // 2 + n_blocks // 2, n_blocks // 2) * rows
        held = jnp.where(i // 2 <= z, held, 0.0).astype(jnp.bfloat16)
        ref[pl.ds(pl.multiple_of(at, rows), rows), :] = held


def attention(place, queries, out_grad, kv_blocks, first, count, query_grad, after=()):
    rows, q_width = queries.shape
    n_blocks = len(kv_blocks)
    group = HEADS // KV_HEADS
    keys = n_blocks * rows
    heads_step = max(1, min(group, 2**20 // (keys * rows)))
    n_parts = group // heads_step
    width = heads_step * rows
    q_spec = pl.BlockSpec(
        (rows, heads_step * HEAD_DIM), lambda g, u: (0, (g + first) * n_parts + u)
    )
    kv_spec = pl.BlockSpec((rows, 2 * HEAD_DIM), lambda g, u: (0, g + first))
    part_spec = pl.BlockSpec((keys // 2, 2 * HEAD_DIM), lambda g, u: (0, g))
    part_shape = jax.ShapeDtypeStruct((keys // 2, count * 2 * HEAD_DIM), jnp.bfloat16)
    held = [] if query_grad is None else [query_grad]
    return pl.pallas_call(
        functools.partial(attention_kernel, n_blocks, heads_step, rows, n_parts),
        grid=(count, n_parts),
        in_specs=[pl.BlockSpec(memory_space=pltpu.SMEM), q_spec, q_spec]
        + [kv_spec] * n_blocks
        + [pl.BlockSpec(memory_space=pl.ANY)] * (len(held) + len(after)),
        out_specs=[q_spec, part_spec, part_spec],
        out_shape=[jax.ShapeDtypeStruct((rows, q_width), jnp.bfloat16), part_shape, part_shape],
        scratch_shapes=[
            pltpu.VMEM((keys, 2 * HEAD_DIM), jnp.bfloat16),
            pltpu.VMEM((n_blocks // 2, HEAD_DIM, 2 * rows), jnp.bfloat16),
            pltpu.VMEM((width, HEAD_DIM), jnp.bfloat16),
            pltpu.VMEM((width, HEAD_DIM), jnp.bfloat16),
            pltpu.VMEM((HEAD_DIM, width), jnp.bfloat16),
            pltpu.VMEM((HEAD_DIM, width), jnp.bfloat16),
            pltpu.VMEM((keys, width), jnp.float32),
            pltpu.VMEM((keys, width), jnp.float32),
            pltpu.VMEM((keys, 2 * HEAD_DIM), jnp.float32),
            pltpu.VMEM((HEAD_DIM, width), jnp.float32),
        ],
        input_output_aliases={3 + n_blocks: 0} if held else {},
        compiler_params=pltpu.CompilerParams(
            vmem_limit_bytes=vmem_limit, dimension_semantics=("arbitrary", "arbitrary")
        ),
        cost_estimate=small_cost
        if held
        else pl.CostEstimate(
            flops=100 * rows * keys * group * count * HEAD_DIM,
            bytes_accessed=8 * (rows * group + keys) * count * HEAD_DIM,
            transcendentals=rows * keys * group * count,
        ),
        name="attention_backward",
    )(place, queries, out_grad, *kv_blocks, *held, *after)


def fold_kernel(mine_ref, *refs):
    out_ref, width = refs[-1], mine_ref.shape[1]
    total = mine_ref[...].astype(jnp.float32) + refs[0][...].astype(jnp.float32)
    out_ref[:, :width] = total.astype(out_ref.dtype)
    first = width
    for ref in refs[1:-1]:
        out_ref[:, first : first + ref.shape[1]] = ref[...]
        first += ref.shape[1]


def fold(mine, got, others):
    arrays = (mine, got, *others)
    rows, width = mine.shape[0], sum(part.shape[1] for part in arrays[1:])
    return pl.pallas_call(
        fold_kernel,
        grid=(4,),
        in_specs=[pl.BlockSpec((rows // 4, part.shape[1]), lambda i: (i, 0)) for part in arrays],
        out_specs=pl.BlockSpec((rows // 4, width), lambda i: (i, 0)),
        out_shape=jax.ShapeDtypeStruct((rows, width), jnp.bfloat16),
        compiler_params=pltpu.CompilerParams(vmem_limit_bytes=vmem_limit),
        cost_estimate=small_cost,
        name="fold",
    )(*arrays)


def finish_kernel(counts, total_ref, *refs):
    key_ref, value_ref = refs[-2:]
    size = 2 * HEAD_DIM
    for g in range(sum(counts)):
        lanes = slice(g * HEAD_DIM, (g + 1) * HEAD_DIM)
        held = total_ref[:, g * size : (g + 1) * size]
        if g >= counts[0]:
            at = (g - counts[0]) * size
            held = held.astype(jnp.float32) + refs[0][:, at : at + size].astype(jnp.float32)
            held = held.astype(jnp.bfloat16)
        key_ref[0, :, lanes] = held[:, :HEAD_DIM]
        value_ref[0, :, lanes] = held[:, HEAD_DIM:]


def finish(counts, total, crossed, after):
    shape = jax.ShapeDtypeStruct((1, total.shape[0], sum(counts) * HEAD_DIM), jnp.bfloat16)
    return pl.pallas_call(
        functools.partial(finish_kernel, counts),
        in_specs=[pl.BlockSpec(memory_space=pltpu.VMEM)] * (1 + len(crossed))
        + [pl.BlockSpec(memory_space=pl.ANY)],
        out_shape=[shape, shape],
        compiler_params=pltpu.CompilerParams(vmem_limit_bytes=vmem_limit),
        cost_estimate=small_cost,
        name="finish",
    )(total, *crossed, after)


def join_kernel(
    n_z, n_dp, key_ref, value_ref, rows_ref, ids_ref, combine_ref, kv_ref, ext_ref, rest_ref
):
    for g in range(kv_ref.shape[1] // (2 * HEAD_DIM)):
        lanes = slice(g * HEAD_DIM, (g + 1) * HEAD_DIM)
        kv_ref[:, 2 * g * HEAD_DIM : (2 * g + 1) * HEAD_DIM] = key_ref[0, :, lanes]
        kv_ref[:, (2 * g + 1) * HEAD_DIM : (2 * g + 2) * HEAD_DIM] = value_ref[0, :, lanes]
    tokens, feat = rows_ref.shape
    lines = 4 * n_dp
    line = lax.broadcasted_iota(jnp.int32, (n_z * lines, tokens), 0)
    kind = line % lines
    member = kind % (2 * n_dp)
    expert = (member // 2) * (2 * n_z) + line // lines * 2 + member % 2
    hits = jnp.zeros((n_z * lines, tokens), jnp.float32)
    weights = jnp.zeros((n_z * lines, tokens), jnp.float32)
    combine = combine_ref[...].astype(jnp.float32)
    for k in range(TOPK):
        hit = ids_ref[k : k + 1, :] == expert
        hits = hits + jnp.where(hit, 1.0, 0.0)
        weights = weights + jnp.where(hit, combine[k : k + 1, :], 0.0)
    before = lax.broadcasted_iota(jnp.int32, (tokens, tokens), 0) < lax.broadcasted_iota(
        jnp.int32, (tokens, tokens), 1
    )
    ranks = mul(hits.astype(jnp.bfloat16), jnp.where(before, 1.0, 0.0).astype(jnp.bfloat16))
    table = jnp.where(kind < 2 * n_dp, jnp.where(hits > 0.0, ranks, -1.0), weights)
    half = feat // 2
    ext_ref[:tokens, :] = rows_ref[:, :half]
    rest_ref[...] = rows_ref[:, half:]
    squares = [table[i * lines : (i + 1) * lines] for i in range(n_z)]
    per_row = half // tokens
    squares += [jnp.zeros((lines, tokens), jnp.float32)] * (-n_z % per_row)
    for i in range(len(squares) // per_row):
        line_of = jnp.concatenate(squares[i * per_row : (i + 1) * per_row], axis=1)
        here = slice(tokens + i * lines, tokens + (i + 1) * lines)
        ext_ref[here, :] = line_of.astype(jnp.bfloat16)


def join(keys, values, full_rows, ids, combine, n_z, n_dp):
    rows, width = keys.shape[1:]
    tokens, feat = full_rows.shape
    return pl.pallas_call(
        functools.partial(join_kernel, n_z, n_dp),
        out_shape=[
            jax.ShapeDtypeStruct((rows, 2 * width), jnp.bfloat16),
            jax.ShapeDtypeStruct(
                (tokens + 4 * n_dp * -(-2 * n_z * tokens // feat), feat // 2), jnp.bfloat16
            ),
            jax.ShapeDtypeStruct((tokens, feat // 2), jnp.bfloat16),
        ],
        compiler_params=pltpu.CompilerParams(vmem_limit_bytes=vmem_limit),
        cost_estimate=small_cost,
        name="join",
    )(keys, values, full_rows, ids.T, combine.T)


def pick_kernel(count, n_dp, capacity, place, *refs):
    table_refs, row_refs = refs[:count], refs[count : 2 * count]
    out_ref, pick_s = refs[-2:]
    tokens = pick_s.shape[2]

    @pl.when(pl.program_id(0) == 0)
    def _():
        for i, ref in enumerate(table_refs):
            table = ref[...].astype(jnp.float32)
            slot = lax.broadcasted_iota(jnp.int32, (capacity, tokens), 0).astype(jnp.float32)
            picks = [
                jnp.where(
                    slot == table[q : q + 1, :], table[2 * n_dp + q : 2 * n_dp + q + 1, :], 0.0
                )
                for q in range(2 * n_dp)
            ]
            pick_s[i] = jnp.concatenate(picks, axis=0).astype(jnp.bfloat16)

    results = [mul(pick_s[i], ref[:tokens, :]) for i, ref in enumerate(row_refs)]
    for q in range(2 * n_dp):
        here = slice(q * capacity, (q + 1) * capacity)
        total = jnp.concatenate([part[here] for part in results], axis=0)
        size = count * capacity
        out_ref[q * size : (q + 1) * size, :] = total.astype(jnp.bfloat16)


def pick_rows(place, table, block_table, array, block, ks, tokens, n_dp, capacity, after=()):
    lines, feat = 4 * n_dp, array.shape[1]
    step = math.gcd(feat, 512)
    out_rows = len(ks) * 2 * n_dp * capacity
    per_row = table.shape[1] // tokens

    def at(place, k, whole, part):
        return (place[0] & (whole.shape[0] // part - 1)) ^ k

    def table_spec(k):
        def index(f, place):
            first = (at(place, k, table, block_table) * block_table + tokens) // lines
            return first + place[0] // per_row, place[0] % per_row

        return pl.BlockSpec((lines, tokens), index)

    def rows_spec(k):
        return pl.BlockSpec((block, step), lambda f, place: (at(place, k, array, block), f))

    return pl.pallas_call(
        functools.partial(pick_kernel, len(ks), n_dp, capacity),
        grid_spec=pltpu.PrefetchScalarGridSpec(
            num_scalar_prefetch=1,
            grid=(feat // step,),
            in_specs=[table_spec(k) for k in ks]
            + [rows_spec(k) for k in ks]
            + [pl.BlockSpec(memory_space=pl.ANY)] * len(after),
            out_specs=pl.BlockSpec((out_rows, step), lambda f, place: (0, f)),
            scratch_shapes=[pltpu.VMEM((len(ks), 2 * n_dp * capacity, tokens), jnp.bfloat16)],
        ),
        out_shape=jax.ShapeDtypeStruct((out_rows, feat), jnp.bfloat16),
        compiler_params=pltpu.CompilerParams(vmem_limit_bytes=vmem_limit),
        cost_estimate=small_cost,
        name="pick_rows",
    )(place, *[table] * len(ks), *[array] * len(ks), *after)


def partial_kernel(rows_ref, w_ref, out_ref):
    out_ref[...] = lax.dot_general(
        rows_ref[...], w_ref[0], (((1,), (1,)), ((), ())), preferred_element_type=jnp.float32
    )


def partial_rows(rows, w_down):
    count, half = rows.shape
    hid = w_down.shape[1]
    step = math.gcd(hid, 512)
    return pl.pallas_call(
        partial_kernel,
        grid=(hid // step,),
        in_specs=[
            pl.BlockSpec((count, half), lambda n: (0, 0)),
            pl.BlockSpec((1, step, half), lambda n: (0, n, 0)),
        ],
        out_specs=pl.BlockSpec((count, step), lambda n: (0, n)),
        out_shape=jax.ShapeDtypeStruct((count, hid), jnp.float32),
        compiler_params=pltpu.CompilerParams(vmem_limit_bytes=vmem_limit),
        cost_estimate=small_cost,
        name="partial_rows",
    )(rows, w_down)


def expert_kernel(ks, with_base, n_z, n_dp, capacity, slots, place, rows_ref, w_ref, *refs):
    out_ref, out_s, sem = refs[-3:]
    step, steps = pl.program_id(0), out_s.shape[0]
    width = out_s.shape[-1]
    blocks = [(q, k) for q in range(2 * n_dp) for k in ks]
    result = lax.dot_general(
        rows_ref[...], w_ref[0], (((1,), (1,)), ((), ())), preferred_element_type=jnp.float32
    )
    if with_base:
        result = result + refs[0][...]
    for i in range(len(blocks)):
        out_s[step, i] = result[i * capacity : i * capacity + slots].astype(jnp.bfloat16)

    def copies(at):
        z = place[0]
        for i, (q, k) in enumerate(blocks):
            source = (q // 2) * (2 * n_z) + (z ^ k) * 2 + q % 2
            lanes = pl.ds(pl.multiple_of(at * width, width), width)
            yield pltpu.make_async_copy(
                out_s.at[at, i], out_ref.at[0, source, :, lanes], sem.at[at, i]
            )

    for copy in copies(step):
        copy.start()

    @pl.when(step == steps - 1)
    def _():
        for at in range(steps):
            for copy in copies(at):
                copy.wait()


def expert_rows(place, rows, ks, w_down, n_z, n_dp, capacity, slots, base, hidden_grad, after=()):
    hid = w_down.shape[1]
    step = math.gcd(hid, 512)
    count = rows.shape[0] // capacity
    part = w_down.shape[2] // rows.shape[1] - 1
    extra = [] if base is None else [base]
    held = [] if hidden_grad is None else [hidden_grad]
    return pl.pallas_call(
        functools.partial(expert_kernel, ks, bool(extra), n_z, n_dp, capacity, slots),
        grid=(hid // step,),
        in_specs=[
            pl.BlockSpec(memory_space=pltpu.SMEM),
            pl.BlockSpec(rows.shape, lambda n: (0, 0)),
            pl.BlockSpec((1, step, rows.shape[1]), lambda n: (0, n, part)),
        ]
        + [pl.BlockSpec((rows.shape[0], step), lambda n: (0, n))] * len(extra)
        + [pl.BlockSpec(memory_space=pl.ANY)] * (len(held) + len(after)),
        out_specs=pl.BlockSpec(memory_space=pl.ANY),
        out_shape=jax.ShapeDtypeStruct((1, n_dp * 2 * n_z, slots, hid), jnp.bfloat16),
        scratch_shapes=[
            pltpu.VMEM((hid // step, count, slots, step), jnp.bfloat16),
            pltpu.SemaphoreType.DMA((hid // step, count)),
        ],
        input_output_aliases={3 + len(extra): 0} if held else {},
        compiler_params=pltpu.CompilerParams(vmem_limit_bytes=vmem_limit),
        cost_estimate=small_cost,
        name="expert_rows",
    )(place, rows, w_down, *extra, *held, *after)


def per_device(queries, keys, values, out_grad, mixed_grad, expert_ids, combine, w_down):
    rows_dev = queries.shape[1]
    kv_local = keys.shape[2] // HEAD_DIM
    n_ctx, n_dp = lax.axis_size("ctx"), lax.axis_size("dp")
    n_z = n_ctx // 2
    position = lax.axis_index("ctx")
    place = jnp.stack([position >> 1, position & 1]).astype(jnp.int32)
    token_rows = expert_ids.shape[0]
    experts_all = n_dp * n_ctx
    slots = min(
        token_rows,
        max(
            2,
            token_rows * TOPK * 5 // (4 * experts_all),
            (token_rows * TOPK + experts_all - 1) // experts_all,
        ),
    )
    capacity = -(-slots // 8) * 8
    full_rows = mixed_grad
    if lax.axis_size("tp") > 1:
        full_rows = lax.all_gather(mixed_grad, "tp", axis=1, tiled=True)
    own, *own_halves = join(keys, values, full_rows, expert_ids, combine, n_z, n_dp)

    def along_z(array, targets):
        pairs = [(2 * i + x, 2 * j + x) for i, j in targets for x in range(2)]
        return lax.ppermute(array, "ctx", pairs)

    def across_x(k):
        pairs = [(i, i ^ 1) for i in range(2 * k, n_ctx) if k > 0 or i % 2 == 0]
        return lax.ppermute(columns[k], "ctx", pairs)

    columns, others = [own], []
    for k in range(1, n_z):
        others.append(across_x(k - 1))
        if k > 2:
            columns[-1], others[k - 3] = lax.optimization_barrier((columns[-1], others[k - 3]))
        columns.append(along_z(columns[-1], [(i, i + 1) for i in range(k - 1, n_z - 1)]))
    columns[-1], *others[-2:] = lax.optimization_barrier((columns[-1], *others[-2:]))
    others.append(across_x(n_z - 1))
    blocks = [block for pair in zip(columns, others) for block in pair]

    plane_groups = [
        [d * n_ctx + 2 * i + j for d in range(n_dp) for j in range(2)] for i in range(n_z)
    ]
    line_groups = [[2 * i + x for i in range(n_z)] for x in range(2)]
    first_half, columns[n_z // 2] = lax.optimization_barrier((own_halves[0], columns[n_z // 2]))
    last_half, columns[n_z - 1] = lax.optimization_barrier((own_halves[1], columns[n_z - 1]))
    all_halves = [
        lax.all_gather(half, "ctx", axis=0, tiled=True, axis_index_groups=line_groups)
        for half in (first_half, last_half)
    ]

    def pick(table, array, ks, after):
        block = token_rows if array.shape[0] % own_halves[0].shape[0] else own_halves[0].shape[0]
        sizes = (ks, token_rows, n_dp, capacity)
        return pick_rows(place, table, own_halves[0].shape[0], array, block, *sizes, after)

    def exchange(picked):
        return lax.all_to_all(
            picked,
            ("dp", "ctx"),
            split_axis=0,
            concat_axis=0,
            tiled=True,
            axis_index_groups=plane_groups,
        )

    def cross(array):
        return lax.ppermute(array, "ctx", [(i, i ^ 1) for i in range(n_ctx)])

    counts = [1] if kv_local == 1 else [kv_local // 2, kv_local - kv_local // 2]
    rest = tuple(range(1, n_z))
    picked = pick(own_halves[0], full_rows, (0,), (columns[n_z - 1],))
    got_own = exchange(picked)
    query_grad, mine, other = attention(
        place, queries[0], out_grad[0], blocks, 0, counts[0], None, (picked,)
    )
    crossed = cross(other)
    picked = pick(all_halves[0], all_halves[0], rest, (query_grad,))
    picked, crossed = lax.optimization_barrier((picked, crossed))
    got_first = exchange(picked)
    others = []
    if len(counts) > 1:
        query_grad, *others = attention(
            place, queries[0], out_grad[0], blocks, counts[0], counts[1], query_grad, (picked,)
        )
    picked = pick(all_halves[0], all_halves[1], rest, (query_grad,))
    got_last = exchange(picked)
    total = lax.psum_scatter(
        fold(mine, crossed, others),
        "ctx",
        scatter_dimension=0,
        tiled=True,
        axis_index_groups=line_groups,
    )
    sizes = (n_z, n_dp, capacity, slots)
    hidden_grad = expert_rows(place, got_own, (0,), w_down, *sizes, None, None, (picked,))
    base = partial_rows(got_first, w_down)
    total, base = lax.optimization_barrier((total, base))
    last = [cross(total[:, -others[1].shape[1] :])] if others else []
    key_grad, value_grad = finish(counts, total, last, base)
    hidden_grad = expert_rows(place, got_last, rest, w_down, *sizes, base, hidden_grad)
    return (query_grad[None], key_grad, value_grad, hidden_grad)


def solution(mesh):
    placed = (
        P("dp", "ctx", "tp"),
        P("dp", "ctx", "tp"),
        P("dp", "ctx", "tp"),
        P("dp", "ctx", "tp"),
        P(("dp", "ctx"), "tp"),
        P(("dp", "ctx"), None),
        P(("dp", "ctx"), None),
        P(("dp", "ctx"), "tp", None),
    )
    return jax.shard_map(
        per_device,
        mesh=mesh,
        in_specs=placed,
        out_specs=(
            P("dp", "ctx", "tp"),
            P("dp", "ctx", "tp"),
            P("dp", "ctx", "tp"),
            P(("dp", "ctx"), None, None, "tp"),
        ),
        check_vma=False,
    )
```

```python
import functools
import math

import jax
import jax.numpy as jnp
from jax import lax
from jax.experimental import pallas as pl
from jax.experimental.pallas import tpu as pltpu
from jax.sharding import PartitionSpec as P

HEADS = 32
KV_HEADS = 4
HEAD_DIM = 128
TOPK = 8

masked_score = -1e30
vmem_limit = 56 * 1024 * 1024
small_cost = pl.CostEstimate(flops=1, bytes_accessed=1, transcendentals=0)


def mul(a, b):
    return jnp.dot(a, b, preferred_element_type=jnp.float32)


def attention_kernel(n_blocks, heads_step, rows, n_parts, place, q_ref, do_ref, *refs):
    kv_refs = refs[:n_blocks]
    dq_ref, mine_ref, other_ref = refs[-13:-10]
    kv_s, kt_s, q_s, do_s, qt_s, dot_s, s_s, dp_s, dkv_s, dqt_s = refs[-10:]
    part = pl.program_id(1)
    pair = 2 * rows
    width = heads_step * rows
    z, x = place[0], place[1]
    scale = HEAD_DIM ** (-0.5)
    to_exp2 = scale * math.log2(math.e)
    for i, ref in enumerate(kv_refs):
        kv_s[i * rows : (i + 1) * rows, :] = ref[...]
        kt_s[i // 2, :, (i % 2) * rows : (i % 2 + 1) * rows] = ref[:, :HEAD_DIM].T
    for h in range(heads_step):
        lanes = slice(h * HEAD_DIM, (h + 1) * HEAD_DIM)
        here = slice(h * rows, (h + 1) * rows)
        q_s[here, :] = q_ref[:, lanes]
        do_s[here, :] = do_ref[:, lanes]
        qt_s[:, here] = q_ref[:, lanes].T
        dot_s[:, here] = do_ref[:, lanes].T

    def part_of(k):
        return pl.ds(pl.multiple_of(k * pair, pair), pair)

    cut = math.gcd(width, 256)
    slices = [slice(i, i + cut) for i in range(0, width, cut)]

    def scores(k, tops, first):
        results = []
        for here, top in zip(slices, tops):
            s = mul(kv_s[part_of(k), :HEAD_DIM], qt_s[:, here])
            if first:
                key = lax.broadcasted_iota(jnp.int32, (pair, cut), 0)
                query = lax.broadcasted_iota(jnp.int32, (pair, cut), 1) & (rows - 1)
                bound = jnp.where(key < rows, query, jnp.where(x == 1, pair, -1))
                s = jnp.where(key <= bound, s, masked_score)
            s_s[part_of(k), here] = s
            results.append(jnp.maximum(top, jnp.max(s, axis=0, keepdims=True)))
        return tuple(results)

    tops = scores(0, tuple(jnp.full((1, cut), masked_score, jnp.float32) for _ in slices), True)
    tops = lax.fori_loop(1, z + 1, functools.partial(scores, first=False), tops)

    def sums(k, carry):
        results = []
        for here, top, (total, accum) in zip(slices, tops, carry):
            dp = mul(kv_s[part_of(k), HEAD_DIM:], dot_s[:, here])
            e = jnp.exp2((s_s[part_of(k), here] - top) * to_exp2)
            s_s[part_of(k), here] = e
            dp_s[part_of(k), here] = dp
            results.append(
                (
                    total + jnp.sum(e, axis=0, keepdims=True),
                    accum + jnp.sum(e * dp, axis=0, keepdims=True),
                )
            )
        return tuple(results)

    zero = jnp.zeros((1, cut), jnp.float32)
    stats = lax.fori_loop(0, z + 1, sums, tuple((zero, zero) for _ in slices))
    shares = [1.0 / total for total, _ in stats]
    deltas = [accum * share for (_, accum), share in zip(stats, shares)]
    dqt_s[...] = jnp.zeros_like(dqt_s)

    def grads(k, carry):
        dk = jnp.zeros((pair, HEAD_DIM), jnp.float32)
        dv = jnp.zeros((pair, HEAD_DIM), jnp.float32)
        for here, share, delta in zip(slices, shares, deltas):
            p = s_s[part_of(k), here] * share
            ds = (p * (dp_s[part_of(k), here] - delta)).astype(jnp.bfloat16)
            dv = dv + mul(p.astype(jnp.bfloat16), do_s[here, :])
            dk = dk + mul(ds, q_s[here, :])
            dqt_s[:, here] += mul(kt_s[k], ds)
        dk = dk * scale
        if n_parts > 1:
            dk = dk + jnp.where(part == 0, 0.0, dkv_s[part_of(k), :HEAD_DIM])
            dv = dv + jnp.where(part == 0, 0.0, dkv_s[part_of(k), HEAD_DIM:])
        dkv_s[part_of(k), :HEAD_DIM] = dk
        dkv_s[part_of(k), HEAD_DIM:] = dv
        return carry

    lax.fori_loop(0, z + 1, grads, 0)
    for h in range(heads_step):
        part_t = dqt_s[:, h * rows : (h + 1) * rows] * scale
        dq_ref[:, h * HEAD_DIM : (h + 1) * HEAD_DIM] = part_t.T.astype(jnp.bfloat16)
    for i in range(n_blocks):
        held = dkv_s[i * rows : (i + 1) * rows, :]
        ref = mine_ref if i % 2 == 0 else other_ref
        at = lax.rem(z - i // 2 + n_blocks // 2, n_blocks // 2) * rows
        held = jnp.where(i // 2 <= z, held, 0.0).astype(jnp.bfloat16)
        ref[pl.ds(pl.multiple_of(at, rows), rows), :] = held


def attention(place, queries, out_grad, kv_blocks, first, count, query_grad, after=()):
    rows, q_width = queries.shape
    n_blocks = len(kv_blocks)
    group = HEADS // KV_HEADS
    keys = n_blocks * rows
    heads_step = max(1, min(group, 2**20 // (keys * rows)))
    n_parts = group // heads_step
    width = heads_step * rows
    q_spec = pl.BlockSpec(
        (rows, heads_step * HEAD_DIM), lambda g, u: (0, (g + first) * n_parts + u)
    )
    kv_spec = pl.BlockSpec((rows, 2 * HEAD_DIM), lambda g, u: (0, g + first))
    part_spec = pl.BlockSpec((keys // 2, 2 * HEAD_DIM), lambda g, u: (0, g))
    part_shape = jax.ShapeDtypeStruct((keys // 2, count * 2 * HEAD_DIM), jnp.bfloat16)
    held = [] if query_grad is None else [query_grad]
    return pl.pallas_call(
        functools.partial(attention_kernel, n_blocks, heads_step, rows, n_parts),
        grid=(count, n_parts),
        in_specs=[pl.BlockSpec(memory_space=pltpu.SMEM), q_spec, q_spec]
        + [kv_spec] * n_blocks
        + [pl.BlockSpec(memory_space=pl.ANY)] * (len(held) + len(after)),
        out_specs=[q_spec, part_spec, part_spec],
        out_shape=[jax.ShapeDtypeStruct((rows, q_width), jnp.bfloat16), part_shape, part_shape],
        scratch_shapes=[
            pltpu.VMEM((keys, 2 * HEAD_DIM), jnp.bfloat16),
            pltpu.VMEM((n_blocks // 2, HEAD_DIM, 2 * rows), jnp.bfloat16),
            pltpu.VMEM((width, HEAD_DIM), jnp.bfloat16),
            pltpu.VMEM((width, HEAD_DIM), jnp.bfloat16),
            pltpu.VMEM((HEAD_DIM, width), jnp.bfloat16),
            pltpu.VMEM((HEAD_DIM, width), jnp.bfloat16),
            pltpu.VMEM((keys, width), jnp.float32),
            pltpu.VMEM((keys, width), jnp.float32),
            pltpu.VMEM((keys, 2 * HEAD_DIM), jnp.float32),
            pltpu.VMEM((HEAD_DIM, width), jnp.float32),
        ],
        input_output_aliases={3 + n_blocks: 0} if held else {},
        compiler_params=pltpu.CompilerParams(
            vmem_limit_bytes=vmem_limit, dimension_semantics=("arbitrary", "arbitrary")
        ),
        cost_estimate=small_cost
        if held
        else pl.CostEstimate(
            flops=100 * rows * keys * group * count * HEAD_DIM,
            bytes_accessed=8 * (rows * group + keys) * count * HEAD_DIM,
            transcendentals=rows * keys * group * count,
        ),
        name="attention_backward",
    )(place, queries, out_grad, *kv_blocks, *held, *after)


def fold_kernel(mine_ref, *refs):
    out_ref, width = refs[-1], mine_ref.shape[1]
    total = mine_ref[...].astype(jnp.float32) + refs[0][...].astype(jnp.float32)
    out_ref[:, :width] = total.astype(out_ref.dtype)
    first = width
    for ref in refs[1:-1]:
        out_ref[:, first : first + ref.shape[1]] = ref[...]
        first += ref.shape[1]


def fold(mine, got, others):
    arrays = (mine, got, *others)
    rows, width = mine.shape[0], sum(part.shape[1] for part in arrays[1:])
    return pl.pallas_call(
        fold_kernel,
        grid=(4,),
        in_specs=[pl.BlockSpec((rows // 4, part.shape[1]), lambda i: (i, 0)) for part in arrays],
        out_specs=pl.BlockSpec((rows // 4, width), lambda i: (i, 0)),
        out_shape=jax.ShapeDtypeStruct((rows, width), jnp.bfloat16),
        compiler_params=pltpu.CompilerParams(vmem_limit_bytes=vmem_limit),
        cost_estimate=small_cost,
        name="fold",
    )(*arrays)


def finish_kernel(counts, total_ref, *refs):
    key_ref, value_ref = refs[-2:]
    size = 2 * HEAD_DIM
    for g in range(sum(counts)):
        lanes = slice(g * HEAD_DIM, (g + 1) * HEAD_DIM)
        held = total_ref[:, g * size : (g + 1) * size]
        if g >= counts[0]:
            at = (g - counts[0]) * size
            held = held.astype(jnp.float32) + refs[0][:, at : at + size].astype(jnp.float32)
            held = held.astype(jnp.bfloat16)
        key_ref[0, :, lanes] = held[:, :HEAD_DIM]
        value_ref[0, :, lanes] = held[:, HEAD_DIM:]


def finish(counts, total, crossed, after):
    shape = jax.ShapeDtypeStruct((1, total.shape[0], sum(counts) * HEAD_DIM), jnp.bfloat16)
    return pl.pallas_call(
        functools.partial(finish_kernel, counts),
        in_specs=[pl.BlockSpec(memory_space=pltpu.VMEM)] * (1 + len(crossed))
        + [pl.BlockSpec(memory_space=pl.ANY)],
        out_shape=[shape, shape],
        compiler_params=pltpu.CompilerParams(vmem_limit_bytes=vmem_limit),
        cost_estimate=small_cost,
        name="finish",
    )(total, *crossed, after)


def join_kernel(
    n_z, n_dp, key_ref, value_ref, rows_ref, ids_ref, combine_ref, kv_ref, ext_ref, rest_ref
):
    for g in range(kv_ref.shape[1] // (2 * HEAD_DIM)):
        lanes = slice(g * HEAD_DIM, (g + 1) * HEAD_DIM)
        kv_ref[:, 2 * g * HEAD_DIM : (2 * g + 1) * HEAD_DIM] = key_ref[0, :, lanes]
        kv_ref[:, (2 * g + 1) * HEAD_DIM : (2 * g + 2) * HEAD_DIM] = value_ref[0, :, lanes]
    tokens, feat = rows_ref.shape
    lines = 4 * n_dp
    line = lax.broadcasted_iota(jnp.int32, (n_z * lines, tokens), 0)
    kind = line % lines
    member = kind % (2 * n_dp)
    expert = (member // 2) * (2 * n_z) + line // lines * 2 + member % 2
    hits = jnp.zeros((n_z * lines, tokens), jnp.float32)
    weights = jnp.zeros((n_z * lines, tokens), jnp.float32)
    combine = combine_ref[...].astype(jnp.float32)
    for k in range(TOPK):
        hit = ids_ref[k : k + 1, :] == expert
        hits = hits + jnp.where(hit, 1.0, 0.0)
        weights = weights + jnp.where(hit, combine[k : k + 1, :], 0.0)
    before = lax.broadcasted_iota(jnp.int32, (tokens, tokens), 0) < lax.broadcasted_iota(
        jnp.int32, (tokens, tokens), 1
    )
    ranks = mul(hits.astype(jnp.bfloat16), jnp.where(before, 1.0, 0.0).astype(jnp.bfloat16))
    table = jnp.where(kind < 2 * n_dp, jnp.where(hits > 0.0, ranks, -1.0), weights)
    half = feat // 2
    ext_ref[:tokens, :] = rows_ref[:, :half]
    rest_ref[...] = rows_ref[:, half:]
    squares = [table[i * lines : (i + 1) * lines] for i in range(n_z)]
    per_row = half // tokens
    squares += [jnp.zeros((lines, tokens), jnp.float32)] * (-n_z % per_row)
    for i in range(len(squares) // per_row):
        line_of = jnp.concatenate(squares[i * per_row : (i + 1) * per_row], axis=1)
        here = slice(tokens + i * lines, tokens + (i + 1) * lines)
        ext_ref[here, :] = line_of.astype(jnp.bfloat16)


def join(keys, values, full_rows, ids, combine, n_z, n_dp):
    rows, width = keys.shape[1:]
    tokens, feat = full_rows.shape
    return pl.pallas_call(
        functools.partial(join_kernel, n_z, n_dp),
        out_shape=[
            jax.ShapeDtypeStruct((rows, 2 * width), jnp.bfloat16),
            jax.ShapeDtypeStruct(
                (tokens + 4 * n_dp * -(-2 * n_z * tokens // feat), feat // 2), jnp.bfloat16
            ),
            jax.ShapeDtypeStruct((tokens, feat // 2), jnp.bfloat16),
        ],
        compiler_params=pltpu.CompilerParams(vmem_limit_bytes=vmem_limit),
        cost_estimate=small_cost,
        name="join",
    )(keys, values, full_rows, ids.T, combine.T)


def pick_kernel(count, n_dp, capacity, place, *refs):
    table_refs, row_refs = refs[:count], refs[count : 2 * count]
    out_ref, pick_s = refs[-2:]
    tokens = pick_s.shape[2]

    @pl.when(pl.program_id(0) == 0)
    def _():
        for i, ref in enumerate(table_refs):
            table = ref[...].astype(jnp.float32)
            slot = lax.broadcasted_iota(jnp.int32, (capacity, tokens), 0).astype(jnp.float32)
            picks = [
                jnp.where(
                    slot == table[q : q + 1, :], table[2 * n_dp + q : 2 * n_dp + q + 1, :], 0.0
                )
                for q in range(2 * n_dp)
            ]
            pick_s[i] = jnp.concatenate(picks, axis=0).astype(jnp.bfloat16)

    results = [mul(pick_s[i], ref[:tokens, :]) for i, ref in enumerate(row_refs)]
    for q in range(2 * n_dp):
        here = slice(q * capacity, (q + 1) * capacity)
        total = jnp.concatenate([part[here] for part in results], axis=0)
        size = count * capacity
        out_ref[q * size : (q + 1) * size, :] = total.astype(jnp.bfloat16)


def pick_rows(place, table, block_table, array, block, ks, tokens, n_dp, capacity, after=()):
    lines, feat = 4 * n_dp, array.shape[1]
    step = math.gcd(feat, 1024 if len(ks) == 1 else 512)
    out_rows = len(ks) * 2 * n_dp * capacity
    per_row = table.shape[1] // tokens

    def at(place, k, whole, part):
        return (place[0] & (whole.shape[0] // part - 1)) ^ k

    def table_spec(k):
        def index(f, place):
            first = (at(place, k, table, block_table) * block_table + tokens) // lines
            return first + place[0] // per_row, place[0] % per_row

        return pl.BlockSpec((lines, tokens), index)

    def rows_spec(k):
        return pl.BlockSpec((block, step), lambda f, place: (at(place, k, array, block), f))

    return pl.pallas_call(
        functools.partial(pick_kernel, len(ks), n_dp, capacity),
        grid_spec=pltpu.PrefetchScalarGridSpec(
            num_scalar_prefetch=1,
            grid=(feat // step,),
            in_specs=[table_spec(k) for k in ks]
            + [rows_spec(k) for k in ks]
            + [pl.BlockSpec(memory_space=pl.ANY)] * len(after),
            out_specs=pl.BlockSpec((out_rows, step), lambda f, place: (0, f)),
            scratch_shapes=[pltpu.VMEM((len(ks), 2 * n_dp * capacity, tokens), jnp.bfloat16)],
        ),
        out_shape=jax.ShapeDtypeStruct((out_rows, feat), jnp.bfloat16),
        compiler_params=pltpu.CompilerParams(vmem_limit_bytes=vmem_limit),
        cost_estimate=small_cost,
        name="pick_rows",
    )(place, *[table] * len(ks), *[array] * len(ks), *after)


def partial_kernel(rows_ref, w_ref, out_ref):
    out_ref[...] = lax.dot_general(
        rows_ref[...], w_ref[0], (((1,), (1,)), ((), ())), preferred_element_type=jnp.float32
    )


def partial_rows(rows, w_down):
    count, half = rows.shape
    hid = w_down.shape[1]
    step = math.gcd(hid, 512)
    return pl.pallas_call(
        partial_kernel,
        grid=(hid // step,),
        in_specs=[
            pl.BlockSpec((count, half), lambda n: (0, 0)),
            pl.BlockSpec((1, step, half), lambda n: (0, n, 0)),
        ],
        out_specs=pl.BlockSpec((count, step), lambda n: (0, n)),
        out_shape=jax.ShapeDtypeStruct((count, hid), jnp.float32),
        compiler_params=pltpu.CompilerParams(vmem_limit_bytes=vmem_limit),
        cost_estimate=small_cost,
        name="partial_rows",
    )(rows, w_down)


def expert_kernel(ks, with_base, n_z, n_dp, capacity, slots, place, rows_ref, w_ref, *refs):
    out_ref, out_s, sem = refs[-3:]
    step, steps = pl.program_id(0), out_s.shape[0]
    width = out_s.shape[-1]
    blocks = [(q, k) for q in range(2 * n_dp) for k in ks]
    result = lax.dot_general(
        rows_ref[...], w_ref[0], (((1,), (1,)), ((), ())), preferred_element_type=jnp.float32
    )
    if with_base:
        result = result + refs[0][...]
    for i in range(len(blocks)):
        out_s[step, i] = result[i * capacity : i * capacity + slots].astype(jnp.bfloat16)

    def copies(at):
        z = place[0]
        for i, (q, k) in enumerate(blocks):
            source = (q // 2) * (2 * n_z) + (z ^ k) * 2 + q % 2
            lanes = pl.ds(pl.multiple_of(at * width, width), width)
            yield pltpu.make_async_copy(
                out_s.at[at, i], out_ref.at[0, source, :, lanes], sem.at[at, i]
            )

    for copy in copies(step):
        copy.start()

    @pl.when(step == steps - 1)
    def _():
        for at in range(steps):
            for copy in copies(at):
                copy.wait()


def expert_rows(place, rows, ks, w_down, n_z, n_dp, capacity, slots, base, hidden_grad, after=()):
    hid = w_down.shape[1]
    step = math.gcd(hid, 512)
    count = rows.shape[0] // capacity
    part = w_down.shape[2] // rows.shape[1] - 1
    extra = [] if base is None else [base]
    held = [] if hidden_grad is None else [hidden_grad]
    return pl.pallas_call(
        functools.partial(expert_kernel, ks, bool(extra), n_z, n_dp, capacity, slots),
        grid=(hid // step,),
        in_specs=[
            pl.BlockSpec(memory_space=pltpu.SMEM),
            pl.BlockSpec(rows.shape, lambda n: (0, 0)),
            pl.BlockSpec((1, step, rows.shape[1]), lambda n: (0, n, part)),
        ]
        + [pl.BlockSpec((rows.shape[0], step), lambda n: (0, n))] * len(extra)
        + [pl.BlockSpec(memory_space=pl.ANY)] * (len(held) + len(after)),
        out_specs=pl.BlockSpec(memory_space=pl.ANY),
        out_shape=jax.ShapeDtypeStruct((1, n_dp * 2 * n_z, slots, hid), jnp.bfloat16),
        scratch_shapes=[
            pltpu.VMEM((hid // step, count, slots, step), jnp.bfloat16),
            pltpu.SemaphoreType.DMA((hid // step, count)),
        ],
        input_output_aliases={3 + len(extra): 0} if held else {},
        compiler_params=pltpu.CompilerParams(vmem_limit_bytes=vmem_limit),
        cost_estimate=small_cost,
        name="expert_rows",
    )(place, rows, w_down, *extra, *held, *after)


def per_device(queries, keys, values, out_grad, mixed_grad, expert_ids, combine, w_down):
    rows_dev = queries.shape[1]
    kv_local = keys.shape[2] // HEAD_DIM
    n_ctx, n_dp = lax.axis_size("ctx"), lax.axis_size("dp")
    n_z = n_ctx // 2
    position = lax.axis_index("ctx")
    place = jnp.stack([position >> 1, position & 1]).astype(jnp.int32)
    token_rows = expert_ids.shape[0]
    experts_all = n_dp * n_ctx
    slots = min(
        token_rows,
        max(
            2,
            token_rows * TOPK * 5 // (4 * experts_all),
            (token_rows * TOPK + experts_all - 1) // experts_all,
        ),
    )
    capacity = -(-slots // 8) * 8
    full_rows = mixed_grad
    if lax.axis_size("tp") > 1:
        full_rows = lax.all_gather(mixed_grad, "tp", axis=1, tiled=True)
    own, *own_halves = join(keys, values, full_rows, expert_ids, combine, n_z, n_dp)

    def along_z(array, targets):
        pairs = [(2 * i + x, 2 * j + x) for i, j in targets for x in range(2)]
        return lax.ppermute(array, "ctx", pairs)

    def pick(table, array, ks, after):
        block = token_rows if array.shape[0] % own_halves[0].shape[0] else own_halves[0].shape[0]
        sizes = (ks, token_rows, n_dp, capacity)
        return pick_rows(place, table, own_halves[0].shape[0], array, block, *sizes, after)

    def across_x(k):
        pairs = [(i, i ^ 1) for i in range(2 * k, n_ctx) if k > 0 or i % 2 == 0]
        return lax.ppermute(columns[k], "ctx", pairs)

    columns, others = [own], []
    for k in range(1, n_z):
        others.append(across_x(k - 1))
        if k == 2:
            own_picked = pick(own_halves[0], full_rows, (0,), (columns[1],))
        if k > 2:
            held = lax.optimization_barrier((columns[-1], *others[k - 3 : k - 1]))
            columns[-1], *others[k - 3 : k - 1] = held
        if k == n_z - 1:
            columns[-1], own_picked = lax.optimization_barrier((columns[-1], own_picked))
        columns.append(along_z(columns[-1], [(i, i + 1) for i in range(k - 1, n_z - 1)]))
    columns[-1], others[-1] = lax.optimization_barrier((columns[-1], others[-1]))
    others.append(across_x(n_z - 1))
    blocks = [block for pair in zip(columns, others) for block in pair]

    plane_groups = [
        [d * n_ctx + 2 * i + j for d in range(n_dp) for j in range(2)] for i in range(n_z)
    ]
    line_groups = [[2 * i + x for i in range(n_z)] for x in range(2)]
    first_half, columns[n_z - 1] = lax.optimization_barrier((own_halves[0], columns[n_z - 1]))
    last_half, columns[n_z - 1] = lax.optimization_barrier((own_halves[1], columns[n_z - 1]))
    all_halves = [
        lax.all_gather(half, "ctx", axis=0, tiled=True, axis_index_groups=line_groups)
        for half in (first_half, last_half)
    ]

    def exchange(picked):
        return lax.all_to_all(
            picked,
            ("dp", "ctx"),
            split_axis=0,
            concat_axis=0,
            tiled=True,
            axis_index_groups=plane_groups,
        )

    def cross(array):
        return lax.ppermute(array, "ctx", [(i, i ^ 1) for i in range(n_ctx)])

    counts = [1] if kv_local == 1 else [kv_local // 2, kv_local - kv_local // 2]
    rest = tuple(range(1, n_z))
    own_picked, columns[n_z - 1] = lax.optimization_barrier((own_picked, columns[n_z - 1]))
    got_own = exchange(own_picked)
    query_grad, mine, other = attention(
        place, queries[0], out_grad[0], blocks, 0, counts[0], None, (own_picked,)
    )
    crossed = cross(other)
    others = []
    if len(counts) > 1:
        query_grad, *others = attention(
            place, queries[0], out_grad[0], blocks, counts[0], counts[1], query_grad
        )
    picked = pick(all_halves[0], all_halves[0], rest, (query_grad,))
    picked, crossed = lax.optimization_barrier((picked, crossed))
    got_first = exchange(picked)
    picked = pick(all_halves[0], all_halves[1], rest, (picked,))
    got_last = exchange(picked)
    total = lax.psum_scatter(
        fold(mine, crossed, others),
        "ctx",
        scatter_dimension=0,
        tiled=True,
        axis_index_groups=line_groups,
    )
    sizes = (n_z, n_dp, capacity, slots)
    hidden_grad = expert_rows(place, got_own, (0,), w_down, *sizes, None, None, (picked,))
    base = partial_rows(got_first, w_down)
    total, base, hidden_grad = lax.optimization_barrier((total, base, hidden_grad))
    last = [cross(total[:, -others[1].shape[1] :])] if others else []
    key_grad, value_grad = finish(counts, total, last, base)
    hidden_grad = expert_rows(place, got_last, rest, w_down, *sizes, base, hidden_grad)
    return (query_grad[None], key_grad, value_grad, hidden_grad)


def solution(mesh):
    placed = (
        P("dp", "ctx", "tp"),
        P("dp", "ctx", "tp"),
        P("dp", "ctx", "tp"),
        P("dp", "ctx", "tp"),
        P(("dp", "ctx"), "tp"),
        P(("dp", "ctx"), None),
        P(("dp", "ctx"), None),
        P(("dp", "ctx"), "tp", None),
    )
    return jax.shard_map(
        per_device,
        mesh=mesh,
        in_specs=placed,
        out_specs=(
            P("dp", "ctx", "tp"),
            P("dp", "ctx", "tp"),
            P("dp", "ctx", "tp"),
            P(("dp", "ctx"), None, None, "tp"),
        ),
        check_vma=False,
    )
```

```python
import functools
import math

import jax
import jax.numpy as jnp
from jax import lax
from jax.experimental import pallas as pl
from jax.experimental.pallas import tpu as pltpu
from jax.sharding import PartitionSpec as P

HEADS = 32
KV_HEADS = 4
HEAD_DIM = 128
TOPK = 8

masked_score = -1e30
vmem_limit = 56 * 1024 * 1024
small_cost = pl.CostEstimate(flops=1, bytes_accessed=1, transcendentals=0)


def mul(a, b):
    return jnp.dot(a, b, preferred_element_type=jnp.float32)


def attention_kernel(n_blocks, heads_step, rows, n_parts, place, q_ref, do_ref, *refs):
    kv_refs = refs[:n_blocks]
    dq_ref, mine_ref, other_ref = refs[-13:-10]
    kv_s, kt_s, q_s, do_s, qt_s, dot_s, s_s, dp_s, dkv_s, dqt_s = refs[-10:]
    part = pl.program_id(1)
    pair = 2 * rows
    width = heads_step * rows
    z, x = place[0], place[1]
    scale = HEAD_DIM ** (-0.5)
    to_exp2 = scale * math.log2(math.e)
    for i, ref in enumerate(kv_refs):
        kv_s[i * rows : (i + 1) * rows, :] = ref[...]
        kt_s[i // 2, :, (i % 2) * rows : (i % 2 + 1) * rows] = ref[:, :HEAD_DIM].T
    for h in range(heads_step):
        lanes = slice(h * HEAD_DIM, (h + 1) * HEAD_DIM)
        here = slice(h * rows, (h + 1) * rows)
        q_s[here, :] = q_ref[:, lanes]
        do_s[here, :] = do_ref[:, lanes]
        qt_s[:, here] = q_ref[:, lanes].T
        dot_s[:, here] = do_ref[:, lanes].T

    def part_of(k):
        return pl.ds(pl.multiple_of(k * pair, pair), pair)

    cut = math.gcd(width, 256)
    slices = [slice(i, i + cut) for i in range(0, width, cut)]

    def scores(k, tops, first):
        results = []
        for here, top in zip(slices, tops):
            s = mul(kv_s[part_of(k), :HEAD_DIM], qt_s[:, here])
            if first:
                key = lax.broadcasted_iota(jnp.int32, (pair, cut), 0)
                query = lax.broadcasted_iota(jnp.int32, (pair, cut), 1) & (rows - 1)
                bound = jnp.where(key < rows, query, jnp.where(x == 1, pair, -1))
                s = jnp.where(key <= bound, s, masked_score)
            s_s[part_of(k), here] = s
            results.append(jnp.maximum(top, jnp.max(s, axis=0, keepdims=True)))
        return tuple(results)

    tops = scores(0, tuple(jnp.full((1, cut), masked_score, jnp.float32) for _ in slices), True)
    tops = lax.fori_loop(1, z + 1, functools.partial(scores, first=False), tops)

    def sums(k, carry):
        results = []
        for here, top, (total, accum) in zip(slices, tops, carry):
            dp = mul(kv_s[part_of(k), HEAD_DIM:], dot_s[:, here])
            e = jnp.exp2((s_s[part_of(k), here] - top) * to_exp2)
            s_s[part_of(k), here] = e
            dp_s[part_of(k), here] = dp
            results.append(
                (
                    total + jnp.sum(e, axis=0, keepdims=True),
                    accum + jnp.sum(e * dp, axis=0, keepdims=True),
                )
            )
        return tuple(results)

    zero = jnp.zeros((1, cut), jnp.float32)
    stats = lax.fori_loop(0, z + 1, sums, tuple((zero, zero) for _ in slices))
    shares = [1.0 / total for total, _ in stats]
    deltas = [accum * share for (_, accum), share in zip(stats, shares)]
    dqt_s[...] = jnp.zeros_like(dqt_s)

    def grads(k, carry):
        dk = jnp.zeros((pair, HEAD_DIM), jnp.float32)
        dv = jnp.zeros((pair, HEAD_DIM), jnp.float32)
        for here, share, delta in zip(slices, shares, deltas):
            p = s_s[part_of(k), here] * share
            ds = (p * (dp_s[part_of(k), here] - delta)).astype(jnp.bfloat16)
            dv = dv + mul(p.astype(jnp.bfloat16), do_s[here, :])
            dk = dk + mul(ds, q_s[here, :])
            dqt_s[:, here] += mul(kt_s[k], ds)
        dk = dk * scale
        if n_parts > 1:
            dk = dk + jnp.where(part == 0, 0.0, dkv_s[part_of(k), :HEAD_DIM])
            dv = dv + jnp.where(part == 0, 0.0, dkv_s[part_of(k), HEAD_DIM:])
        dkv_s[part_of(k), :HEAD_DIM] = dk
        dkv_s[part_of(k), HEAD_DIM:] = dv
        return carry

    lax.fori_loop(0, z + 1, grads, 0)
    for h in range(heads_step):
        part_t = dqt_s[:, h * rows : (h + 1) * rows] * scale
        dq_ref[:, h * HEAD_DIM : (h + 1) * HEAD_DIM] = part_t.T.astype(jnp.bfloat16)
    for i in range(n_blocks):
        held = dkv_s[i * rows : (i + 1) * rows, :]
        ref = mine_ref if i % 2 == 0 else other_ref
        at = lax.rem(z - i // 2 + n_blocks // 2, n_blocks // 2) * rows
        held = jnp.where(i // 2 <= z, held, 0.0).astype(jnp.bfloat16)
        ref[pl.ds(pl.multiple_of(at, rows), rows), :] = held


def attention(place, queries, out_grad, kv_blocks, first, count, query_grad, after=()):
    rows, q_width = queries.shape
    n_blocks = len(kv_blocks)
    group = HEADS // KV_HEADS
    keys = n_blocks * rows
    heads_step = max(1, min(group, 2**20 // (keys * rows)))
    n_parts = group // heads_step
    width = heads_step * rows
    q_spec = pl.BlockSpec(
        (rows, heads_step * HEAD_DIM), lambda g, u: (0, (g + first) * n_parts + u)
    )
    kv_spec = pl.BlockSpec((rows, 2 * HEAD_DIM), lambda g, u: (0, g + first))
    part_spec = pl.BlockSpec((keys // 2, 2 * HEAD_DIM), lambda g, u: (0, g))
    part_shape = jax.ShapeDtypeStruct((keys // 2, count * 2 * HEAD_DIM), jnp.bfloat16)
    held = [] if query_grad is None else [query_grad]
    return pl.pallas_call(
        functools.partial(attention_kernel, n_blocks, heads_step, rows, n_parts),
        grid=(count, n_parts),
        in_specs=[pl.BlockSpec(memory_space=pltpu.SMEM), q_spec, q_spec]
        + [kv_spec] * n_blocks
        + [pl.BlockSpec(memory_space=pl.ANY)] * (len(held) + len(after)),
        out_specs=[q_spec, part_spec, part_spec],
        out_shape=[jax.ShapeDtypeStruct((rows, q_width), jnp.bfloat16), part_shape, part_shape],
        scratch_shapes=[
            pltpu.VMEM((keys, 2 * HEAD_DIM), jnp.bfloat16),
            pltpu.VMEM((n_blocks // 2, HEAD_DIM, 2 * rows), jnp.bfloat16),
            pltpu.VMEM((width, HEAD_DIM), jnp.bfloat16),
            pltpu.VMEM((width, HEAD_DIM), jnp.bfloat16),
            pltpu.VMEM((HEAD_DIM, width), jnp.bfloat16),
            pltpu.VMEM((HEAD_DIM, width), jnp.bfloat16),
            pltpu.VMEM((keys, width), jnp.float32),
            pltpu.VMEM((keys, width), jnp.float32),
            pltpu.VMEM((keys, 2 * HEAD_DIM), jnp.float32),
            pltpu.VMEM((HEAD_DIM, width), jnp.float32),
        ],
        input_output_aliases={3 + n_blocks: 0} if held else {},
        compiler_params=pltpu.CompilerParams(
            vmem_limit_bytes=vmem_limit, dimension_semantics=("arbitrary", "arbitrary")
        ),
        cost_estimate=small_cost
        if held
        else pl.CostEstimate(
            flops=100 * rows * keys * group * count * HEAD_DIM,
            bytes_accessed=8 * (rows * group + keys) * count * HEAD_DIM,
            transcendentals=rows * keys * group * count,
        ),
        name="attention_backward",
    )(place, queries, out_grad, *kv_blocks, *held, *after)


def fold_kernel(mine_ref, *refs):
    out_ref, width = refs[-1], mine_ref.shape[1]
    total = mine_ref[...].astype(jnp.float32) + refs[0][...].astype(jnp.float32)
    out_ref[:, :width] = total.astype(out_ref.dtype)
    first = width
    for ref in refs[1:-1]:
        out_ref[:, first : first + ref.shape[1]] = ref[...]
        first += ref.shape[1]


def fold(mine, got, others):
    arrays = (mine, got, *others)
    rows, width = mine.shape[0], sum(part.shape[1] for part in arrays[1:])
    return pl.pallas_call(
        fold_kernel,
        grid=(4,),
        in_specs=[pl.BlockSpec((rows // 4, part.shape[1]), lambda i: (i, 0)) for part in arrays],
        out_specs=pl.BlockSpec((rows // 4, width), lambda i: (i, 0)),
        out_shape=jax.ShapeDtypeStruct((rows, width), jnp.bfloat16),
        compiler_params=pltpu.CompilerParams(vmem_limit_bytes=vmem_limit),
        cost_estimate=small_cost,
        name="fold",
    )(*arrays)


def finish_kernel(counts, total_ref, *refs):
    key_ref, value_ref = refs[-2:]
    size = 2 * HEAD_DIM
    for g in range(sum(counts)):
        lanes = slice(g * HEAD_DIM, (g + 1) * HEAD_DIM)
        held = total_ref[:, g * size : (g + 1) * size]
        if g >= counts[0]:
            at = (g - counts[0]) * size
            held = held.astype(jnp.float32) + refs[0][:, at : at + size].astype(jnp.float32)
            held = held.astype(jnp.bfloat16)
        key_ref[0, :, lanes] = held[:, :HEAD_DIM]
        value_ref[0, :, lanes] = held[:, HEAD_DIM:]


def finish(counts, total, crossed, after):
    shape = jax.ShapeDtypeStruct((1, total.shape[0], sum(counts) * HEAD_DIM), jnp.bfloat16)
    return pl.pallas_call(
        functools.partial(finish_kernel, counts),
        in_specs=[pl.BlockSpec(memory_space=pltpu.VMEM)] * (1 + len(crossed))
        + [pl.BlockSpec(memory_space=pl.ANY)],
        out_shape=[shape, shape],
        compiler_params=pltpu.CompilerParams(vmem_limit_bytes=vmem_limit),
        cost_estimate=small_cost,
        name="finish",
    )(total, *crossed, after)


def join_kernel(
    n_z, n_dp, key_ref, value_ref, rows_ref, ids_ref, combine_ref, kv_ref, ext_ref, rest_ref
):
    for g in range(kv_ref.shape[1] // (2 * HEAD_DIM)):
        lanes = slice(g * HEAD_DIM, (g + 1) * HEAD_DIM)
        kv_ref[:, 2 * g * HEAD_DIM : (2 * g + 1) * HEAD_DIM] = key_ref[0, :, lanes]
        kv_ref[:, (2 * g + 1) * HEAD_DIM : (2 * g + 2) * HEAD_DIM] = value_ref[0, :, lanes]
    tokens, feat = rows_ref.shape
    lines = 4 * n_dp
    line = lax.broadcasted_iota(jnp.int32, (n_z * lines, tokens), 0)
    kind = line % lines
    member = kind % (2 * n_dp)
    expert = (member // 2) * (2 * n_z) + line // lines * 2 + member % 2
    hits = jnp.zeros((n_z * lines, tokens), jnp.float32)
    weights = jnp.zeros((n_z * lines, tokens), jnp.float32)
    combine = combine_ref[...].astype(jnp.float32)
    for k in range(TOPK):
        hit = ids_ref[k : k + 1, :] == expert
        hits = hits + jnp.where(hit, 1.0, 0.0)
        weights = weights + jnp.where(hit, combine[k : k + 1, :], 0.0)
    before = lax.broadcasted_iota(jnp.int32, (tokens, tokens), 0) < lax.broadcasted_iota(
        jnp.int32, (tokens, tokens), 1
    )
    ranks = mul(hits.astype(jnp.bfloat16), jnp.where(before, 1.0, 0.0).astype(jnp.bfloat16))
    table = jnp.where(kind < 2 * n_dp, jnp.where(hits > 0.0, ranks, -1.0), weights)
    half = feat // 2
    ext_ref[:tokens, :] = rows_ref[:, :half]
    rest_ref[...] = rows_ref[:, half:]
    squares = [table[i * lines : (i + 1) * lines] for i in range(n_z)]
    per_row = half // tokens
    squares += [jnp.zeros((lines, tokens), jnp.float32)] * (-n_z % per_row)
    for i in range(len(squares) // per_row):
        line_of = jnp.concatenate(squares[i * per_row : (i + 1) * per_row], axis=1)
        here = slice(tokens + i * lines, tokens + (i + 1) * lines)
        ext_ref[here, :] = line_of.astype(jnp.bfloat16)


def join(keys, values, full_rows, ids, combine, n_z, n_dp):
    rows, width = keys.shape[1:]
    tokens, feat = full_rows.shape
    return pl.pallas_call(
        functools.partial(join_kernel, n_z, n_dp),
        out_shape=[
            jax.ShapeDtypeStruct((rows, 2 * width), jnp.bfloat16),
            jax.ShapeDtypeStruct(
                (tokens + 4 * n_dp * -(-2 * n_z * tokens // feat), feat // 2), jnp.bfloat16
            ),
            jax.ShapeDtypeStruct((tokens, feat // 2), jnp.bfloat16),
        ],
        compiler_params=pltpu.CompilerParams(vmem_limit_bytes=vmem_limit),
        cost_estimate=small_cost,
        name="join",
    )(keys, values, full_rows, ids.T, combine.T)


def pick_kernel(count, n_dp, capacity, place, *refs):
    table_refs, row_refs = refs[:count], refs[count : 2 * count]
    out_ref, pick_s = refs[-2:]
    tokens = pick_s.shape[2]

    @pl.when(pl.program_id(0) == 0)
    def _():
        for i, ref in enumerate(table_refs):
            table = ref[...].astype(jnp.float32)
            slot = lax.broadcasted_iota(jnp.int32, (capacity, tokens), 0).astype(jnp.float32)
            picks = [
                jnp.where(
                    slot == table[q : q + 1, :], table[2 * n_dp + q : 2 * n_dp + q + 1, :], 0.0
                )
                for q in range(2 * n_dp)
            ]
            pick_s[i] = jnp.concatenate(picks, axis=0).astype(jnp.bfloat16)

    results = [mul(pick_s[i], ref[:tokens, :]) for i, ref in enumerate(row_refs)]
    for q in range(2 * n_dp):
        here = slice(q * capacity, (q + 1) * capacity)
        total = jnp.concatenate([part[here] for part in results], axis=0)
        size = count * capacity
        out_ref[q * size : (q + 1) * size, :] = total.astype(jnp.bfloat16)


def pick_rows(place, table, block_table, array, block, ks, tokens, n_dp, capacity, after=()):
    lines, feat = 4 * n_dp, array.shape[1]
    step = math.gcd(feat, 1024 if len(ks) == 1 else 512)
    out_rows = len(ks) * 2 * n_dp * capacity
    per_row = table.shape[1] // tokens

    def at(place, k, whole, part):
        return (place[0] & (whole.shape[0] // part - 1)) ^ k

    def table_spec(k):
        def index(f, place):
            first = (at(place, k, table, block_table) * block_table + tokens) // lines
            return first + place[0] // per_row, place[0] % per_row

        return pl.BlockSpec((lines, tokens), index)

    def rows_spec(k):
        return pl.BlockSpec((block, step), lambda f, place: (at(place, k, array, block), f))

    return pl.pallas_call(
        functools.partial(pick_kernel, len(ks), n_dp, capacity),
        grid_spec=pltpu.PrefetchScalarGridSpec(
            num_scalar_prefetch=1,
            grid=(feat // step,),
            in_specs=[table_spec(k) for k in ks]
            + [rows_spec(k) for k in ks]
            + [pl.BlockSpec(memory_space=pl.ANY)] * len(after),
            out_specs=pl.BlockSpec((out_rows, step), lambda f, place: (0, f)),
            scratch_shapes=[pltpu.VMEM((len(ks), 2 * n_dp * capacity, tokens), jnp.bfloat16)],
        ),
        out_shape=jax.ShapeDtypeStruct((out_rows, feat), jnp.bfloat16),
        compiler_params=pltpu.CompilerParams(vmem_limit_bytes=vmem_limit),
        cost_estimate=small_cost,
        name="pick_rows",
    )(place, *[table] * len(ks), *[array] * len(ks), *after)


def partial_kernel(rows_ref, w_ref, out_ref):
    out_ref[...] = lax.dot_general(
        rows_ref[...], w_ref[0], (((1,), (1,)), ((), ())), preferred_element_type=jnp.float32
    )


def partial_rows(rows, w_down):
    count, half = rows.shape
    hid = w_down.shape[1]
    step = math.gcd(hid, 512)
    return pl.pallas_call(
        partial_kernel,
        grid=(hid // step,),
        in_specs=[
            pl.BlockSpec((count, half), lambda n: (0, 0)),
            pl.BlockSpec((1, step, half), lambda n: (0, n, 0)),
        ],
        out_specs=pl.BlockSpec((count, step), lambda n: (0, n)),
        out_shape=jax.ShapeDtypeStruct((count, hid), jnp.float32),
        compiler_params=pltpu.CompilerParams(vmem_limit_bytes=vmem_limit),
        cost_estimate=small_cost,
        name="partial_rows",
    )(rows, w_down)


def expert_kernel(ks, with_base, n_z, n_dp, capacity, slots, place, rows_ref, w_ref, *refs):
    out_ref, out_s, sem = refs[-3:]
    step, steps = pl.program_id(0), out_s.shape[0]
    width = out_s.shape[-1]
    blocks = [(q, k) for q in range(2 * n_dp) for k in ks]
    result = lax.dot_general(
        rows_ref[...], w_ref[0], (((1,), (1,)), ((), ())), preferred_element_type=jnp.float32
    )
    if with_base:
        result = result + refs[0][...]
    for i in range(len(blocks)):
        out_s[step, i] = result[i * capacity : i * capacity + slots].astype(jnp.bfloat16)

    def copies(at):
        z = place[0]
        for i, (q, k) in enumerate(blocks):
            source = (q // 2) * (2 * n_z) + (z ^ k) * 2 + q % 2
            lanes = pl.ds(pl.multiple_of(at * width, width), width)
            yield pltpu.make_async_copy(
                out_s.at[at, i], out_ref.at[0, source, :, lanes], sem.at[at, i]
            )

    for copy in copies(step):
        copy.start()

    @pl.when(step == steps - 1)
    def _():
        for at in range(steps):
            for copy in copies(at):
                copy.wait()


def expert_rows(place, rows, ks, w_down, n_z, n_dp, capacity, slots, base, hidden_grad, after=()):
    hid = w_down.shape[1]
    step = math.gcd(hid, 512)
    count = rows.shape[0] // capacity
    part = w_down.shape[2] // rows.shape[1] - 1
    extra = [] if base is None else [base]
    held = [] if hidden_grad is None else [hidden_grad]
    return pl.pallas_call(
        functools.partial(expert_kernel, ks, bool(extra), n_z, n_dp, capacity, slots),
        grid=(hid // step,),
        in_specs=[
            pl.BlockSpec(memory_space=pltpu.SMEM),
            pl.BlockSpec(rows.shape, lambda n: (0, 0)),
            pl.BlockSpec((1, step, rows.shape[1]), lambda n: (0, n, part)),
        ]
        + [pl.BlockSpec((rows.shape[0], step), lambda n: (0, n))] * len(extra)
        + [pl.BlockSpec(memory_space=pl.ANY)] * (len(held) + len(after)),
        out_specs=pl.BlockSpec(memory_space=pl.ANY),
        out_shape=jax.ShapeDtypeStruct((1, n_dp * 2 * n_z, slots, hid), jnp.bfloat16),
        scratch_shapes=[
            pltpu.VMEM((hid // step, count, slots, step), jnp.bfloat16),
            pltpu.SemaphoreType.DMA((hid // step, count)),
        ],
        input_output_aliases={3 + len(extra): 0} if held else {},
        compiler_params=pltpu.CompilerParams(vmem_limit_bytes=vmem_limit),
        cost_estimate=small_cost,
        name="expert_rows",
    )(place, rows, w_down, *extra, *held, *after)


def per_device(queries, keys, values, out_grad, mixed_grad, expert_ids, combine, w_down):
    rows_dev = queries.shape[1]
    kv_local = keys.shape[2] // HEAD_DIM
    n_ctx, n_dp = lax.axis_size("ctx"), lax.axis_size("dp")
    n_z = n_ctx // 2
    position = lax.axis_index("ctx")
    place = jnp.stack([position >> 1, position & 1]).astype(jnp.int32)
    token_rows = expert_ids.shape[0]
    experts_all = n_dp * n_ctx
    slots = min(
        token_rows,
        max(
            2,
            token_rows * TOPK * 5 // (4 * experts_all),
            (token_rows * TOPK + experts_all - 1) // experts_all,
        ),
    )
    capacity = -(-slots // 8) * 8
    full_rows = mixed_grad
    if lax.axis_size("tp") > 1:
        full_rows = lax.all_gather(mixed_grad, "tp", axis=1, tiled=True)
    own, *own_halves = join(keys, values, full_rows, expert_ids, combine, n_z, n_dp)

    def along_z(array, targets):
        pairs = [(2 * i + x, 2 * j + x) for i, j in targets for x in range(2)]
        return lax.ppermute(array, "ctx", pairs)

    def pick(table, array, ks, after):
        block = token_rows if array.shape[0] % own_halves[0].shape[0] else own_halves[0].shape[0]
        sizes = (ks, token_rows, n_dp, capacity)
        return pick_rows(place, table, own_halves[0].shape[0], array, block, *sizes, after)

    def across_x(k):
        pairs = [(i, i ^ 1) for i in range(2 * k, n_ctx) if k > 0 or i % 2 == 0]
        return lax.ppermute(columns[k], "ctx", pairs)

    columns, others = [own], []
    for k in range(1, n_z):
        others.append(across_x(k - 1))
        if k > 2:
            held = lax.optimization_barrier((columns[-1], *others[k - 3 : k - 1]))
            columns[-1], *others[k - 3 : k - 1] = held
        columns.append(along_z(columns[-1], [(i, i + 1) for i in range(k - 1, n_z - 1)]))
    columns[-1], others[-1] = lax.optimization_barrier((columns[-1], others[-1]))
    others.append(across_x(n_z - 1))
    blocks = [block for pair in zip(columns, others) for block in pair]

    plane_groups = [
        [d * n_ctx + 2 * i + j for d in range(n_dp) for j in range(2)] for i in range(n_z)
    ]
    line_groups = [[2 * i + x for i in range(n_z)] for x in range(2)]
    last_half, columns[n_z - 1] = lax.optimization_barrier((own_halves[1], columns[n_z - 1]))
    all_halves = [
        lax.all_gather(half, "ctx", axis=0, tiled=True, axis_index_groups=line_groups)
        for half in (own_halves[0], last_half)
    ]

    def exchange(picked):
        return lax.all_to_all(
            picked,
            ("dp", "ctx"),
            split_axis=0,
            concat_axis=0,
            tiled=True,
            axis_index_groups=plane_groups,
        )

    def cross(array):
        return lax.ppermute(array, "ctx", [(i, i ^ 1) for i in range(n_ctx)])

    counts = [1] if kv_local == 1 else [kv_local // 2, kv_local - kv_local // 2]
    every = tuple(range(n_z))
    picked = pick(all_halves[0], all_halves[0], every, ())
    picked, columns[n_z - 1] = lax.optimization_barrier((picked, columns[n_z - 1]))
    got_first = exchange(picked)
    query_grad, mine, other = attention(
        place, queries[0], out_grad[0], blocks, 0, counts[0], None, (picked,)
    )
    crossed = cross(other)
    others = []
    if len(counts) > 1:
        query_grad, *others = attention(
            place, queries[0], out_grad[0], blocks, counts[0], counts[1], query_grad
        )
    picked = pick(all_halves[0], all_halves[1], every, (query_grad,))
    picked, crossed = lax.optimization_barrier((picked, crossed))
    got_last = exchange(picked)
    total = lax.psum_scatter(
        fold(mine, crossed, others),
        "ctx",
        scatter_dimension=0,
        tiled=True,
        axis_index_groups=line_groups,
    )
    sizes = (n_z, n_dp, capacity, slots)
    base = partial_rows(got_first, w_down)
    total, base = lax.optimization_barrier((total, base))
    last = [cross(total[:, -others[1].shape[1] :])] if others else []
    key_grad, value_grad = finish(counts, total, last, base)
    hidden_grad = expert_rows(place, got_last, every, w_down, *sizes, base, None)
    return (query_grad[None], key_grad, value_grad, hidden_grad)


def solution(mesh):
    placed = (
        P("dp", "ctx", "tp"),
        P("dp", "ctx", "tp"),
        P("dp", "ctx", "tp"),
        P("dp", "ctx", "tp"),
        P(("dp", "ctx"), "tp"),
        P(("dp", "ctx"), None),
        P(("dp", "ctx"), None),
        P(("dp", "ctx"), "tp", None),
    )
    return jax.shard_map(
        per_device,
        mesh=mesh,
        in_specs=placed,
        out_specs=(
            P("dp", "ctx", "tp"),
            P("dp", "ctx", "tp"),
            P("dp", "ctx", "tp"),
            P(("dp", "ctx"), None, None, "tp"),
        ),
        check_vma=False,
    )
```

```python
import functools
import math

import jax
import jax.numpy as jnp
from jax import lax
from jax.experimental import pallas as pl
from jax.experimental.pallas import tpu as pltpu
from jax.sharding import PartitionSpec as P

HEADS = 32
KV_HEADS = 4
HEAD_DIM = 128
TOPK = 8

masked_score = -1e30
vmem_limit = 56 * 1024 * 1024
small_cost = pl.CostEstimate(flops=1, bytes_accessed=1, transcendentals=0)


def mul(a, b):
    return jnp.dot(a, b, preferred_element_type=jnp.float32)


def attention_kernel(n_blocks, heads_step, rows, n_parts, place, q_ref, do_ref, *refs):
    kv_refs = refs[:n_blocks]
    dq_ref, mine_ref, other_ref = refs[-13:-10]
    kv_s, kt_s, q_s, do_s, qt_s, dot_s, s_s, dp_s, dkv_s, dqt_s = refs[-10:]
    part = pl.program_id(1)
    pair = 2 * rows
    width = heads_step * rows
    z, x = place[0], place[1]
    scale = HEAD_DIM ** (-0.5)
    to_exp2 = scale * math.log2(math.e)
    for i, ref in enumerate(kv_refs):
        kv_s[i * rows : (i + 1) * rows, :] = ref[...]
        kt_s[i // 2, :, (i % 2) * rows : (i % 2 + 1) * rows] = ref[:, :HEAD_DIM].T
    for h in range(heads_step):
        lanes = slice(h * HEAD_DIM, (h + 1) * HEAD_DIM)
        here = slice(h * rows, (h + 1) * rows)
        q_s[here, :] = q_ref[:, lanes]
        do_s[here, :] = do_ref[:, lanes]
        qt_s[:, here] = q_ref[:, lanes].T
        dot_s[:, here] = do_ref[:, lanes].T

    def part_of(k):
        return pl.ds(pl.multiple_of(k * pair, pair), pair)

    cut = math.gcd(width, 256)
    slices = [slice(i, i + cut) for i in range(0, width, cut)]

    def scores(k, tops, first):
        results = []
        for here, top in zip(slices, tops):
            s = mul(kv_s[part_of(k), :HEAD_DIM], qt_s[:, here])
            if first:
                key = lax.broadcasted_iota(jnp.int32, (pair, cut), 0)
                query = lax.broadcasted_iota(jnp.int32, (pair, cut), 1) & (rows - 1)
                bound = jnp.where(key < rows, query, jnp.where(x == 1, pair, -1))
                s = jnp.where(key <= bound, s, masked_score)
            s_s[part_of(k), here] = s
            results.append(jnp.maximum(top, jnp.max(s, axis=0, keepdims=True)))
        return tuple(results)

    tops = scores(0, tuple(jnp.full((1, cut), masked_score, jnp.float32) for _ in slices), True)
    tops = lax.fori_loop(1, z + 1, functools.partial(scores, first=False), tops)

    def sums(k, carry):
        results = []
        for here, top, (total, accum) in zip(slices, tops, carry):
            dp = mul(kv_s[part_of(k), HEAD_DIM:], dot_s[:, here])
            e = jnp.exp2((s_s[part_of(k), here] - top) * to_exp2)
            s_s[part_of(k), here] = e
            dp_s[part_of(k), here] = dp
            results.append(
                (
                    total + jnp.sum(e, axis=0, keepdims=True),
                    accum + jnp.sum(e * dp, axis=0, keepdims=True),
                )
            )
        return tuple(results)

    zero = jnp.zeros((1, cut), jnp.float32)
    stats = lax.fori_loop(0, z + 1, sums, tuple((zero, zero) for _ in slices))
    shares = [1.0 / total for total, _ in stats]
    deltas = [accum * share for (_, accum), share in zip(stats, shares)]
    dqt_s[...] = jnp.zeros_like(dqt_s)

    def grads(k, carry):
        dk = jnp.zeros((pair, HEAD_DIM), jnp.float32)
        dv = jnp.zeros((pair, HEAD_DIM), jnp.float32)
        for here, share, delta in zip(slices, shares, deltas):
            p = s_s[part_of(k), here] * share
            ds = (p * (dp_s[part_of(k), here] - delta)).astype(jnp.bfloat16)
            dv = dv + mul(p.astype(jnp.bfloat16), do_s[here, :])
            dk = dk + mul(ds, q_s[here, :])
            dqt_s[:, here] += mul(kt_s[k], ds)
        dk = dk * scale
        if n_parts > 1:
            dk = dk + jnp.where(part == 0, 0.0, dkv_s[part_of(k), :HEAD_DIM])
            dv = dv + jnp.where(part == 0, 0.0, dkv_s[part_of(k), HEAD_DIM:])
        dkv_s[part_of(k), :HEAD_DIM] = dk
        dkv_s[part_of(k), HEAD_DIM:] = dv
        return carry

    lax.fori_loop(0, z + 1, grads, 0)
    for h in range(heads_step):
        part_t = dqt_s[:, h * rows : (h + 1) * rows] * scale
        dq_ref[:, h * HEAD_DIM : (h + 1) * HEAD_DIM] = part_t.T.astype(jnp.bfloat16)
    for i in range(n_blocks):
        held = dkv_s[i * rows : (i + 1) * rows, :]
        ref = mine_ref if i % 2 == 0 else other_ref
        at = lax.rem(z - i // 2 + n_blocks // 2, n_blocks // 2) * rows
        held = jnp.where(i // 2 <= z, held, 0.0).astype(jnp.bfloat16)
        ref[pl.ds(pl.multiple_of(at, rows), rows), :] = held


def attention(place, queries, out_grad, kv_blocks, first, count, query_grad, after=()):
    rows, q_width = queries.shape
    n_blocks = len(kv_blocks)
    group = HEADS // KV_HEADS
    keys = n_blocks * rows
    heads_step = max(1, min(group, 2**20 // (keys * rows)))
    n_parts = group // heads_step
    width = heads_step * rows
    q_spec = pl.BlockSpec(
        (rows, heads_step * HEAD_DIM), lambda g, u: (0, (g + first) * n_parts + u)
    )
    kv_spec = pl.BlockSpec((rows, 2 * HEAD_DIM), lambda g, u: (0, g + first))
    part_spec = pl.BlockSpec((keys // 2, 2 * HEAD_DIM), lambda g, u: (0, g))
    part_shape = jax.ShapeDtypeStruct((keys // 2, count * 2 * HEAD_DIM), jnp.bfloat16)
    held = [] if query_grad is None else [query_grad]
    return pl.pallas_call(
        functools.partial(attention_kernel, n_blocks, heads_step, rows, n_parts),
        grid=(count, n_parts),
        in_specs=[pl.BlockSpec(memory_space=pltpu.SMEM), q_spec, q_spec]
        + [kv_spec] * n_blocks
        + [pl.BlockSpec(memory_space=pl.ANY)] * (len(held) + len(after)),
        out_specs=[q_spec, part_spec, part_spec],
        out_shape=[jax.ShapeDtypeStruct((rows, q_width), jnp.bfloat16), part_shape, part_shape],
        scratch_shapes=[
            pltpu.VMEM((keys, 2 * HEAD_DIM), jnp.bfloat16),
            pltpu.VMEM((n_blocks // 2, HEAD_DIM, 2 * rows), jnp.bfloat16),
            pltpu.VMEM((width, HEAD_DIM), jnp.bfloat16),
            pltpu.VMEM((width, HEAD_DIM), jnp.bfloat16),
            pltpu.VMEM((HEAD_DIM, width), jnp.bfloat16),
            pltpu.VMEM((HEAD_DIM, width), jnp.bfloat16),
            pltpu.VMEM((keys, width), jnp.float32),
            pltpu.VMEM((keys, width), jnp.float32),
            pltpu.VMEM((keys, 2 * HEAD_DIM), jnp.float32),
            pltpu.VMEM((HEAD_DIM, width), jnp.float32),
        ],
        input_output_aliases={3 + n_blocks: 0} if held else {},
        compiler_params=pltpu.CompilerParams(
            vmem_limit_bytes=vmem_limit, dimension_semantics=("arbitrary", "arbitrary")
        ),
        cost_estimate=small_cost
        if held
        else pl.CostEstimate(
            flops=100 * rows * keys * group * count * HEAD_DIM,
            bytes_accessed=8 * (rows * group + keys) * count * HEAD_DIM,
            transcendentals=rows * keys * group * count,
        ),
        name="attention_backward",
    )(place, queries, out_grad, *kv_blocks, *held, *after)


def fold_kernel(mine_ref, *refs):
    out_ref, width = refs[-1], mine_ref.shape[1]
    total = mine_ref[...].astype(jnp.float32) + refs[0][...].astype(jnp.float32)
    out_ref[:, :width] = total.astype(out_ref.dtype)
    first = width
    for ref in refs[1:-1]:
        out_ref[:, first : first + ref.shape[1]] = ref[...]
        first += ref.shape[1]


def fold(mine, got, others):
    arrays = (mine, got, *others)
    rows, width = mine.shape[0], sum(part.shape[1] for part in arrays[1:])
    return pl.pallas_call(
        fold_kernel,
        grid=(4,),
        in_specs=[pl.BlockSpec((rows // 4, part.shape[1]), lambda i: (i, 0)) for part in arrays],
        out_specs=pl.BlockSpec((rows // 4, width), lambda i: (i, 0)),
        out_shape=jax.ShapeDtypeStruct((rows, width), jnp.bfloat16),
        compiler_params=pltpu.CompilerParams(vmem_limit_bytes=vmem_limit),
        cost_estimate=small_cost,
        name="fold",
    )(*arrays)


def finish_kernel(counts, total_ref, *refs):
    key_ref, value_ref = refs[-2:]
    size = 2 * HEAD_DIM
    for g in range(sum(counts)):
        lanes = slice(g * HEAD_DIM, (g + 1) * HEAD_DIM)
        held = total_ref[:, g * size : (g + 1) * size]
        if g >= counts[0]:
            at = (g - counts[0]) * size
            held = held.astype(jnp.float32) + refs[0][:, at : at + size].astype(jnp.float32)
            held = held.astype(jnp.bfloat16)
        key_ref[0, :, lanes] = held[:, :HEAD_DIM]
        value_ref[0, :, lanes] = held[:, HEAD_DIM:]


def finish(counts, total, crossed, after):
    shape = jax.ShapeDtypeStruct((1, total.shape[0], sum(counts) * HEAD_DIM), jnp.bfloat16)
    return pl.pallas_call(
        functools.partial(finish_kernel, counts),
        in_specs=[pl.BlockSpec(memory_space=pltpu.VMEM)] * (1 + len(crossed))
        + [pl.BlockSpec(memory_space=pl.ANY)],
        out_shape=[shape, shape],
        compiler_params=pltpu.CompilerParams(vmem_limit_bytes=vmem_limit),
        cost_estimate=small_cost,
        name="finish",
    )(total, *crossed, after)


def join_kernel(key_ref, value_ref, kv_ref):
    for g in range(kv_ref.shape[1] // (2 * HEAD_DIM)):
        lanes = slice(g * HEAD_DIM, (g + 1) * HEAD_DIM)
        kv_ref[:, 2 * g * HEAD_DIM : (2 * g + 1) * HEAD_DIM] = key_ref[0, :, lanes]
        kv_ref[:, (2 * g + 1) * HEAD_DIM : (2 * g + 2) * HEAD_DIM] = value_ref[0, :, lanes]


def join(keys, values):
    rows, width = keys.shape[1:]
    return pl.pallas_call(
        join_kernel,
        out_shape=jax.ShapeDtypeStruct((rows, 2 * width), jnp.bfloat16),
        compiler_params=pltpu.CompilerParams(vmem_limit_bytes=vmem_limit),
        cost_estimate=small_cost,
        name="join",
    )(keys, values)


def table_kernel(n_z, n_dp, rows_ref, ids_ref, combine_ref, *refs):
    ext_ref, rest_ref = refs[-2:]
    tokens, feat = rows_ref.shape
    lines = 4 * n_dp
    line = lax.broadcasted_iota(jnp.int32, (n_z * lines, tokens), 0)
    kind = line % lines
    member = kind % (2 * n_dp)
    expert = (member // 2) * (2 * n_z) + line // lines * 2 + member % 2
    hits = jnp.zeros((n_z * lines, tokens), jnp.float32)
    weights = jnp.zeros((n_z * lines, tokens), jnp.float32)
    combine = combine_ref[...].astype(jnp.float32)
    for k in range(TOPK):
        hit = ids_ref[k : k + 1, :] == expert
        hits = hits + jnp.where(hit, 1.0, 0.0)
        weights = weights + jnp.where(hit, combine[k : k + 1, :], 0.0)
    before = lax.broadcasted_iota(jnp.int32, (tokens, tokens), 0) < lax.broadcasted_iota(
        jnp.int32, (tokens, tokens), 1
    )
    ranks = mul(hits.astype(jnp.bfloat16), jnp.where(before, 1.0, 0.0).astype(jnp.bfloat16))
    table = jnp.where(kind < 2 * n_dp, jnp.where(hits > 0.0, ranks, -1.0), weights)
    half = feat // 2
    ext_ref[:tokens, :] = rows_ref[:, :half]
    rest_ref[...] = rows_ref[:, half:]
    squares = [table[i * lines : (i + 1) * lines] for i in range(n_z)]
    per_row = half // tokens
    squares += [jnp.zeros((lines, tokens), jnp.float32)] * (-n_z % per_row)
    for i in range(len(squares) // per_row):
        line_of = jnp.concatenate(squares[i * per_row : (i + 1) * per_row], axis=1)
        here = slice(tokens + i * lines, tokens + (i + 1) * lines)
        ext_ref[here, :] = line_of.astype(jnp.bfloat16)


def halves(full_rows, ids, combine, n_z, n_dp, after):
    tokens, feat = full_rows.shape
    return pl.pallas_call(
        functools.partial(table_kernel, n_z, n_dp),
        in_specs=[pl.BlockSpec(memory_space=pltpu.VMEM)] * 3 + [pl.BlockSpec(memory_space=pl.ANY)],
        out_shape=[
            jax.ShapeDtypeStruct(
                (tokens + 4 * n_dp * -(-2 * n_z * tokens // feat), feat // 2), jnp.bfloat16
            ),
            jax.ShapeDtypeStruct((tokens, feat // 2), jnp.bfloat16),
        ],
        compiler_params=pltpu.CompilerParams(vmem_limit_bytes=vmem_limit),
        cost_estimate=small_cost,
        name="slot_table",
    )(full_rows, ids.T, combine.T, after)


def pick_kernel(count, n_dp, capacity, place, *refs):
    table_refs, row_refs = refs[:count], refs[count : 2 * count]
    out_ref, pick_s = refs[-2:]
    tokens = pick_s.shape[2]

    @pl.when(pl.program_id(0) == 0)
    def _():
        for i, ref in enumerate(table_refs):
            table = ref[...].astype(jnp.float32)
            slot = lax.broadcasted_iota(jnp.int32, (capacity, tokens), 0).astype(jnp.float32)
            picks = [
                jnp.where(
                    slot == table[q : q + 1, :], table[2 * n_dp + q : 2 * n_dp + q + 1, :], 0.0
                )
                for q in range(2 * n_dp)
            ]
            pick_s[i] = jnp.concatenate(picks, axis=0).astype(jnp.bfloat16)

    results = [mul(pick_s[i], ref[:tokens, :]) for i, ref in enumerate(row_refs)]
    for q in range(2 * n_dp):
        here = slice(q * capacity, (q + 1) * capacity)
        total = jnp.concatenate([part[here] for part in results], axis=0)
        size = count * capacity
        out_ref[q * size : (q + 1) * size, :] = total.astype(jnp.bfloat16)


def pick_rows(place, table, block_table, array, block, ks, tokens, n_dp, capacity, after=()):
    lines, feat = 4 * n_dp, array.shape[1]
    step = math.gcd(feat, 1024 if len(ks) == 1 else 512)
    out_rows = len(ks) * 2 * n_dp * capacity
    per_row = table.shape[1] // tokens

    def at(place, k, whole, part):
        return (place[0] & (whole.shape[0] // part - 1)) ^ k

    def table_spec(k):
        def index(f, place):
            first = (at(place, k, table, block_table) * block_table + tokens) // lines
            return first + place[0] // per_row, place[0] % per_row

        return pl.BlockSpec((lines, tokens), index)

    def rows_spec(k):
        return pl.BlockSpec((block, step), lambda f, place: (at(place, k, array, block), f))

    return pl.pallas_call(
        functools.partial(pick_kernel, len(ks), n_dp, capacity),
        grid_spec=pltpu.PrefetchScalarGridSpec(
            num_scalar_prefetch=1,
            grid=(feat // step,),
            in_specs=[table_spec(k) for k in ks]
            + [rows_spec(k) for k in ks]
            + [pl.BlockSpec(memory_space=pl.ANY)] * len(after),
            out_specs=pl.BlockSpec((out_rows, step), lambda f, place: (0, f)),
            scratch_shapes=[pltpu.VMEM((len(ks), 2 * n_dp * capacity, tokens), jnp.bfloat16)],
        ),
        out_shape=jax.ShapeDtypeStruct((out_rows, feat), jnp.bfloat16),
        compiler_params=pltpu.CompilerParams(vmem_limit_bytes=vmem_limit),
        cost_estimate=small_cost,
        name="pick_rows",
    )(place, *[table] * len(ks), *[array] * len(ks), *after)


def partial_kernel(rows_ref, w_ref, out_ref):
    out_ref[...] = lax.dot_general(
        rows_ref[...], w_ref[0], (((1,), (1,)), ((), ())), preferred_element_type=jnp.float32
    ).astype(jnp.bfloat16)


def partial_rows(rows, w_down):
    count, half = rows.shape
    hid = w_down.shape[1]
    step = math.gcd(hid, 512)
    return pl.pallas_call(
        partial_kernel,
        grid=(hid // step,),
        in_specs=[
            pl.BlockSpec((count, half), lambda n: (0, 0)),
            pl.BlockSpec((1, step, half), lambda n: (0, n, 0)),
        ],
        out_specs=pl.BlockSpec((count, step), lambda n: (0, n)),
        out_shape=jax.ShapeDtypeStruct((count, hid), jnp.bfloat16),
        compiler_params=pltpu.CompilerParams(vmem_limit_bytes=vmem_limit),
        cost_estimate=small_cost,
        name="partial_rows",
    )(rows, w_down)


def expert_kernel(ks, with_base, n_z, n_dp, capacity, slots, place, rows_ref, w_ref, *refs):
    out_ref, out_s, sem = refs[-3:]
    step, steps = pl.program_id(0), out_s.shape[0]
    width = out_s.shape[-1]
    blocks = [(q, k) for q in range(2 * n_dp) for k in ks]
    result = lax.dot_general(
        rows_ref[...], w_ref[0], (((1,), (1,)), ((), ())), preferred_element_type=jnp.float32
    )
    if with_base:
        result = result + refs[0][...].astype(jnp.float32)
    for i in range(len(blocks)):
        out_s[step, i] = result[i * capacity : i * capacity + slots].astype(jnp.bfloat16)

    def copies(at):
        z = place[0]
        for i, (q, k) in enumerate(blocks):
            source = (q // 2) * (2 * n_z) + (z ^ k) * 2 + q % 2
            lanes = pl.ds(pl.multiple_of(at * width, width), width)
            yield pltpu.make_async_copy(
                out_s.at[at, i], out_ref.at[0, source, :, lanes], sem.at[at, i]
            )

    for copy in copies(step):
        copy.start()

    @pl.when(step == steps - 1)
    def _():
        for at in range(steps):
            for copy in copies(at):
                copy.wait()


def expert_rows(place, rows, ks, w_down, n_z, n_dp, capacity, slots, base, hidden_grad, after=()):
    hid = w_down.shape[1]
    step = math.gcd(hid, 512 if base is None else 256)
    count = rows.shape[0] // capacity
    part = w_down.shape[2] // rows.shape[1] - 1
    extra = [] if base is None else [base]
    held = [] if hidden_grad is None else [hidden_grad]
    return pl.pallas_call(
        functools.partial(expert_kernel, ks, bool(extra), n_z, n_dp, capacity, slots),
        grid=(hid // step,),
        in_specs=[
            pl.BlockSpec(memory_space=pltpu.SMEM),
            pl.BlockSpec(rows.shape, lambda n: (0, 0)),
            pl.BlockSpec((1, step, rows.shape[1]), lambda n: (0, n, part)),
        ]
        + [pl.BlockSpec((rows.shape[0], step), lambda n: (0, n))] * len(extra)
        + [pl.BlockSpec(memory_space=pl.ANY)] * (len(held) + len(after)),
        out_specs=pl.BlockSpec(memory_space=pl.ANY),
        out_shape=jax.ShapeDtypeStruct((1, n_dp * 2 * n_z, slots, hid), jnp.bfloat16),
        scratch_shapes=[
            pltpu.VMEM((hid // step, count, slots, step), jnp.bfloat16),
            pltpu.SemaphoreType.DMA((hid // step, count)),
        ],
        input_output_aliases={3 + len(extra): 0} if held else {},
        compiler_params=pltpu.CompilerParams(vmem_limit_bytes=vmem_limit),
        cost_estimate=small_cost,
        name="expert_rows",
    )(place, rows, w_down, *extra, *held, *after)


def per_device(queries, keys, values, out_grad, mixed_grad, expert_ids, combine, w_down):
    rows_dev = queries.shape[1]
    kv_local = keys.shape[2] // HEAD_DIM
    n_ctx, n_dp = lax.axis_size("ctx"), lax.axis_size("dp")
    n_z = n_ctx // 2
    position = lax.axis_index("ctx")
    place = jnp.stack([position >> 1, position & 1]).astype(jnp.int32)
    token_rows = expert_ids.shape[0]
    experts_all = n_dp * n_ctx
    slots = min(
        token_rows,
        max(
            2,
            token_rows * TOPK * 5 // (4 * experts_all),
            (token_rows * TOPK + experts_all - 1) // experts_all,
        ),
    )
    capacity = -(-slots // 8) * 8
    full_rows = mixed_grad
    if lax.axis_size("tp") > 1:
        full_rows = lax.all_gather(mixed_grad, "tp", axis=1, tiled=True)
    own = join(keys, values)
    own_halves = list(halves(full_rows, expert_ids, combine, n_z, n_dp, own))

    def along_z(array, targets):
        pairs = [(2 * i + x, 2 * j + x) for i, j in targets for x in range(2)]
        return lax.ppermute(array, "ctx", pairs)

    def pick(table, array, ks, after):
        block = token_rows if array.shape[0] % own_halves[0].shape[0] else own_halves[0].shape[0]
        sizes = (ks, token_rows, n_dp, capacity)
        return pick_rows(place, table, own_halves[0].shape[0], array, block, *sizes, after)

    def across_x(k):
        pairs = [(i, i ^ 1) for i in range(2 * k, n_ctx) if k > 0 or i % 2 == 0]
        return lax.ppermute(columns[k], "ctx", pairs)

    columns, others = [own], []
    for k in range(1, n_z):
        others.append(across_x(k - 1))
        if k == 2:
            columns[-1], own_halves[0] = lax.optimization_barrier((columns[-1], own_halves[0]))
            own_picked = pick(own_halves[0], full_rows, (0,), (columns[1],))
        if k > 2:
            held = lax.optimization_barrier((columns[-1], *others[k - 3 : k - 1]))
            columns[-1], *others[k - 3 : k - 1] = held
        if k == n_z - 1:
            columns[-1], own_picked = lax.optimization_barrier((columns[-1], own_picked))
        columns.append(along_z(columns[-1], [(i, i + 1) for i in range(k - 1, n_z - 1)]))
    columns[-1], others[-1] = lax.optimization_barrier((columns[-1], others[-1]))
    others.append(across_x(n_z - 1))
    blocks = [block for pair in zip(columns, others) for block in pair]

    plane_groups = [
        [d * n_ctx + 2 * i + j for d in range(n_dp) for j in range(2)] for i in range(n_z)
    ]
    line_groups = [[2 * i + x for i in range(n_z)] for x in range(2)]
    first_half, columns[n_z - 1] = lax.optimization_barrier((own_halves[0], columns[n_z - 1]))
    last_half, columns[n_z - 1] = lax.optimization_barrier((own_halves[1], columns[n_z - 1]))
    all_halves = [
        lax.all_gather(half, "ctx", axis=0, tiled=True, axis_index_groups=line_groups)
        for half in (first_half, last_half)
    ]

    def exchange(picked):
        return lax.all_to_all(
            picked,
            ("dp", "ctx"),
            split_axis=0,
            concat_axis=0,
            tiled=True,
            axis_index_groups=plane_groups,
        )

    def cross(array):
        return lax.ppermute(array, "ctx", [(i, i ^ 1) for i in range(n_ctx)])

    counts = [1] if kv_local == 1 else [kv_local // 2, kv_local - kv_local // 2]
    rest = tuple(range(1, n_z))
    own_picked, columns[n_z - 1] = lax.optimization_barrier((own_picked, columns[n_z - 1]))
    got_own = exchange(own_picked)
    query_grad, mine, other = attention(
        place, queries[0], out_grad[0], blocks, 0, counts[0], None, (own_picked,)
    )
    crossed = cross(other)
    others = []
    if len(counts) > 1:
        query_grad, *others = attention(
            place, queries[0], out_grad[0], blocks, counts[0], counts[1], query_grad
        )
    picked = pick(all_halves[0], all_halves[0], rest, (query_grad,))
    picked, crossed = lax.optimization_barrier((picked, crossed))
    got_first = exchange(picked)
    picked = pick(all_halves[0], all_halves[1], rest, (picked,))
    got_last = exchange(picked)
    total = lax.psum_scatter(
        fold(mine, crossed, others),
        "ctx",
        scatter_dimension=0,
        tiled=True,
        axis_index_groups=line_groups,
    )
    sizes = (n_z, n_dp, capacity, slots)
    hidden_grad = expert_rows(place, got_own, (0,), w_down, *sizes, None, None, (picked,))
    base = partial_rows(got_first, w_down)
    total, base, hidden_grad = lax.optimization_barrier((total, base, hidden_grad))
    last = [cross(total[:, -others[1].shape[1] :])] if others else []
    key_grad, value_grad = finish(counts, total, last, base)
    hidden_grad = expert_rows(place, got_last, rest, w_down, *sizes, base, hidden_grad)
    return (query_grad[None], key_grad, value_grad, hidden_grad)


def solution(mesh):
    placed = (
        P("dp", "ctx", "tp"),
        P("dp", "ctx", "tp"),
        P("dp", "ctx", "tp"),
        P("dp", "ctx", "tp"),
        P(("dp", "ctx"), "tp"),
        P(("dp", "ctx"), None),
        P(("dp", "ctx"), None),
        P(("dp", "ctx"), "tp", None),
    )
    return jax.shard_map(
        per_device,
        mesh=mesh,
        in_specs=placed,
        out_specs=(
            P("dp", "ctx", "tp"),
            P("dp", "ctx", "tp"),
            P("dp", "ctx", "tp"),
            P(("dp", "ctx"), None, None, "tp"),
        ),
        check_vma=False,
    )
```

```python
import functools
import math

import jax
import jax.numpy as jnp
from jax import lax
from jax.experimental import pallas as pl
from jax.experimental.pallas import tpu as pltpu
from jax.sharding import PartitionSpec as P

HEADS = 32
KV_HEADS = 4
HEAD_DIM = 128
TOPK = 8

masked_score = -1e30
vmem_limit = 56 * 1024 * 1024
small_cost = pl.CostEstimate(flops=1, bytes_accessed=1, transcendentals=0)


def mul(a, b):
    return jnp.dot(a, b, preferred_element_type=jnp.float32)


def attention_kernel(n_blocks, heads_step, rows, n_parts, place, q_ref, do_ref, *refs):
    kv_refs = refs[:n_blocks]
    dq_ref, mine_ref, other_ref = refs[-13:-10]
    kv_s, kt_s, q_s, do_s, qt_s, dot_s, s_s, dp_s, dkv_s, dqt_s = refs[-10:]
    part = pl.program_id(1)
    pair = 2 * rows
    width = heads_step * rows
    z, x = place[0], place[1]
    scale = HEAD_DIM ** (-0.5)
    to_exp2 = scale * math.log2(math.e)
    for i, ref in enumerate(kv_refs):
        kv_s[i * rows : (i + 1) * rows, :] = ref[...]
        kt_s[i // 4, :, (i % 4) * rows : (i % 4 + 1) * rows] = ref[:, :HEAD_DIM].T
    for h in range(heads_step):
        lanes = slice(h * HEAD_DIM, (h + 1) * HEAD_DIM)
        here = slice(h * rows, (h + 1) * rows)
        q_s[here, :] = q_ref[:, lanes]
        do_s[here, :] = do_ref[:, lanes]
        qt_s[:, here] = q_ref[:, lanes].T
        dot_s[:, here] = do_ref[:, lanes].T

    def part_of(k):
        return pl.ds(pl.multiple_of(k * 2 * pair, 2 * pair), 2 * pair)

    cut = math.gcd(width, 256)
    slices = [slice(i, i + cut) for i in range(0, width, cut)]

    def scores(k, tops, first):
        results = []
        for here, top in zip(slices, tops):
            s = mul(kv_s[part_of(k), :HEAD_DIM], qt_s[:, here])
            if first:
                key = lax.broadcasted_iota(jnp.int32, (pair, cut), 0)
                query = lax.broadcasted_iota(jnp.int32, (pair, cut), 1) & (rows - 1)
                bound = jnp.where(key < rows, query, jnp.where(x == 1, pair, -1))
                head = jnp.where(key <= bound, s[:pair], masked_score)
            else:
                head = s[:pair]
            tail = jnp.where(2 * k + 1 <= z, s[pair:], masked_score)
            s = jnp.concatenate([head, tail], axis=0)
            s_s[part_of(k), here] = s
            results.append(jnp.maximum(top, jnp.max(s, axis=0, keepdims=True)))
        return tuple(results)

    tops = scores(0, tuple(jnp.full((1, cut), masked_score, jnp.float32) for _ in slices), True)
    chunks = lax.div(z, 2) + 1
    tops = lax.fori_loop(1, chunks, functools.partial(scores, first=False), tops)

    def sums(k, carry):
        results = []
        for here, top, (total, accum) in zip(slices, tops, carry):
            dp = mul(kv_s[part_of(k), HEAD_DIM:], dot_s[:, here])
            e = jnp.exp2((s_s[part_of(k), here] - top) * to_exp2)
            s_s[part_of(k), here] = e
            dp_s[part_of(k), here] = dp
            results.append(
                (
                    total + jnp.sum(e, axis=0, keepdims=True),
                    accum + jnp.sum(e * dp, axis=0, keepdims=True),
                )
            )
        return tuple(results)

    zero = jnp.zeros((1, cut), jnp.float32)
    stats = lax.fori_loop(0, chunks, sums, tuple((zero, zero) for _ in slices))
    shares = [1.0 / total for total, _ in stats]
    deltas = [accum * share for (_, accum), share in zip(stats, shares)]
    dqt_s[...] = jnp.zeros_like(dqt_s)

    def grads(k, carry):
        dk = jnp.zeros((2 * pair, HEAD_DIM), jnp.float32)
        dv = jnp.zeros((2 * pair, HEAD_DIM), jnp.float32)
        for here, share, delta in zip(slices, shares, deltas):
            p = s_s[part_of(k), here] * share
            ds = (p * (dp_s[part_of(k), here] - delta)).astype(jnp.bfloat16)
            dv = dv + mul(p.astype(jnp.bfloat16), do_s[here, :])
            dk = dk + mul(ds, q_s[here, :])
            dqt_s[:, here] += mul(kt_s[k], ds)
        dk = dk * scale
        if n_parts > 1:
            dk = dk + jnp.where(part == 0, 0.0, dkv_s[part_of(k), :HEAD_DIM])
            dv = dv + jnp.where(part == 0, 0.0, dkv_s[part_of(k), HEAD_DIM:])
        dkv_s[part_of(k), :HEAD_DIM] = dk
        dkv_s[part_of(k), HEAD_DIM:] = dv
        return carry

    lax.fori_loop(0, chunks, grads, 0)
    for h in range(heads_step):
        part_t = dqt_s[:, h * rows : (h + 1) * rows] * scale
        dq_ref[:, h * HEAD_DIM : (h + 1) * HEAD_DIM] = part_t.T.astype(jnp.bfloat16)
    for i in range(n_blocks):
        held = dkv_s[i * rows : (i + 1) * rows, :]
        ref = mine_ref if i % 2 == 0 else other_ref
        at = lax.rem(z - i // 2 + n_blocks // 2, n_blocks // 2) * rows
        held = jnp.where(i // 2 <= z, held, 0.0).astype(jnp.bfloat16)
        ref[pl.ds(pl.multiple_of(at, rows), rows), :] = held


def attention(place, queries, out_grad, kv_blocks, first, count, query_grad, after=()):
    rows, q_width = queries.shape
    n_blocks = len(kv_blocks)
    group = HEADS // KV_HEADS
    keys = n_blocks * rows
    heads_step = max(1, min(group, 2**20 // (keys * rows)))
    n_parts = group // heads_step
    width = heads_step * rows
    q_spec = pl.BlockSpec(
        (rows, heads_step * HEAD_DIM), lambda g, u: (0, (g + first) * n_parts + u)
    )
    kv_spec = pl.BlockSpec((rows, 2 * HEAD_DIM), lambda g, u: (0, g + first))
    part_spec = pl.BlockSpec((keys // 2, 2 * HEAD_DIM), lambda g, u: (0, g))
    part_shape = jax.ShapeDtypeStruct((keys // 2, count * 2 * HEAD_DIM), jnp.bfloat16)
    held = [] if query_grad is None else [query_grad]
    return pl.pallas_call(
        functools.partial(attention_kernel, n_blocks, heads_step, rows, n_parts),
        grid=(count, n_parts),
        in_specs=[pl.BlockSpec(memory_space=pltpu.SMEM), q_spec, q_spec]
        + [kv_spec] * n_blocks
        + [pl.BlockSpec(memory_space=pl.ANY)] * (len(held) + len(after)),
        out_specs=[q_spec, part_spec, part_spec],
        out_shape=[jax.ShapeDtypeStruct((rows, q_width), jnp.bfloat16), part_shape, part_shape],
        scratch_shapes=[
            pltpu.VMEM((keys, 2 * HEAD_DIM), jnp.bfloat16),
            pltpu.VMEM((n_blocks // 4, HEAD_DIM, 4 * rows), jnp.bfloat16),
            pltpu.VMEM((width, HEAD_DIM), jnp.bfloat16),
            pltpu.VMEM((width, HEAD_DIM), jnp.bfloat16),
            pltpu.VMEM((HEAD_DIM, width), jnp.bfloat16),
            pltpu.VMEM((HEAD_DIM, width), jnp.bfloat16),
            pltpu.VMEM((keys, width), jnp.float32),
            pltpu.VMEM((keys, width), jnp.float32),
            pltpu.VMEM((keys, 2 * HEAD_DIM), jnp.float32),
            pltpu.VMEM((HEAD_DIM, width), jnp.float32),
        ],
        input_output_aliases={3 + n_blocks: 0} if held else {},
        compiler_params=pltpu.CompilerParams(
            vmem_limit_bytes=vmem_limit, dimension_semantics=("arbitrary", "arbitrary")
        ),
        cost_estimate=small_cost
        if held
        else pl.CostEstimate(
            flops=100 * rows * keys * group * count * HEAD_DIM,
            bytes_accessed=8 * (rows * group + keys) * count * HEAD_DIM,
            transcendentals=rows * keys * group * count,
        ),
        name="attention_backward",
    )(place, queries, out_grad, *kv_blocks, *held, *after)


def fold_kernel(mine_ref, *refs):
    out_ref, width = refs[-1], mine_ref.shape[1]
    total = mine_ref[...].astype(jnp.float32) + refs[0][...].astype(jnp.float32)
    out_ref[:, :width] = total.astype(out_ref.dtype)
    first = width
    for ref in refs[1:-1]:
        out_ref[:, first : first + ref.shape[1]] = ref[...]
        first += ref.shape[1]


def fold(mine, got, others):
    arrays = (mine, got, *others)
    rows, width = mine.shape[0], sum(part.shape[1] for part in arrays[1:])
    return pl.pallas_call(
        fold_kernel,
        grid=(4,),
        in_specs=[pl.BlockSpec((rows // 4, part.shape[1]), lambda i: (i, 0)) for part in arrays],
        out_specs=pl.BlockSpec((rows // 4, width), lambda i: (i, 0)),
        out_shape=jax.ShapeDtypeStruct((rows, width), jnp.bfloat16),
        compiler_params=pltpu.CompilerParams(vmem_limit_bytes=vmem_limit),
        cost_estimate=small_cost,
        name="fold",
    )(*arrays)


def finish_kernel(counts, total_ref, *refs):
    key_ref, value_ref = refs[-2:]
    size = 2 * HEAD_DIM
    for g in range(sum(counts)):
        lanes = slice(g * HEAD_DIM, (g + 1) * HEAD_DIM)
        held = total_ref[:, g * size : (g + 1) * size]
        if g >= counts[0]:
            at = (g - counts[0]) * size
            held = held.astype(jnp.float32) + refs[0][:, at : at + size].astype(jnp.float32)
            held = held.astype(jnp.bfloat16)
        key_ref[0, :, lanes] = held[:, :HEAD_DIM]
        value_ref[0, :, lanes] = held[:, HEAD_DIM:]


def finish(counts, total, crossed, after):
    shape = jax.ShapeDtypeStruct((1, total.shape[0], sum(counts) * HEAD_DIM), jnp.bfloat16)
    return pl.pallas_call(
        functools.partial(finish_kernel, counts),
        in_specs=[pl.BlockSpec(memory_space=pltpu.VMEM)] * (1 + len(crossed))
        + [pl.BlockSpec(memory_space=pl.ANY)],
        out_shape=[shape, shape],
        compiler_params=pltpu.CompilerParams(vmem_limit_bytes=vmem_limit),
        cost_estimate=small_cost,
        name="finish",
    )(total, *crossed, after)


def join_kernel(key_ref, value_ref, kv_ref):
    for g in range(kv_ref.shape[1] // (2 * HEAD_DIM)):
        lanes = slice(g * HEAD_DIM, (g + 1) * HEAD_DIM)
        kv_ref[:, 2 * g * HEAD_DIM : (2 * g + 1) * HEAD_DIM] = key_ref[0, :, lanes]
        kv_ref[:, (2 * g + 1) * HEAD_DIM : (2 * g + 2) * HEAD_DIM] = value_ref[0, :, lanes]


def join(keys, values):
    rows, width = keys.shape[1:]
    return pl.pallas_call(
        join_kernel,
        out_shape=jax.ShapeDtypeStruct((rows, 2 * width), jnp.bfloat16),
        compiler_params=pltpu.CompilerParams(vmem_limit_bytes=vmem_limit),
        cost_estimate=small_cost,
        name="join",
    )(keys, values)


def table_kernel(n_z, n_dp, rows_ref, ids_ref, combine_ref, *refs):
    ext_ref, rest_ref = refs[-2:]
    tokens, feat = rows_ref.shape
    lines = 4 * n_dp
    line = lax.broadcasted_iota(jnp.int32, (n_z * lines, tokens), 0)
    kind = line % lines
    member = kind % (2 * n_dp)
    expert = (member // 2) * (2 * n_z) + line // lines * 2 + member % 2
    hits = jnp.zeros((n_z * lines, tokens), jnp.float32)
    weights = jnp.zeros((n_z * lines, tokens), jnp.float32)
    combine = combine_ref[...].astype(jnp.float32)
    for k in range(TOPK):
        hit = ids_ref[k : k + 1, :] == expert
        hits = hits + jnp.where(hit, 1.0, 0.0)
        weights = weights + jnp.where(hit, combine[k : k + 1, :], 0.0)
    before = lax.broadcasted_iota(jnp.int32, (tokens, tokens), 0) < lax.broadcasted_iota(
        jnp.int32, (tokens, tokens), 1
    )
    ranks = mul(hits.astype(jnp.bfloat16), jnp.where(before, 1.0, 0.0).astype(jnp.bfloat16))
    table = jnp.where(kind < 2 * n_dp, jnp.where(hits > 0.0, ranks, -1.0), weights)
    half = feat // 2
    ext_ref[:tokens, :] = rows_ref[:, :half]
    rest_ref[...] = rows_ref[:, half:]
    squares = [table[i * lines : (i + 1) * lines] for i in range(n_z)]
    per_row = half // tokens
    squares += [jnp.zeros((lines, tokens), jnp.float32)] * (-n_z % per_row)
    for i in range(len(squares) // per_row):
        line_of = jnp.concatenate(squares[i * per_row : (i + 1) * per_row], axis=1)
        here = slice(tokens + i * lines, tokens + (i + 1) * lines)
        ext_ref[here, :] = line_of.astype(jnp.bfloat16)


def halves(full_rows, ids, combine, n_z, n_dp, after):
    tokens, feat = full_rows.shape
    return pl.pallas_call(
        functools.partial(table_kernel, n_z, n_dp),
        in_specs=[pl.BlockSpec(memory_space=pltpu.VMEM)] * 3 + [pl.BlockSpec(memory_space=pl.ANY)],
        out_shape=[
            jax.ShapeDtypeStruct(
                (tokens + 4 * n_dp * -(-2 * n_z * tokens // feat), feat // 2), jnp.bfloat16
            ),
            jax.ShapeDtypeStruct((tokens, feat // 2), jnp.bfloat16),
        ],
        compiler_params=pltpu.CompilerParams(vmem_limit_bytes=vmem_limit),
        cost_estimate=small_cost,
        name="slot_table",
    )(full_rows, ids.T, combine.T, after)


def pick_kernel(count, n_dp, capacity, place, *refs):
    table_refs, row_refs = refs[:count], refs[count : 2 * count]
    out_ref, pick_s = refs[-2:]
    tokens = pick_s.shape[2]

    @pl.when(pl.program_id(0) == 0)
    def _():
        for i, ref in enumerate(table_refs):
            table = ref[...].astype(jnp.float32)
            slot = lax.broadcasted_iota(jnp.int32, (capacity, tokens), 0).astype(jnp.float32)
            picks = [
                jnp.where(
                    slot == table[q : q + 1, :], table[2 * n_dp + q : 2 * n_dp + q + 1, :], 0.0
                )
                for q in range(2 * n_dp)
            ]
            pick_s[i] = jnp.concatenate(picks, axis=0).astype(jnp.bfloat16)

    results = [mul(pick_s[i], ref[:tokens, :]) for i, ref in enumerate(row_refs)]
    for q in range(2 * n_dp):
        here = slice(q * capacity, (q + 1) * capacity)
        total = jnp.concatenate([part[here] for part in results], axis=0)
        size = count * capacity
        out_ref[q * size : (q + 1) * size, :] = total.astype(jnp.bfloat16)


def pick_rows(place, table, block_table, array, block, ks, tokens, n_dp, capacity, after=()):
    lines, feat = 4 * n_dp, array.shape[1]
    step = math.gcd(feat, 1024 if len(ks) == 1 else 512)
    out_rows = len(ks) * 2 * n_dp * capacity
    per_row = table.shape[1] // tokens

    def at(place, k, whole, part):
        return (place[0] & (whole.shape[0] // part - 1)) ^ k

    def table_spec(k):
        def index(f, place):
            first = (at(place, k, table, block_table) * block_table + tokens) // lines
            return first + place[0] // per_row, place[0] % per_row

        return pl.BlockSpec((lines, tokens), index)

    def rows_spec(k):
        return pl.BlockSpec((block, step), lambda f, place: (at(place, k, array, block), f))

    return pl.pallas_call(
        functools.partial(pick_kernel, len(ks), n_dp, capacity),
        grid_spec=pltpu.PrefetchScalarGridSpec(
            num_scalar_prefetch=1,
            grid=(feat // step,),
            in_specs=[table_spec(k) for k in ks]
            + [rows_spec(k) for k in ks]
            + [pl.BlockSpec(memory_space=pl.ANY)] * len(after),
            out_specs=pl.BlockSpec((out_rows, step), lambda f, place: (0, f)),
            scratch_shapes=[pltpu.VMEM((len(ks), 2 * n_dp * capacity, tokens), jnp.bfloat16)],
        ),
        out_shape=jax.ShapeDtypeStruct((out_rows, feat), jnp.bfloat16),
        compiler_params=pltpu.CompilerParams(vmem_limit_bytes=vmem_limit),
        cost_estimate=small_cost,
        name="pick_rows",
    )(place, *[table] * len(ks), *[array] * len(ks), *after)


def partial_kernel(rows_ref, w_ref, out_ref):
    out_ref[...] = lax.dot_general(
        rows_ref[...], w_ref[0], (((1,), (1,)), ((), ())), preferred_element_type=jnp.float32
    ).astype(jnp.bfloat16)


def partial_rows(rows, w_down):
    count, half = rows.shape
    hid = w_down.shape[1]
    step = math.gcd(hid, 512)
    return pl.pallas_call(
        partial_kernel,
        grid=(hid // step,),
        in_specs=[
            pl.BlockSpec((count, half), lambda n: (0, 0)),
            pl.BlockSpec((1, step, half), lambda n: (0, n, 0)),
        ],
        out_specs=pl.BlockSpec((count, step), lambda n: (0, n)),
        out_shape=jax.ShapeDtypeStruct((count, hid), jnp.bfloat16),
        compiler_params=pltpu.CompilerParams(vmem_limit_bytes=vmem_limit),
        cost_estimate=small_cost,
        name="partial_rows",
    )(rows, w_down)


def expert_kernel(ks, with_base, n_z, n_dp, capacity, slots, place, rows_ref, w_ref, *refs):
    out_ref, out_s, sem = refs[-3:]
    step, steps = pl.program_id(0), out_s.shape[0]
    width = out_s.shape[-1]
    blocks = [(q, k) for q in range(2 * n_dp) for k in ks]
    result = lax.dot_general(
        rows_ref[...], w_ref[0], (((1,), (1,)), ((), ())), preferred_element_type=jnp.float32
    )
    if with_base:
        result = result + refs[0][...].astype(jnp.float32)
    for i in range(len(blocks)):
        out_s[step, i] = result[i * capacity : i * capacity + slots].astype(jnp.bfloat16)

    def copies(at):
        z = place[0]
        for i, (q, k) in enumerate(blocks):
            source = (q // 2) * (2 * n_z) + (z ^ k) * 2 + q % 2
            lanes = pl.ds(pl.multiple_of(at * width, width), width)
            yield pltpu.make_async_copy(
                out_s.at[at, i], out_ref.at[0, source, :, lanes], sem.at[at, i]
            )

    for copy in copies(step):
        copy.start()

    @pl.when(step == steps - 1)
    def _():
        for at in range(steps):
            for copy in copies(at):
                copy.wait()


def expert_rows(place, rows, ks, w_down, n_z, n_dp, capacity, slots, base, hidden_grad, after=()):
    hid = w_down.shape[1]
    step = math.gcd(hid, 512)
    count = rows.shape[0] // capacity
    part = w_down.shape[2] // rows.shape[1] - 1
    extra = [] if base is None else [base]
    held = [] if hidden_grad is None else [hidden_grad]
    return pl.pallas_call(
        functools.partial(expert_kernel, ks, bool(extra), n_z, n_dp, capacity, slots),
        grid=(hid // step,),
        in_specs=[
            pl.BlockSpec(memory_space=pltpu.SMEM),
            pl.BlockSpec(rows.shape, lambda n: (0, 0)),
            pl.BlockSpec((1, step, rows.shape[1]), lambda n: (0, n, part)),
        ]
        + [pl.BlockSpec((rows.shape[0], step), lambda n: (0, n))] * len(extra)
        + [pl.BlockSpec(memory_space=pl.ANY)] * (len(held) + len(after)),
        out_specs=pl.BlockSpec(memory_space=pl.ANY),
        out_shape=jax.ShapeDtypeStruct((1, n_dp * 2 * n_z, slots, hid), jnp.bfloat16),
        scratch_shapes=[
            pltpu.VMEM((hid // step, count, slots, step), jnp.bfloat16),
            pltpu.SemaphoreType.DMA((hid // step, count)),
        ],
        input_output_aliases={3 + len(extra): 0} if held else {},
        compiler_params=pltpu.CompilerParams(vmem_limit_bytes=vmem_limit),
        cost_estimate=small_cost,
        name="expert_rows",
    )(place, rows, w_down, *extra, *held, *after)


def per_device(queries, keys, values, out_grad, mixed_grad, expert_ids, combine, w_down):
    rows_dev = queries.shape[1]
    kv_local = keys.shape[2] // HEAD_DIM
    n_ctx, n_dp = lax.axis_size("ctx"), lax.axis_size("dp")
    n_z = n_ctx // 2
    position = lax.axis_index("ctx")
    place = jnp.stack([position >> 1, position & 1]).astype(jnp.int32)
    token_rows = expert_ids.shape[0]
    experts_all = n_dp * n_ctx
    slots = min(
        token_rows,
        max(
            2,
            token_rows * TOPK * 5 // (4 * experts_all),
            (token_rows * TOPK + experts_all - 1) // experts_all,
        ),
    )
    capacity = -(-slots // 8) * 8
    full_rows = mixed_grad
    if lax.axis_size("tp") > 1:
        full_rows = lax.all_gather(mixed_grad, "tp", axis=1, tiled=True)
    own = join(keys, values)
    own_halves = list(halves(full_rows, expert_ids, combine, n_z, n_dp, own))

    def along_z(array, targets):
        pairs = [(2 * i + x, 2 * j + x) for i, j in targets for x in range(2)]
        return lax.ppermute(array, "ctx", pairs)

    def pick(table, array, ks, after):
        block = token_rows if array.shape[0] % own_halves[0].shape[0] else own_halves[0].shape[0]
        sizes = (ks, token_rows, n_dp, capacity)
        return pick_rows(place, table, own_halves[0].shape[0], array, block, *sizes, after)

    def across_x(k):
        pairs = [(i, i ^ 1) for i in range(2 * k, n_ctx) if k > 0 or i % 2 == 0]
        return lax.ppermute(columns[k], "ctx", pairs)

    columns, others = [own], []
    for k in range(1, n_z):
        others.append(across_x(k - 1))
        if k == 2:
            columns[-1], own_halves[0] = lax.optimization_barrier((columns[-1], own_halves[0]))
            own_picked = pick(own_halves[0], full_rows, (0,), (columns[1],))
        if k > 2:
            held = lax.optimization_barrier((columns[-1], *others[k - 3 : k - 1]))
            columns[-1], *others[k - 3 : k - 1] = held
        if k == n_z - 1:
            columns[-1], own_picked = lax.optimization_barrier((columns[-1], own_picked))
        columns.append(along_z(columns[-1], [(i, i + 1) for i in range(k - 1, n_z - 1)]))
    columns[-1], others[-1] = lax.optimization_barrier((columns[-1], others[-1]))
    first_half, columns[-1] = lax.optimization_barrier((own_halves[0], columns[-1]))
    others.append(across_x(n_z - 1))
    blocks = [block for pair in zip(columns, others) for block in pair]

    plane_groups = [
        [d * n_ctx + 2 * i + j for d in range(n_dp) for j in range(2)] for i in range(n_z)
    ]
    line_groups = [[2 * i + x for i in range(n_z)] for x in range(2)]
    last_half, columns[n_z - 1] = lax.optimization_barrier((own_halves[1], columns[n_z - 1]))
    all_halves = [
        lax.all_gather(half, "ctx", axis=0, tiled=True, axis_index_groups=line_groups)
        for half in (first_half, last_half)
    ]

    def exchange(picked):
        return lax.all_to_all(
            picked,
            ("dp", "ctx"),
            split_axis=0,
            concat_axis=0,
            tiled=True,
            axis_index_groups=plane_groups,
        )

    def cross(array):
        return lax.ppermute(array, "ctx", [(i, i ^ 1) for i in range(n_ctx)])

    counts = [1] if kv_local == 1 else [kv_local // 2, kv_local - kv_local // 2]
    rest = tuple(range(1, n_z))
    own_picked, columns[n_z - 1] = lax.optimization_barrier((own_picked, columns[n_z - 1]))
    got_own = exchange(own_picked)
    query_grad, mine, other = attention(
        place, queries[0], out_grad[0], blocks, 0, counts[0], None, (own_picked,)
    )
    crossed = cross(other)
    others = []
    if len(counts) > 1:
        query_grad, *others = attention(
            place, queries[0], out_grad[0], blocks, counts[0], counts[1], query_grad
        )
    picked = pick(all_halves[0], all_halves[0], rest, (query_grad,))
    picked, crossed = lax.optimization_barrier((picked, crossed))
    got_first = exchange(picked)
    picked = pick(all_halves[0], all_halves[1], rest, (picked,))
    got_last = exchange(picked)
    total = lax.psum_scatter(
        fold(mine, crossed, others),
        "ctx",
        scatter_dimension=0,
        tiled=True,
        axis_index_groups=line_groups,
    )
    sizes = (n_z, n_dp, capacity, slots)
    hidden_grad = expert_rows(place, got_own, (0,), w_down, *sizes, None, None, (picked,))
    base = partial_rows(got_first, w_down)
    total, base, hidden_grad = lax.optimization_barrier((total, base, hidden_grad))
    last = [cross(total[:, -others[1].shape[1] :])] if others else []
    key_grad, value_grad = finish(counts, total, last, base)
    hidden_grad = expert_rows(place, got_last, rest, w_down, *sizes, base, hidden_grad)
    return (query_grad[None], key_grad, value_grad, hidden_grad)


def solution(mesh):
    placed = (
        P("dp", "ctx", "tp"),
        P("dp", "ctx", "tp"),
        P("dp", "ctx", "tp"),
        P("dp", "ctx", "tp"),
        P(("dp", "ctx"), "tp"),
        P(("dp", "ctx"), None),
        P(("dp", "ctx"), None),
        P(("dp", "ctx"), "tp", None),
    )
    return jax.shard_map(
        per_device,
        mesh=mesh,
        in_specs=placed,
        out_specs=(
            P("dp", "ctx", "tp"),
            P("dp", "ctx", "tp"),
            P("dp", "ctx", "tp"),
            P(("dp", "ctx"), None, None, "tp"),
        ),
        check_vma=False,
    )
```

```python
import functools
import math

import jax
import jax.numpy as jnp
from jax import lax
from jax.experimental import pallas as pl
from jax.experimental.pallas import tpu as pltpu
from jax.sharding import PartitionSpec as P

HEADS = 32
KV_HEADS = 4
HEAD_DIM = 128
TOPK = 8

masked_score = -1e30
vmem_limit = 56 * 1024 * 1024
small_cost = pl.CostEstimate(flops=1, bytes_accessed=1, transcendentals=0)


def mul(a, b):
    return jnp.dot(a, b, preferred_element_type=jnp.float32)


def attention_kernel(n_blocks, heads_step, rows, n_parts, place, q_ref, do_ref, *refs):
    kv_refs = refs[:n_blocks]
    dq_ref, mine_ref, other_ref = refs[-13:-10]
    kv_s, kt_s, q_s, do_s, qt_s, dot_s, s_s, dp_s, dkv_s, dqt_s = refs[-10:]
    part = pl.program_id(1)
    pair = 2 * rows
    width = heads_step * rows
    z, x = place[0], place[1]
    scale = HEAD_DIM ** (-0.5)
    to_exp2 = scale * math.log2(math.e)
    for i, ref in enumerate(kv_refs):
        kv_s[i * rows : (i + 1) * rows, :] = ref[...]
        kt_s[i // 4, :, (i % 4) * rows : (i % 4 + 1) * rows] = ref[:, :HEAD_DIM].T
    for h in range(heads_step):
        lanes = slice(h * HEAD_DIM, (h + 1) * HEAD_DIM)
        here = slice(h * rows, (h + 1) * rows)
        q_s[here, :] = q_ref[:, lanes]
        do_s[here, :] = do_ref[:, lanes]
        qt_s[:, here] = q_ref[:, lanes].T
        dot_s[:, here] = do_ref[:, lanes].T

    def part_of(k):
        return pl.ds(pl.multiple_of(k * 2 * pair, 2 * pair), 2 * pair)

    cut = math.gcd(width, 256)
    slices = [slice(i, i + cut) for i in range(0, width, cut)]

    def scores(k, tops, first):
        results = []
        for here, top in zip(slices, tops):
            s = mul(kv_s[part_of(k), :HEAD_DIM], qt_s[:, here])
            if first:
                key = lax.broadcasted_iota(jnp.int32, (pair, cut), 0)
                query = lax.broadcasted_iota(jnp.int32, (pair, cut), 1) & (rows - 1)
                bound = jnp.where(key < rows, query, jnp.where(x == 1, pair, -1))
                head = jnp.where(key <= bound, s[:pair], masked_score)
            else:
                head = s[:pair]
            tail = jnp.where(2 * k + 1 <= z, s[pair:], masked_score)
            s = jnp.concatenate([head, tail], axis=0)
            s_s[part_of(k), here] = s
            results.append(jnp.maximum(top, jnp.max(s, axis=0, keepdims=True)))
        return tuple(results)

    tops = scores(0, tuple(jnp.full((1, cut), masked_score, jnp.float32) for _ in slices), True)
    chunks = lax.div(z, 2) + 1
    tops = lax.fori_loop(1, chunks, functools.partial(scores, first=False), tops)

    def sums(k, carry):
        results = []
        for here, top, (total, accum) in zip(slices, tops, carry):
            dp = mul(kv_s[part_of(k), HEAD_DIM:], dot_s[:, here])
            e = jnp.exp2((s_s[part_of(k), here] - top) * to_exp2)
            s_s[part_of(k), here] = e
            dp_s[part_of(k), here] = dp
            results.append(
                (
                    total + jnp.sum(e, axis=0, keepdims=True),
                    accum + jnp.sum(e * dp, axis=0, keepdims=True),
                )
            )
        return tuple(results)

    zero = jnp.zeros((1, cut), jnp.float32)
    stats = lax.fori_loop(0, chunks, sums, tuple((zero, zero) for _ in slices))
    shares = [1.0 / total for total, _ in stats]
    deltas = [accum * share for (_, accum), share in zip(stats, shares)]
    dqt_s[...] = jnp.zeros_like(dqt_s)

    def grads(k, carry):
        dk = jnp.zeros((2 * pair, HEAD_DIM), jnp.float32)
        dv = jnp.zeros((2 * pair, HEAD_DIM), jnp.float32)
        for here, share, delta in zip(slices, shares, deltas):
            p = s_s[part_of(k), here] * share
            ds = (p * (dp_s[part_of(k), here] - delta)).astype(jnp.bfloat16)
            dv = dv + mul(p.astype(jnp.bfloat16), do_s[here, :])
            dk = dk + mul(ds, q_s[here, :])
            dqt_s[:, here] += mul(kt_s[k], ds)
        dk = dk * scale
        if n_parts > 1:
            dk = dk + jnp.where(part == 0, 0.0, dkv_s[part_of(k), :HEAD_DIM])
            dv = dv + jnp.where(part == 0, 0.0, dkv_s[part_of(k), HEAD_DIM:])
        dkv_s[part_of(k), :HEAD_DIM] = dk
        dkv_s[part_of(k), HEAD_DIM:] = dv
        return carry

    lax.fori_loop(0, chunks, grads, 0)
    for h in range(heads_step):
        part_t = dqt_s[:, h * rows : (h + 1) * rows] * scale
        dq_ref[:, h * HEAD_DIM : (h + 1) * HEAD_DIM] = part_t.T.astype(jnp.bfloat16)
    for i in range(n_blocks):
        held = dkv_s[i * rows : (i + 1) * rows, :]
        ref = mine_ref if i % 2 == 0 else other_ref
        at = lax.rem(z - i // 2 + n_blocks // 2, n_blocks // 2) * rows
        held = jnp.where(i // 2 <= z, held, 0.0).astype(jnp.bfloat16)
        ref[pl.ds(pl.multiple_of(at, rows), rows), :] = held


def attention(place, queries, out_grad, kv_blocks, first, count, query_grad, after=()):
    rows, q_width = queries.shape
    n_blocks = len(kv_blocks)
    group = HEADS // KV_HEADS
    keys = n_blocks * rows
    heads_step = max(1, min(group, 2**20 // (keys * rows)))
    n_parts = group // heads_step
    width = heads_step * rows
    q_spec = pl.BlockSpec(
        (rows, heads_step * HEAD_DIM), lambda g, u: (0, (g + first) * n_parts + u)
    )
    kv_spec = pl.BlockSpec((rows, 2 * HEAD_DIM), lambda g, u: (0, g + first))
    part_spec = pl.BlockSpec((keys // 2, 2 * HEAD_DIM), lambda g, u: (0, g))
    part_shape = jax.ShapeDtypeStruct((keys // 2, count * 2 * HEAD_DIM), jnp.bfloat16)
    held = [] if query_grad is None else [query_grad]
    return pl.pallas_call(
        functools.partial(attention_kernel, n_blocks, heads_step, rows, n_parts),
        grid=(count, n_parts),
        in_specs=[pl.BlockSpec(memory_space=pltpu.SMEM), q_spec, q_spec]
        + [kv_spec] * n_blocks
        + [pl.BlockSpec(memory_space=pl.ANY)] * (len(held) + len(after)),
        out_specs=[q_spec, part_spec, part_spec],
        out_shape=[jax.ShapeDtypeStruct((rows, q_width), jnp.bfloat16), part_shape, part_shape],
        scratch_shapes=[
            pltpu.VMEM((keys, 2 * HEAD_DIM), jnp.bfloat16),
            pltpu.VMEM((n_blocks // 4, HEAD_DIM, 4 * rows), jnp.bfloat16),
            pltpu.VMEM((width, HEAD_DIM), jnp.bfloat16),
            pltpu.VMEM((width, HEAD_DIM), jnp.bfloat16),
            pltpu.VMEM((HEAD_DIM, width), jnp.bfloat16),
            pltpu.VMEM((HEAD_DIM, width), jnp.bfloat16),
            pltpu.VMEM((keys, width), jnp.float32),
            pltpu.VMEM((keys, width), jnp.float32),
            pltpu.VMEM((keys, 2 * HEAD_DIM), jnp.float32),
            pltpu.VMEM((HEAD_DIM, width), jnp.float32),
        ],
        input_output_aliases={3 + n_blocks: 0} if held else {},
        compiler_params=pltpu.CompilerParams(
            vmem_limit_bytes=vmem_limit, dimension_semantics=("arbitrary", "arbitrary")
        ),
        cost_estimate=small_cost
        if held
        else pl.CostEstimate(
            flops=100 * rows * keys * group * count * HEAD_DIM,
            bytes_accessed=8 * (rows * group + keys) * count * HEAD_DIM,
            transcendentals=rows * keys * group * count,
        ),
        name="attention_backward",
    )(place, queries, out_grad, *kv_blocks, *held, *after)


def fold_kernel(groups, *refs):
    out_ref = refs[-1]
    first = 0
    for i in range(groups):
        total = refs[2 * i][...].astype(jnp.float32) + refs[2 * i + 1][...].astype(jnp.float32)
        out_ref[:, first : first + total.shape[1]] = total.astype(out_ref.dtype)
        first += total.shape[1]


def fold(parts):
    arrays = [part for pair in parts for part in pair]
    rows, width = arrays[0].shape[0], sum(pair[0].shape[1] for pair in parts)
    return pl.pallas_call(
        functools.partial(fold_kernel, len(parts)),
        grid=(2,),
        in_specs=[pl.BlockSpec((rows // 2, part.shape[1]), lambda i: (i, 0)) for part in arrays],
        out_specs=pl.BlockSpec((rows // 2, width), lambda i: (i, 0)),
        out_shape=jax.ShapeDtypeStruct((rows, width), jnp.bfloat16),
        compiler_params=pltpu.CompilerParams(vmem_limit_bytes=vmem_limit),
        cost_estimate=small_cost,
        name="fold",
    )(*arrays)


def finish_kernel(total_ref, *refs):
    key_ref, value_ref = refs[-2:]
    size = 2 * HEAD_DIM
    for g in range(total_ref.shape[1] // size):
        lanes = slice(g * HEAD_DIM, (g + 1) * HEAD_DIM)
        key_ref[0, :, lanes] = total_ref[:, g * size : g * size + HEAD_DIM]
        value_ref[0, :, lanes] = total_ref[:, g * size + HEAD_DIM : (g + 1) * size]


def finish(total, after):
    shape = jax.ShapeDtypeStruct((1, total.shape[0], total.shape[1] // 2), jnp.bfloat16)
    return pl.pallas_call(
        finish_kernel,
        in_specs=[pl.BlockSpec(memory_space=pltpu.VMEM), pl.BlockSpec(memory_space=pl.ANY)],
        out_shape=[shape, shape],
        compiler_params=pltpu.CompilerParams(vmem_limit_bytes=vmem_limit),
        cost_estimate=small_cost,
        name="finish",
    )(total, after)


def join_kernel(key_ref, value_ref, kv_ref):
    for g in range(kv_ref.shape[1] // (2 * HEAD_DIM)):
        lanes = slice(g * HEAD_DIM, (g + 1) * HEAD_DIM)
        kv_ref[:, 2 * g * HEAD_DIM : (2 * g + 1) * HEAD_DIM] = key_ref[0, :, lanes]
        kv_ref[:, (2 * g + 1) * HEAD_DIM : (2 * g + 2) * HEAD_DIM] = value_ref[0, :, lanes]


def join(keys, values):
    rows, width = keys.shape[1:]
    return pl.pallas_call(
        join_kernel,
        out_shape=jax.ShapeDtypeStruct((rows, 2 * width), jnp.bfloat16),
        compiler_params=pltpu.CompilerParams(vmem_limit_bytes=vmem_limit),
        cost_estimate=small_cost,
        name="join",
    )(keys, values)


def table_kernel(n_z, n_dp, rows_ref, ids_ref, combine_ref, *refs):
    ext_ref, rest_ref = refs[-2:]
    tokens, feat = rows_ref.shape
    lines = 4 * n_dp
    line = lax.broadcasted_iota(jnp.int32, (n_z * lines, tokens), 0)
    kind = line % lines
    member = kind % (2 * n_dp)
    expert = (member // 2) * (2 * n_z) + line // lines * 2 + member % 2
    hits = jnp.zeros((n_z * lines, tokens), jnp.float32)
    weights = jnp.zeros((n_z * lines, tokens), jnp.float32)
    combine = combine_ref[...].astype(jnp.float32)
    for k in range(TOPK):
        hit = ids_ref[k : k + 1, :] == expert
        hits = hits + jnp.where(hit, 1.0, 0.0)
        weights = weights + jnp.where(hit, combine[k : k + 1, :], 0.0)
    before = lax.broadcasted_iota(jnp.int32, (tokens, tokens), 0) < lax.broadcasted_iota(
        jnp.int32, (tokens, tokens), 1
    )
    ranks = mul(hits.astype(jnp.bfloat16), jnp.where(before, 1.0, 0.0).astype(jnp.bfloat16))
    table = jnp.where(kind < 2 * n_dp, jnp.where(hits > 0.0, ranks, -1.0), weights)
    half = feat // 2
    ext_ref[:tokens, :] = rows_ref[:, :half]
    rest_ref[...] = rows_ref[:, half:]
    squares = [table[i * lines : (i + 1) * lines] for i in range(n_z)]
    per_row = half // tokens
    squares += [jnp.zeros((lines, tokens), jnp.float32)] * (-n_z % per_row)
    for i in range(len(squares) // per_row):
        line_of = jnp.concatenate(squares[i * per_row : (i + 1) * per_row], axis=1)
        here = slice(tokens + i * lines, tokens + (i + 1) * lines)
        ext_ref[here, :] = line_of.astype(jnp.bfloat16)


def halves(full_rows, ids, combine, n_z, n_dp, after):
    tokens, feat = full_rows.shape
    return pl.pallas_call(
        functools.partial(table_kernel, n_z, n_dp),
        in_specs=[pl.BlockSpec(memory_space=pltpu.VMEM)] * 3 + [pl.BlockSpec(memory_space=pl.ANY)],
        out_shape=[
            jax.ShapeDtypeStruct(
                (tokens + 4 * n_dp * -(-2 * n_z * tokens // feat), feat // 2), jnp.bfloat16
            ),
            jax.ShapeDtypeStruct((tokens, feat // 2), jnp.bfloat16),
        ],
        compiler_params=pltpu.CompilerParams(vmem_limit_bytes=vmem_limit),
        cost_estimate=small_cost,
        name="slot_table",
    )(full_rows, ids.T, combine.T, after)


def pick_kernel(count, n_dp, capacity, place, *refs):
    table_refs, row_refs = refs[:count], refs[count : 2 * count]
    out_ref, pick_s = refs[-2:]
    tokens = pick_s.shape[2]

    @pl.when(pl.program_id(0) == 0)
    def _():
        for i, ref in enumerate(table_refs):
            table = ref[...].astype(jnp.float32)
            slot = lax.broadcasted_iota(jnp.int32, (capacity, tokens), 0).astype(jnp.float32)
            picks = [
                jnp.where(
                    slot == table[q : q + 1, :], table[2 * n_dp + q : 2 * n_dp + q + 1, :], 0.0
                )
                for q in range(2 * n_dp)
            ]
            pick_s[i] = jnp.concatenate(picks, axis=0).astype(jnp.bfloat16)

    results = [mul(pick_s[i], ref[:tokens, :]) for i, ref in enumerate(row_refs)]
    for q in range(2 * n_dp):
        here = slice(q * capacity, (q + 1) * capacity)
        total = jnp.concatenate([part[here] for part in results], axis=0)
        size = count * capacity
        out_ref[q * size : (q + 1) * size, :] = total.astype(jnp.bfloat16)


def pick_rows(place, table, block_table, array, block, ks, tokens, n_dp, capacity, after=()):
    lines, feat = 4 * n_dp, array.shape[1]
    step = math.gcd(feat, 1024 if len(ks) == 1 else 512)
    out_rows = len(ks) * 2 * n_dp * capacity
    per_row = table.shape[1] // tokens

    def at(place, k, whole, part):
        return (place[0] & (whole.shape[0] // part - 1)) ^ k

    def table_spec(k):
        def index(f, place):
            first = (at(place, k, table, block_table) * block_table + tokens) // lines
            return first + place[0] // per_row, place[0] % per_row

        return pl.BlockSpec((lines, tokens), index)

    def rows_spec(k):
        return pl.BlockSpec((block, step), lambda f, place: (at(place, k, array, block), f))

    return pl.pallas_call(
        functools.partial(pick_kernel, len(ks), n_dp, capacity),
        grid_spec=pltpu.PrefetchScalarGridSpec(
            num_scalar_prefetch=1,
            grid=(feat // step,),
            in_specs=[table_spec(k) for k in ks]
            + [rows_spec(k) for k in ks]
            + [pl.BlockSpec(memory_space=pl.ANY)] * len(after),
            out_specs=pl.BlockSpec((out_rows, step), lambda f, place: (0, f)),
            scratch_shapes=[pltpu.VMEM((len(ks), 2 * n_dp * capacity, tokens), jnp.bfloat16)],
        ),
        out_shape=jax.ShapeDtypeStruct((out_rows, feat), jnp.bfloat16),
        compiler_params=pltpu.CompilerParams(vmem_limit_bytes=vmem_limit),
        cost_estimate=small_cost,
        name="pick_rows",
    )(place, *[table] * len(ks), *[array] * len(ks), *after)


def partial_kernel(rows_ref, w_ref, out_ref):
    out_ref[...] = lax.dot_general(
        rows_ref[...], w_ref[0], (((1,), (1,)), ((), ())), preferred_element_type=jnp.float32
    ).astype(jnp.bfloat16)


def partial_rows(rows, w_down):
    count, half = rows.shape
    hid = w_down.shape[1]
    step = math.gcd(hid, 512)
    return pl.pallas_call(
        partial_kernel,
        grid=(hid // step,),
        in_specs=[
            pl.BlockSpec((count, half), lambda n: (0, 0)),
            pl.BlockSpec((1, step, half), lambda n: (0, n, 0)),
        ],
        out_specs=pl.BlockSpec((count, step), lambda n: (0, n)),
        out_shape=jax.ShapeDtypeStruct((count, hid), jnp.bfloat16),
        compiler_params=pltpu.CompilerParams(vmem_limit_bytes=vmem_limit),
        cost_estimate=small_cost,
        name="partial_rows",
    )(rows, w_down)


def expert_kernel(ks, with_base, n_z, n_dp, capacity, slots, place, rows_ref, w_ref, *refs):
    out_ref, out_s, sem = refs[-3:]
    step, steps = pl.program_id(0), out_s.shape[0]
    width = out_s.shape[-1]
    blocks = [(q, k) for q in range(2 * n_dp) for k in ks]
    result = lax.dot_general(
        rows_ref[...], w_ref[0], (((1,), (1,)), ((), ())), preferred_element_type=jnp.float32
    )
    if with_base:
        result = result + refs[0][...].astype(jnp.float32)
    for i in range(len(blocks)):
        out_s[step, i] = result[i * capacity : i * capacity + slots].astype(jnp.bfloat16)

    def copies(at):
        z = place[0]
        for i, (q, k) in enumerate(blocks):
            source = (q // 2) * (2 * n_z) + (z ^ k) * 2 + q % 2
            lanes = pl.ds(pl.multiple_of(at * width, width), width)
            yield pltpu.make_async_copy(
                out_s.at[at, i], out_ref.at[0, source, :, lanes], sem.at[at, i]
            )

    for copy in copies(step):
        copy.start()

    @pl.when(step == steps - 1)
    def _():
        for at in range(steps):
            for copy in copies(at):
                copy.wait()


def expert_rows(place, rows, ks, w_down, n_z, n_dp, capacity, slots, base, hidden_grad, after=()):
    hid = w_down.shape[1]
    step = math.gcd(hid, 512)
    count = rows.shape[0] // capacity
    part = w_down.shape[2] // rows.shape[1] - 1
    extra = [] if base is None else [base]
    held = [] if hidden_grad is None else [hidden_grad]
    return pl.pallas_call(
        functools.partial(expert_kernel, ks, bool(extra), n_z, n_dp, capacity, slots),
        grid=(hid // step,),
        in_specs=[
            pl.BlockSpec(memory_space=pltpu.SMEM),
            pl.BlockSpec(rows.shape, lambda n: (0, 0)),
            pl.BlockSpec((1, step, rows.shape[1]), lambda n: (0, n, part)),
        ]
        + [pl.BlockSpec((rows.shape[0], step), lambda n: (0, n))] * len(extra)
        + [pl.BlockSpec(memory_space=pl.ANY)] * (len(held) + len(after)),
        out_specs=pl.BlockSpec(memory_space=pl.ANY),
        out_shape=jax.ShapeDtypeStruct((1, n_dp * 2 * n_z, slots, hid), jnp.bfloat16),
        scratch_shapes=[
            pltpu.VMEM((hid // step, count, slots, step), jnp.bfloat16),
            pltpu.SemaphoreType.DMA((hid // step, count)),
        ],
        input_output_aliases={3 + len(extra): 0} if held else {},
        compiler_params=pltpu.CompilerParams(vmem_limit_bytes=vmem_limit),
        cost_estimate=small_cost,
        name="expert_rows",
    )(place, rows, w_down, *extra, *held, *after)


def per_device(queries, keys, values, out_grad, mixed_grad, expert_ids, combine, w_down):
    rows_dev = queries.shape[1]
    kv_local = keys.shape[2] // HEAD_DIM
    n_ctx, n_dp = lax.axis_size("ctx"), lax.axis_size("dp")
    n_z = n_ctx // 2
    position = lax.axis_index("ctx")
    place = jnp.stack([position >> 1, position & 1]).astype(jnp.int32)
    token_rows = expert_ids.shape[0]
    experts_all = n_dp * n_ctx
    slots = min(
        token_rows,
        max(
            2,
            token_rows * TOPK * 5 // (4 * experts_all),
            (token_rows * TOPK + experts_all - 1) // experts_all,
        ),
    )
    capacity = -(-slots // 8) * 8
    full_rows = mixed_grad
    if lax.axis_size("tp") > 1:
        full_rows = lax.all_gather(mixed_grad, "tp", axis=1, tiled=True)
    own = join(keys, values)
    own_halves = list(halves(full_rows, expert_ids, combine, n_z, n_dp, own))

    def along_z(array, targets):
        pairs = [(2 * i + x, 2 * j + x) for i, j in targets for x in range(2)]
        return lax.ppermute(array, "ctx", pairs)

    def pick(table, array, ks, after):
        block = token_rows if array.shape[0] % own_halves[0].shape[0] else own_halves[0].shape[0]
        sizes = (ks, token_rows, n_dp, capacity)
        return pick_rows(place, table, own_halves[0].shape[0], array, block, *sizes, after)

    def across_x(k):
        pairs = [(i, i ^ 1) for i in range(2 * k, n_ctx) if k > 0 or i % 2 == 0]
        return lax.ppermute(columns[k], "ctx", pairs)

    columns, others = [own], []
    for k in range(1, n_z):
        others.append(across_x(k - 1))
        if k == 2:
            columns[-1], own_halves[0] = lax.optimization_barrier((columns[-1], own_halves[0]))
            own_picked = pick(own_halves[0], full_rows, (0,), (columns[1],))
        if k > 2:
            held = lax.optimization_barrier((columns[-1], *others[k - 3 : k - 1]))
            columns[-1], *others[k - 3 : k - 1] = held
        if k == n_z - 1:
            columns[-1], own_picked = lax.optimization_barrier((columns[-1], own_picked))
        columns.append(along_z(columns[-1], [(i, i + 1) for i in range(k - 1, n_z - 1)]))
    columns[-1], others[-1] = lax.optimization_barrier((columns[-1], others[-1]))
    first_half, columns[-1] = lax.optimization_barrier((own_halves[0], columns[-1]))
    others.append(across_x(n_z - 1))
    blocks = [block for pair in zip(columns, others) for block in pair]

    plane_groups = [
        [d * n_ctx + 2 * i + j for d in range(n_dp) for j in range(2)] for i in range(n_z)
    ]
    line_groups = [[2 * i + x for i in range(n_z)] for x in range(2)]
    last_half, columns[n_z - 1] = lax.optimization_barrier((own_halves[1], columns[n_z - 1]))
    all_halves = [
        lax.all_gather(half, "ctx", axis=0, tiled=True, axis_index_groups=line_groups)
        for half in (first_half, last_half)
    ]

    def exchange(picked):
        return lax.all_to_all(
            picked,
            ("dp", "ctx"),
            split_axis=0,
            concat_axis=0,
            tiled=True,
            axis_index_groups=plane_groups,
        )

    def cross(array):
        return lax.ppermute(array, "ctx", [(i, i ^ 1) for i in range(n_ctx)])

    rest = tuple(range(1, n_z))
    own_picked, columns[n_z - 1] = lax.optimization_barrier((own_picked, columns[n_z - 1]))
    got_own = exchange(own_picked)
    query_grad, parts, after = None, [], (own_picked,)
    for g in range(kv_local):
        query_grad, mine, other = attention(
            place, queries[0], out_grad[0], blocks, g, 1, query_grad, after
        )
        parts.append((mine, cross(other)))
        after = ()
    crossed = [got for _, got in parts[:-1]]
    picked = pick(all_halves[0], all_halves[0], rest, (query_grad, *crossed))
    mines = [mine for mine, _ in parts]
    picked, *crossed = lax.optimization_barrier((picked, *[got for _, got in parts]))
    got_first = exchange(picked)
    picked = pick(all_halves[0], all_halves[1], rest, (picked,))
    got_last = exchange(picked)
    total = lax.psum_scatter(
        fold(list(zip(mines, crossed))),
        "ctx",
        scatter_dimension=0,
        tiled=True,
        axis_index_groups=line_groups,
    )
    sizes = (n_z, n_dp, capacity, slots)
    hidden_grad = expert_rows(place, got_own, (0,), w_down, *sizes, None, None, (picked,))
    base = partial_rows(got_first, w_down)
    key_grad, value_grad = finish(total, base)
    hidden_grad = expert_rows(
        place, got_last, rest, w_down, *sizes, base, hidden_grad, (key_grad,)
    )
    return (query_grad[None], key_grad, value_grad, hidden_grad)


def solution(mesh):
    placed = (
        P("dp", "ctx", "tp"),
        P("dp", "ctx", "tp"),
        P("dp", "ctx", "tp"),
        P("dp", "ctx", "tp"),
        P(("dp", "ctx"), "tp"),
        P(("dp", "ctx"), None),
        P(("dp", "ctx"), None),
        P(("dp", "ctx"), "tp", None),
    )
    return jax.shard_map(
        per_device,
        mesh=mesh,
        in_specs=placed,
        out_specs=(
            P("dp", "ctx", "tp"),
            P("dp", "ctx", "tp"),
            P("dp", "ctx", "tp"),
            P(("dp", "ctx"), None, None, "tp"),
        ),
        check_vma=False,
    )
```

```python
import functools
import math

import jax
import jax.numpy as jnp
from jax import lax
from jax.experimental import pallas as pl
from jax.experimental.pallas import tpu as pltpu
from jax.sharding import PartitionSpec as P

HEADS = 32
KV_HEADS = 4
HEAD_DIM = 128
TOPK = 8

masked_score = -1e30
vmem_limit = 56 * 1024 * 1024
small_cost = pl.CostEstimate(flops=1, bytes_accessed=1, transcendentals=0)


def mul(a, b):
    return jnp.dot(a, b, preferred_element_type=jnp.float32)


def attention_kernel(n_blocks, heads_step, rows, n_parts, place, q_ref, do_ref, *refs):
    kv_refs = refs[:n_blocks]
    dq_ref, mine_ref, other_ref = refs[-13:-10]
    kv_s, kt_s, q_s, do_s, qt_s, dot_s, s_s, dp_s, dkv_s, dqt_s = refs[-10:]
    part = pl.program_id(1)
    pair = 2 * rows
    width = heads_step * rows
    z, x = place[0], place[1]
    scale = HEAD_DIM ** (-0.5)
    to_exp2 = scale * math.log2(math.e)
    for i, ref in enumerate(kv_refs):
        kv_s[i * rows : (i + 1) * rows, :] = ref[...]
        kt_s[i // 4, :, (i % 4) * rows : (i % 4 + 1) * rows] = ref[:, :HEAD_DIM].T
    for h in range(heads_step):
        lanes = slice(h * HEAD_DIM, (h + 1) * HEAD_DIM)
        here = slice(h * rows, (h + 1) * rows)
        q_s[here, :] = q_ref[:, lanes]
        do_s[here, :] = do_ref[:, lanes]
        qt_s[:, here] = q_ref[:, lanes].T
        dot_s[:, here] = do_ref[:, lanes].T

    def part_of(k):
        return pl.ds(pl.multiple_of(k * 2 * pair, 2 * pair), 2 * pair)

    cut = math.gcd(width, 256)
    slices = [slice(i, i + cut) for i in range(0, width, cut)]

    def scores(k, tops, first):
        results = []
        for here, top in zip(slices, tops):
            s = mul(kv_s[part_of(k), :HEAD_DIM], qt_s[:, here])
            if first:
                key = lax.broadcasted_iota(jnp.int32, (pair, cut), 0)
                query = lax.broadcasted_iota(jnp.int32, (pair, cut), 1) & (rows - 1)
                bound = jnp.where(key < rows, query, jnp.where(x == 1, pair, -1))
                head = jnp.where(key <= bound, s[:pair], masked_score)
            else:
                head = s[:pair]
            tail = jnp.where(2 * k + 1 <= z, s[pair:], masked_score)
            s = jnp.concatenate([head, tail], axis=0)
            s_s[part_of(k), here] = s
            results.append(jnp.maximum(top, jnp.max(s, axis=0, keepdims=True)))
        return tuple(results)

    tops = scores(0, tuple(jnp.full((1, cut), masked_score, jnp.float32) for _ in slices), True)
    chunks = lax.div(z, 2) + 1
    tops = lax.fori_loop(1, chunks, functools.partial(scores, first=False), tops)

    def sums(k, carry):
        results = []
        for here, top, (total, accum) in zip(slices, tops, carry):
            dp = mul(kv_s[part_of(k), HEAD_DIM:], dot_s[:, here])
            e = jnp.exp2((s_s[part_of(k), here] - top) * to_exp2)
            s_s[part_of(k), here] = e
            dp_s[part_of(k), here] = dp
            results.append(
                (
                    total + jnp.sum(e, axis=0, keepdims=True),
                    accum + jnp.sum(e * dp, axis=0, keepdims=True),
                )
            )
        return tuple(results)

    zero = jnp.zeros((1, cut), jnp.float32)
    stats = lax.fori_loop(0, chunks, sums, tuple((zero, zero) for _ in slices))
    shares = [1.0 / total for total, _ in stats]
    deltas = [accum * share for (_, accum), share in zip(stats, shares)]
    dqt_s[...] = jnp.zeros_like(dqt_s)

    def grads(k, carry):
        dk = jnp.zeros((2 * pair, HEAD_DIM), jnp.float32)
        dv = jnp.zeros((2 * pair, HEAD_DIM), jnp.float32)
        for here, share, delta in zip(slices, shares, deltas):
            p = s_s[part_of(k), here] * share
            ds = (p * (dp_s[part_of(k), here] - delta)).astype(jnp.bfloat16)
            dv = dv + mul(p.astype(jnp.bfloat16), do_s[here, :])
            dk = dk + mul(ds, q_s[here, :])
            dqt_s[:, here] += mul(kt_s[k], ds)
        dk = dk * scale
        if n_parts > 1:
            dk = dk + jnp.where(part == 0, 0.0, dkv_s[part_of(k), :HEAD_DIM])
            dv = dv + jnp.where(part == 0, 0.0, dkv_s[part_of(k), HEAD_DIM:])
        dkv_s[part_of(k), :HEAD_DIM] = dk
        dkv_s[part_of(k), HEAD_DIM:] = dv
        return carry

    lax.fori_loop(0, chunks, grads, 0)
    for h in range(heads_step):
        part_t = dqt_s[:, h * rows : (h + 1) * rows] * scale
        dq_ref[:, h * HEAD_DIM : (h + 1) * HEAD_DIM] = part_t.T.astype(jnp.bfloat16)
    for i in range(n_blocks):
        held = dkv_s[i * rows : (i + 1) * rows, :]
        ref = mine_ref if i % 2 == 0 else other_ref
        at = lax.rem(z - i // 2 + n_blocks // 2, n_blocks // 2) * rows
        held = jnp.where(i // 2 <= z, held, 0.0).astype(jnp.bfloat16)
        ref[pl.ds(pl.multiple_of(at, rows), rows), :] = held


def attention(place, queries, out_grad, kv_blocks, first, count, query_grad, after=()):
    rows, q_width = queries.shape
    n_blocks = len(kv_blocks)
    group = HEADS // KV_HEADS
    keys = n_blocks * rows
    heads_step = max(1, min(group, 2**20 // (keys * rows)))
    n_parts = group // heads_step
    width = heads_step * rows
    q_spec = pl.BlockSpec(
        (rows, heads_step * HEAD_DIM), lambda g, u: (0, (g + first) * n_parts + u)
    )
    kv_spec = pl.BlockSpec((rows, 2 * HEAD_DIM), lambda g, u: (0, g + first))
    part_spec = pl.BlockSpec((keys // 2, 2 * HEAD_DIM), lambda g, u: (0, g))
    part_shape = jax.ShapeDtypeStruct((keys // 2, count * 2 * HEAD_DIM), jnp.bfloat16)
    held = [] if query_grad is None else [query_grad]
    return pl.pallas_call(
        functools.partial(attention_kernel, n_blocks, heads_step, rows, n_parts),
        grid=(count, n_parts),
        in_specs=[pl.BlockSpec(memory_space=pltpu.SMEM), q_spec, q_spec]
        + [kv_spec] * n_blocks
        + [pl.BlockSpec(memory_space=pl.ANY)] * (len(held) + len(after)),
        out_specs=[q_spec, part_spec, part_spec],
        out_shape=[jax.ShapeDtypeStruct((rows, q_width), jnp.bfloat16), part_shape, part_shape],
        scratch_shapes=[
            pltpu.VMEM((keys, 2 * HEAD_DIM), jnp.bfloat16),
            pltpu.VMEM((n_blocks // 4, HEAD_DIM, 4 * rows), jnp.bfloat16),
            pltpu.VMEM((width, HEAD_DIM), jnp.bfloat16),
            pltpu.VMEM((width, HEAD_DIM), jnp.bfloat16),
            pltpu.VMEM((HEAD_DIM, width), jnp.bfloat16),
            pltpu.VMEM((HEAD_DIM, width), jnp.bfloat16),
            pltpu.VMEM((keys, width), jnp.float32),
            pltpu.VMEM((keys, width), jnp.float32),
            pltpu.VMEM((keys, 2 * HEAD_DIM), jnp.float32),
            pltpu.VMEM((HEAD_DIM, width), jnp.float32),
        ],
        input_output_aliases={3 + n_blocks: 0} if held else {},
        compiler_params=pltpu.CompilerParams(
            vmem_limit_bytes=vmem_limit, dimension_semantics=("arbitrary", "arbitrary")
        ),
        cost_estimate=small_cost
        if held
        else pl.CostEstimate(
            flops=100 * rows * keys * group * count * HEAD_DIM,
            bytes_accessed=8 * (rows * group + keys) * count * HEAD_DIM,
            transcendentals=rows * keys * group * count,
        ),
        name="attention_backward",
    )(place, queries, out_grad, *kv_blocks, *held, *after)


def fold_kernel(mine_ref, *refs):
    out_ref, width = refs[-1], mine_ref.shape[1]
    total = mine_ref[...].astype(jnp.float32) + refs[0][...].astype(jnp.float32)
    out_ref[:, :width] = total.astype(out_ref.dtype)
    first = width
    for ref in refs[1:-1]:
        out_ref[:, first : first + ref.shape[1]] = ref[...]
        first += ref.shape[1]


def fold(mine, got, others):
    arrays = (mine, got, *others)
    rows, width = mine.shape[0], sum(part.shape[1] for part in arrays[1:])
    return pl.pallas_call(
        fold_kernel,
        grid=(4,),
        in_specs=[pl.BlockSpec((rows // 4, part.shape[1]), lambda i: (i, 0)) for part in arrays],
        out_specs=pl.BlockSpec((rows // 4, width), lambda i: (i, 0)),
        out_shape=jax.ShapeDtypeStruct((rows, width), jnp.bfloat16),
        compiler_params=pltpu.CompilerParams(vmem_limit_bytes=vmem_limit),
        cost_estimate=small_cost,
        name="fold",
    )(*arrays)


def finish_kernel(counts, total_ref, *refs):
    key_ref, value_ref = refs[-2:]
    size = 2 * HEAD_DIM
    for g in range(sum(counts)):
        lanes = slice(g * HEAD_DIM, (g + 1) * HEAD_DIM)
        held = total_ref[:, g * size : (g + 1) * size]
        if g >= counts[0]:
            at = (g - counts[0]) * size
            held = held.astype(jnp.float32) + refs[0][:, at : at + size].astype(jnp.float32)
            held = held.astype(jnp.bfloat16)
        key_ref[0, :, lanes] = held[:, :HEAD_DIM]
        value_ref[0, :, lanes] = held[:, HEAD_DIM:]


def finish(counts, total, crossed, after):
    shape = jax.ShapeDtypeStruct((1, total.shape[0], sum(counts) * HEAD_DIM), jnp.bfloat16)
    return pl.pallas_call(
        functools.partial(finish_kernel, counts),
        in_specs=[pl.BlockSpec(memory_space=pltpu.VMEM)] * (1 + len(crossed))
        + [pl.BlockSpec(memory_space=pl.ANY)],
        out_shape=[shape, shape],
        compiler_params=pltpu.CompilerParams(vmem_limit_bytes=vmem_limit),
        cost_estimate=small_cost,
        name="finish",
    )(total, *crossed, after)


def join_kernel(key_ref, value_ref, kv_ref):
    for g in range(kv_ref.shape[1] // (2 * HEAD_DIM)):
        lanes = slice(g * HEAD_DIM, (g + 1) * HEAD_DIM)
        kv_ref[:, 2 * g * HEAD_DIM : (2 * g + 1) * HEAD_DIM] = key_ref[0, :, lanes]
        kv_ref[:, (2 * g + 1) * HEAD_DIM : (2 * g + 2) * HEAD_DIM] = value_ref[0, :, lanes]


def join(keys, values):
    rows, width = keys.shape[1:]
    return pl.pallas_call(
        join_kernel,
        out_shape=jax.ShapeDtypeStruct((rows, 2 * width), jnp.bfloat16),
        compiler_params=pltpu.CompilerParams(vmem_limit_bytes=vmem_limit),
        cost_estimate=small_cost,
        name="join",
    )(keys, values)


def table_kernel(n_z, n_dp, rows_ref, ids_ref, combine_ref, *refs):
    ext_ref, rest_ref = refs[-2:]
    tokens, feat = rows_ref.shape
    lines = 4 * n_dp
    line = lax.broadcasted_iota(jnp.int32, (n_z * lines, tokens), 0)
    kind = line % lines
    member = kind % (2 * n_dp)
    expert = (member // 2) * (2 * n_z) + line // lines * 2 + member % 2
    hits = jnp.zeros((n_z * lines, tokens), jnp.float32)
    weights = jnp.zeros((n_z * lines, tokens), jnp.float32)
    combine = combine_ref[...].astype(jnp.float32)
    for k in range(TOPK):
        hit = ids_ref[k : k + 1, :] == expert
        hits = hits + jnp.where(hit, 1.0, 0.0)
        weights = weights + jnp.where(hit, combine[k : k + 1, :], 0.0)
    before = lax.broadcasted_iota(jnp.int32, (tokens, tokens), 0) < lax.broadcasted_iota(
        jnp.int32, (tokens, tokens), 1
    )
    ranks = mul(hits.astype(jnp.bfloat16), jnp.where(before, 1.0, 0.0).astype(jnp.bfloat16))
    table = jnp.where(kind < 2 * n_dp, jnp.where(hits > 0.0, ranks, -1.0), weights)
    half = feat // 2
    ext_ref[:tokens, :] = rows_ref[:, :half]
    rest_ref[...] = rows_ref[:, half:]
    squares = [table[i * lines : (i + 1) * lines] for i in range(n_z)]
    per_row = half // tokens
    squares += [jnp.zeros((lines, tokens), jnp.float32)] * (-n_z % per_row)
    for i in range(len(squares) // per_row):
        line_of = jnp.concatenate(squares[i * per_row : (i + 1) * per_row], axis=1)
        here = slice(tokens + i * lines, tokens + (i + 1) * lines)
        ext_ref[here, :] = line_of.astype(jnp.bfloat16)


def halves(full_rows, ids, combine, n_z, n_dp, after):
    tokens, feat = full_rows.shape
    return pl.pallas_call(
        functools.partial(table_kernel, n_z, n_dp),
        in_specs=[pl.BlockSpec(memory_space=pltpu.VMEM)] * 3 + [pl.BlockSpec(memory_space=pl.ANY)],
        out_shape=[
            jax.ShapeDtypeStruct(
                (tokens + 4 * n_dp * -(-2 * n_z * tokens // feat), feat // 2), jnp.bfloat16
            ),
            jax.ShapeDtypeStruct((tokens, feat // 2), jnp.bfloat16),
        ],
        compiler_params=pltpu.CompilerParams(vmem_limit_bytes=vmem_limit),
        cost_estimate=small_cost,
        name="slot_table",
    )(full_rows, ids.T, combine.T, after)


def pick_kernel(count, n_dp, capacity, place, *refs):
    table_refs, row_refs = refs[:count], refs[count : 2 * count]
    out_ref, pick_s = refs[-2:]
    tokens = pick_s.shape[2]

    @pl.when(pl.program_id(0) == 0)
    def _():
        for i, ref in enumerate(table_refs):
            table = ref[...].astype(jnp.float32)
            slot = lax.broadcasted_iota(jnp.int32, (capacity, tokens), 0).astype(jnp.float32)
            picks = [
                jnp.where(
                    slot == table[q : q + 1, :], table[2 * n_dp + q : 2 * n_dp + q + 1, :], 0.0
                )
                for q in range(2 * n_dp)
            ]
            pick_s[i] = jnp.concatenate(picks, axis=0).astype(jnp.bfloat16)

    results = [mul(pick_s[i], ref[:tokens, :]) for i, ref in enumerate(row_refs)]
    for q in range(2 * n_dp):
        here = slice(q * capacity, (q + 1) * capacity)
        total = jnp.concatenate([part[here] for part in results], axis=0)
        size = count * capacity
        out_ref[q * size : (q + 1) * size, :] = total.astype(jnp.bfloat16)


def pick_rows(place, table, block_table, array, block, ks, tokens, n_dp, capacity, after=()):
    lines, feat = 4 * n_dp, array.shape[1]
    step = math.gcd(feat, 1024 if len(ks) == 1 else 512)
    out_rows = len(ks) * 2 * n_dp * capacity
    per_row = table.shape[1] // tokens

    def at(place, k, whole, part):
        return (place[0] & (whole.shape[0] // part - 1)) ^ k

    def table_spec(k):
        def index(f, place):
            first = (at(place, k, table, block_table) * block_table + tokens) // lines
            return first + place[0] // per_row, place[0] % per_row

        return pl.BlockSpec((lines, tokens), index)

    def rows_spec(k):
        return pl.BlockSpec((block, step), lambda f, place: (at(place, k, array, block), f))

    return pl.pallas_call(
        functools.partial(pick_kernel, len(ks), n_dp, capacity),
        grid_spec=pltpu.PrefetchScalarGridSpec(
            num_scalar_prefetch=1,
            grid=(feat // step,),
            in_specs=[table_spec(k) for k in ks]
            + [rows_spec(k) for k in ks]
            + [pl.BlockSpec(memory_space=pl.ANY)] * len(after),
            out_specs=pl.BlockSpec((out_rows, step), lambda f, place: (0, f)),
            scratch_shapes=[pltpu.VMEM((len(ks), 2 * n_dp * capacity, tokens), jnp.bfloat16)],
        ),
        out_shape=jax.ShapeDtypeStruct((out_rows, feat), jnp.bfloat16),
        compiler_params=pltpu.CompilerParams(vmem_limit_bytes=vmem_limit),
        cost_estimate=small_cost,
        name="pick_rows",
    )(place, *[table] * len(ks), *[array] * len(ks), *after)


def partial_kernel(rows_ref, w_ref, out_ref):
    out_ref[...] = lax.dot_general(
        rows_ref[...], w_ref[0], (((1,), (1,)), ((), ())), preferred_element_type=jnp.float32
    ).astype(jnp.bfloat16)


def partial_rows(rows, w_down):
    count, half = rows.shape
    hid = w_down.shape[1]
    step = math.gcd(hid, 512)
    return pl.pallas_call(
        partial_kernel,
        grid=(hid // step,),
        in_specs=[
            pl.BlockSpec((count, half), lambda n: (0, 0)),
            pl.BlockSpec((1, step, half), lambda n: (0, n, 0)),
        ],
        out_specs=pl.BlockSpec((count, step), lambda n: (0, n)),
        out_shape=jax.ShapeDtypeStruct((count, hid), jnp.bfloat16),
        compiler_params=pltpu.CompilerParams(vmem_limit_bytes=vmem_limit),
        cost_estimate=small_cost,
        name="partial_rows",
    )(rows, w_down)


def expert_kernel(ks, with_base, n_z, n_dp, capacity, slots, place, rows_ref, w_ref, *refs):
    out_ref, out_s, sem = refs[-3:]
    step, steps = pl.program_id(0), out_s.shape[0]
    width = out_s.shape[-1]
    blocks = [(q, k) for q in range(2 * n_dp) for k in ks]
    result = lax.dot_general(
        rows_ref[...], w_ref[0], (((1,), (1,)), ((), ())), preferred_element_type=jnp.float32
    )
    if with_base:
        result = result + refs[0][...].astype(jnp.float32)
    for i in range(len(blocks)):
        out_s[step, i] = result[i * capacity : i * capacity + slots].astype(jnp.bfloat16)

    def copies(at):
        z = place[0]
        for i, (q, k) in enumerate(blocks):
            source = (q // 2) * (2 * n_z) + (z ^ k) * 2 + q % 2
            lanes = pl.ds(pl.multiple_of(at * width, width), width)
            yield pltpu.make_async_copy(
                out_s.at[at, i], out_ref.at[0, source, :, lanes], sem.at[at, i]
            )

    for copy in copies(step):
        copy.start()

    @pl.when(step == steps - 1)
    def _():
        for at in range(steps):
            for copy in copies(at):
                copy.wait()


def expert_rows(place, rows, ks, w_down, n_z, n_dp, capacity, slots, base, hidden_grad, after=()):
    hid = w_down.shape[1]
    step = math.gcd(hid, 512)
    count = rows.shape[0] // capacity
    part = w_down.shape[2] // rows.shape[1] - 1
    extra = [] if base is None else [base]
    held = [] if hidden_grad is None else [hidden_grad]
    return pl.pallas_call(
        functools.partial(expert_kernel, ks, bool(extra), n_z, n_dp, capacity, slots),
        grid=(hid // step,),
        in_specs=[
            pl.BlockSpec(memory_space=pltpu.SMEM),
            pl.BlockSpec(rows.shape, lambda n: (0, 0)),
            pl.BlockSpec((1, step, rows.shape[1]), lambda n: (0, n, part)),
        ]
        + [pl.BlockSpec((rows.shape[0], step), lambda n: (0, n))] * len(extra)
        + [pl.BlockSpec(memory_space=pl.ANY)] * (len(held) + len(after)),
        out_specs=pl.BlockSpec(memory_space=pl.ANY),
        out_shape=jax.ShapeDtypeStruct((1, n_dp * 2 * n_z, slots, hid), jnp.bfloat16),
        scratch_shapes=[
            pltpu.VMEM((hid // step, count, slots, step), jnp.bfloat16),
            pltpu.SemaphoreType.DMA((hid // step, count)),
        ],
        input_output_aliases={3 + len(extra): 0} if held else {},
        compiler_params=pltpu.CompilerParams(vmem_limit_bytes=vmem_limit),
        cost_estimate=small_cost,
        name="expert_rows",
    )(place, rows, w_down, *extra, *held, *after)


def per_device(queries, keys, values, out_grad, mixed_grad, expert_ids, combine, w_down):
    rows_dev = queries.shape[1]
    kv_local = keys.shape[2] // HEAD_DIM
    n_ctx, n_dp = lax.axis_size("ctx"), lax.axis_size("dp")
    n_z = n_ctx // 2
    position = lax.axis_index("ctx")
    place = jnp.stack([position >> 1, position & 1]).astype(jnp.int32)
    token_rows = expert_ids.shape[0]
    experts_all = n_dp * n_ctx
    slots = min(
        token_rows,
        max(
            2,
            token_rows * TOPK * 5 // (4 * experts_all),
            (token_rows * TOPK + experts_all - 1) // experts_all,
        ),
    )
    capacity = -(-slots // 8) * 8
    full_rows = mixed_grad
    if lax.axis_size("tp") > 1:
        full_rows = lax.all_gather(mixed_grad, "tp", axis=1, tiled=True)
    own = join(keys, values)
    own_halves = list(halves(full_rows, expert_ids, combine, n_z, n_dp, own))

    def along_z(array, targets):
        pairs = [(2 * i + x, 2 * j + x) for i, j in targets for x in range(2)]
        return lax.ppermute(array, "ctx", pairs)

    def pick(table, array, ks, after):
        block = token_rows if array.shape[0] % own_halves[0].shape[0] else own_halves[0].shape[0]
        sizes = (ks, token_rows, n_dp, capacity)
        return pick_rows(place, table, own_halves[0].shape[0], array, block, *sizes, after)

    def across_x(k):
        pairs = [(i, i ^ 1) for i in range(2 * k, n_ctx) if k > 0 or i % 2 == 0]
        return lax.ppermute(columns[k], "ctx", pairs)

    columns, others = [own], []
    for k in range(1, n_z):
        others.append(across_x(k - 1))
        if k == 2:
            columns[-1], own_halves[0] = lax.optimization_barrier((columns[-1], own_halves[0]))
            own_picked = pick(own_halves[0], full_rows, (0,), (columns[1],))
        if k > 2:
            held = lax.optimization_barrier((columns[-1], *others[k - 3 : k - 1]))
            columns[-1], *others[k - 3 : k - 1] = held
        if k == n_z - 1:
            columns[-1], own_picked = lax.optimization_barrier((columns[-1], own_picked))
        columns.append(along_z(columns[-1], [(i, i + 1) for i in range(k - 1, n_z - 1)]))
    columns[-1], others[-1] = lax.optimization_barrier((columns[-1], others[-1]))
    first_half, columns[n_z // 2] = lax.optimization_barrier((own_halves[0], columns[n_z // 2]))
    others.append(across_x(n_z - 1))
    blocks = [block for pair in zip(columns, others) for block in pair]

    plane_groups = [
        [d * n_ctx + 2 * i + j for d in range(n_dp) for j in range(2)] for i in range(n_z)
    ]
    line_groups = [[2 * i + x for i in range(n_z)] for x in range(2)]
    last_half, columns[n_z - 1] = lax.optimization_barrier((own_halves[1], columns[n_z - 1]))
    all_halves = [
        lax.all_gather(half, "ctx", axis=0, tiled=True, axis_index_groups=line_groups)
        for half in (first_half, last_half)
    ]

    def exchange(picked):
        return lax.all_to_all(
            picked,
            ("dp", "ctx"),
            split_axis=0,
            concat_axis=0,
            tiled=True,
            axis_index_groups=plane_groups,
        )

    def cross(array):
        return lax.ppermute(array, "ctx", [(i, i ^ 1) for i in range(n_ctx)])

    counts = [1] if kv_local == 1 else [kv_local // 2, kv_local - kv_local // 2]
    rest = tuple(range(1, n_z))
    own_picked, columns[n_z - 1] = lax.optimization_barrier((own_picked, columns[n_z - 1]))
    got_own = exchange(own_picked)
    query_grad, mine, other = attention(
        place, queries[0], out_grad[0], blocks, 0, counts[0], None, (own_picked,)
    )
    crossed = cross(other)
    others = []
    if len(counts) > 1:
        query_grad, *others = attention(
            place, queries[0], out_grad[0], blocks, counts[0], counts[1], query_grad
        )
    picked = pick(all_halves[0], all_halves[0], rest, (query_grad,))
    picked, crossed = lax.optimization_barrier((picked, crossed))
    got_first = exchange(picked)
    picked = pick(all_halves[0], all_halves[1], rest, (picked,))
    got_last = exchange(picked)
    total = lax.psum_scatter(
        fold(mine, crossed, others),
        "ctx",
        scatter_dimension=0,
        tiled=True,
        axis_index_groups=line_groups,
    )
    sizes = (n_z, n_dp, capacity, slots)
    hidden_grad = expert_rows(place, got_own, (0,), w_down, *sizes, None, None, (picked,))
    base = partial_rows(got_first, w_down)
    total, base, hidden_grad = lax.optimization_barrier((total, base, hidden_grad))
    last = [cross(total[:, -others[1].shape[1] :])] if others else []
    key_grad, value_grad = finish(counts, total, last, base)
    hidden_grad = expert_rows(
        place, got_last, rest, w_down, *sizes, base, hidden_grad, (key_grad,)
    )
    return (query_grad[None], key_grad, value_grad, hidden_grad)


def solution(mesh):
    placed = (
        P("dp", "ctx", "tp"),
        P("dp", "ctx", "tp"),
        P("dp", "ctx", "tp"),
        P("dp", "ctx", "tp"),
        P(("dp", "ctx"), "tp"),
        P(("dp", "ctx"), None),
        P(("dp", "ctx"), None),
        P(("dp", "ctx"), "tp", None),
    )
    return jax.shard_map(
        per_device,
        mesh=mesh,
        in_specs=placed,
        out_specs=(
            P("dp", "ctx", "tp"),
            P("dp", "ctx", "tp"),
            P("dp", "ctx", "tp"),
            P(("dp", "ctx"), None, None, "tp"),
        ),
        check_vma=False,
    )
```

```python
import functools
import math

import jax
import jax.numpy as jnp
from jax import lax
from jax.experimental import pallas as pl
from jax.experimental.pallas import tpu as pltpu
from jax.sharding import PartitionSpec as P

HEADS = 32
KV_HEADS = 4
HEAD_DIM = 128
TOPK = 8

masked_score = -1e30
vmem_limit = 56 * 1024 * 1024
small_cost = pl.CostEstimate(flops=1, bytes_accessed=1, transcendentals=0)


def mul(a, b):
    return jnp.dot(a, b, preferred_element_type=jnp.float32)


def attention_kernel(n_blocks, heads_step, rows, n_parts, place, q_ref, do_ref, *refs):
    kv_refs = refs[:n_blocks]
    dq_ref, mine_ref, other_ref = refs[-13:-10]
    kv_s, kt_s, q_s, do_s, qt_s, dot_s, s_s, dp_s, dkv_s, dqt_s = refs[-10:]
    part = pl.program_id(1)
    pair = 2 * rows
    width = heads_step * rows
    z, x = place[0], place[1]
    scale = HEAD_DIM ** (-0.5)
    to_exp2 = scale * math.log2(math.e)
    for i, ref in enumerate(kv_refs):
        kv_s[i * rows : (i + 1) * rows, :] = ref[...]
        kt_s[i // 4, :, (i % 4) * rows : (i % 4 + 1) * rows] = ref[:, :HEAD_DIM].T
    for h in range(heads_step):
        lanes = slice(h * HEAD_DIM, (h + 1) * HEAD_DIM)
        here = slice(h * rows, (h + 1) * rows)
        q_s[here, :] = q_ref[:, lanes]
        do_s[here, :] = do_ref[:, lanes]
        qt_s[:, here] = q_ref[:, lanes].T
        dot_s[:, here] = do_ref[:, lanes].T

    def part_of(k):
        return pl.ds(pl.multiple_of(k * 2 * pair, 2 * pair), 2 * pair)

    cut = math.gcd(width, 256)
    slices = [slice(i, i + cut) for i in range(0, width, cut)]

    def scores(k, tops, first):
        results = []
        for here, top in zip(slices, tops):
            s = mul(kv_s[part_of(k), :HEAD_DIM], qt_s[:, here])
            if first:
                key = lax.broadcasted_iota(jnp.int32, (pair, cut), 0)
                query = lax.broadcasted_iota(jnp.int32, (pair, cut), 1) & (rows - 1)
                bound = jnp.where(key < rows, query, jnp.where(x == 1, pair, -1))
                head = jnp.where(key <= bound, s[:pair], masked_score)
            else:
                head = s[:pair]
            tail = jnp.where(2 * k + 1 <= z, s[pair:], masked_score)
            s = jnp.concatenate([head, tail], axis=0)
            s_s[part_of(k), here] = s
            results.append(jnp.maximum(top, jnp.max(s, axis=0, keepdims=True)))
        return tuple(results)

    tops = scores(0, tuple(jnp.full((1, cut), masked_score, jnp.float32) for _ in slices), True)
    chunks = lax.div(z, 2) + 1
    tops = lax.fori_loop(1, chunks, functools.partial(scores, first=False), tops)

    def sums(k, carry):
        results = []
        for here, top, (total, accum) in zip(slices, tops, carry):
            dp = mul(kv_s[part_of(k), HEAD_DIM:], dot_s[:, here])
            e = jnp.exp2((s_s[part_of(k), here] - top) * to_exp2)
            s_s[part_of(k), here] = e
            dp_s[part_of(k), here] = dp
            results.append(
                (
                    total + jnp.sum(e, axis=0, keepdims=True),
                    accum + jnp.sum(e * dp, axis=0, keepdims=True),
                )
            )
        return tuple(results)

    zero = jnp.zeros((1, cut), jnp.float32)
    stats = lax.fori_loop(0, chunks, sums, tuple((zero, zero) for _ in slices))
    shares = [1.0 / total for total, _ in stats]
    deltas = [accum * share for (_, accum), share in zip(stats, shares)]
    dqt_s[...] = jnp.zeros_like(dqt_s)

    def grads(k, carry):
        dk = jnp.zeros((2 * pair, HEAD_DIM), jnp.float32)
        dv = jnp.zeros((2 * pair, HEAD_DIM), jnp.float32)
        for here, share, delta in zip(slices, shares, deltas):
            p = s_s[part_of(k), here] * share
            ds = (p * (dp_s[part_of(k), here] - delta)).astype(jnp.bfloat16)
            dv = dv + mul(p.astype(jnp.bfloat16), do_s[here, :])
            dk = dk + mul(ds, q_s[here, :])
            dqt_s[:, here] += mul(kt_s[k], ds)
        dk = dk * scale
        if n_parts > 1:
            dk = dk + jnp.where(part == 0, 0.0, dkv_s[part_of(k), :HEAD_DIM])
            dv = dv + jnp.where(part == 0, 0.0, dkv_s[part_of(k), HEAD_DIM:])
        dkv_s[part_of(k), :HEAD_DIM] = dk
        dkv_s[part_of(k), HEAD_DIM:] = dv
        return carry

    lax.fori_loop(0, chunks, grads, 0)
    for h in range(heads_step):
        part_t = dqt_s[:, h * rows : (h + 1) * rows] * scale
        dq_ref[:, h * HEAD_DIM : (h + 1) * HEAD_DIM] = part_t.T.astype(jnp.bfloat16)
    for i in range(n_blocks):
        held = dkv_s[i * rows : (i + 1) * rows, :]
        ref = mine_ref if i % 2 == 0 else other_ref
        at = lax.rem(z - i // 2 + n_blocks // 2, n_blocks // 2) * rows
        held = jnp.where(i // 2 <= z, held, 0.0).astype(jnp.bfloat16)
        ref[pl.ds(pl.multiple_of(at, rows), rows), :] = held


def attention(place, queries, out_grad, kv_blocks, first, count, query_grad, after=()):
    rows, q_width = queries.shape
    n_blocks = len(kv_blocks)
    group = HEADS // KV_HEADS
    keys = n_blocks * rows
    heads_step = max(1, min(group, 2**20 // (keys * rows)))
    n_parts = group // heads_step
    width = heads_step * rows
    q_spec = pl.BlockSpec(
        (rows, heads_step * HEAD_DIM), lambda g, u: (0, (g + first) * n_parts + u)
    )
    kv_spec = pl.BlockSpec((rows, 2 * HEAD_DIM), lambda g, u: (0, g + first))
    part_spec = pl.BlockSpec((keys // 2, 2 * HEAD_DIM), lambda g, u: (0, g))
    part_shape = jax.ShapeDtypeStruct((keys // 2, count * 2 * HEAD_DIM), jnp.bfloat16)
    held = [] if query_grad is None else [query_grad]
    return pl.pallas_call(
        functools.partial(attention_kernel, n_blocks, heads_step, rows, n_parts),
        grid=(count, n_parts),
        in_specs=[pl.BlockSpec(memory_space=pltpu.SMEM), q_spec, q_spec]
        + [kv_spec] * n_blocks
        + [pl.BlockSpec(memory_space=pl.ANY)] * (len(held) + len(after)),
        out_specs=[q_spec, part_spec, part_spec],
        out_shape=[jax.ShapeDtypeStruct((rows, q_width), jnp.bfloat16), part_shape, part_shape],
        scratch_shapes=[
            pltpu.VMEM((keys, 2 * HEAD_DIM), jnp.bfloat16),
            pltpu.VMEM((n_blocks // 4, HEAD_DIM, 4 * rows), jnp.bfloat16),
            pltpu.VMEM((width, HEAD_DIM), jnp.bfloat16),
            pltpu.VMEM((width, HEAD_DIM), jnp.bfloat16),
            pltpu.VMEM((HEAD_DIM, width), jnp.bfloat16),
            pltpu.VMEM((HEAD_DIM, width), jnp.bfloat16),
            pltpu.VMEM((keys, width), jnp.float32),
            pltpu.VMEM((keys, width), jnp.float32),
            pltpu.VMEM((keys, 2 * HEAD_DIM), jnp.float32),
            pltpu.VMEM((HEAD_DIM, width), jnp.float32),
        ],
        input_output_aliases={3 + n_blocks: 0} if held else {},
        compiler_params=pltpu.CompilerParams(
            vmem_limit_bytes=vmem_limit, dimension_semantics=("arbitrary", "arbitrary")
        ),
        cost_estimate=small_cost
        if held
        else pl.CostEstimate(
            flops=100 * rows * keys * group * count * HEAD_DIM,
            bytes_accessed=8 * (rows * group + keys) * count * HEAD_DIM,
            transcendentals=rows * keys * group * count,
        ),
        name="attention_backward",
    )(place, queries, out_grad, *kv_blocks, *held, *after)


def fold_kernel(mine_ref, *refs):
    out_ref, width = refs[-1], mine_ref.shape[1]
    total = mine_ref[...].astype(jnp.float32) + refs[0][...].astype(jnp.float32)
    out_ref[:, :width] = total.astype(out_ref.dtype)
    first = width
    for ref in refs[1:-1]:
        out_ref[:, first : first + ref.shape[1]] = ref[...]
        first += ref.shape[1]


def fold(mine, got, others):
    arrays = (mine, got, *others)
    rows, width = mine.shape[0], sum(part.shape[1] for part in arrays[1:])
    return pl.pallas_call(
        fold_kernel,
        grid=(4,),
        in_specs=[pl.BlockSpec((rows // 4, part.shape[1]), lambda i: (i, 0)) for part in arrays],
        out_specs=pl.BlockSpec((rows // 4, width), lambda i: (i, 0)),
        out_shape=jax.ShapeDtypeStruct((rows, width), jnp.bfloat16),
        compiler_params=pltpu.CompilerParams(vmem_limit_bytes=vmem_limit),
        cost_estimate=small_cost,
        name="fold",
    )(*arrays)


def finish_kernel(counts, total_ref, *refs):
    key_ref, value_ref = refs[-2:]
    size = 2 * HEAD_DIM
    for g in range(sum(counts)):
        lanes = slice(g * HEAD_DIM, (g + 1) * HEAD_DIM)
        held = total_ref[:, g * size : (g + 1) * size]
        if g >= counts[0]:
            at = (g - counts[0]) * size
            held = held.astype(jnp.float32) + refs[0][:, at : at + size].astype(jnp.float32)
            held = held.astype(jnp.bfloat16)
        key_ref[0, :, lanes] = held[:, :HEAD_DIM]
        value_ref[0, :, lanes] = held[:, HEAD_DIM:]


def finish(counts, total, crossed, after):
    shape = jax.ShapeDtypeStruct((1, total.shape[0], sum(counts) * HEAD_DIM), jnp.bfloat16)
    return pl.pallas_call(
        functools.partial(finish_kernel, counts),
        in_specs=[pl.BlockSpec(memory_space=pltpu.VMEM)] * (1 + len(crossed))
        + [pl.BlockSpec(memory_space=pl.ANY)],
        out_shape=[shape, shape],
        compiler_params=pltpu.CompilerParams(vmem_limit_bytes=vmem_limit),
        cost_estimate=small_cost,
        name="finish",
    )(total, *crossed, after)


def join_kernel(key_ref, value_ref, kv_ref):
    for g in range(kv_ref.shape[1] // (2 * HEAD_DIM)):
        lanes = slice(g * HEAD_DIM, (g + 1) * HEAD_DIM)
        kv_ref[:, 2 * g * HEAD_DIM : (2 * g + 1) * HEAD_DIM] = key_ref[0, :, lanes]
        kv_ref[:, (2 * g + 1) * HEAD_DIM : (2 * g + 2) * HEAD_DIM] = value_ref[0, :, lanes]


def join(keys, values):
    rows, width = keys.shape[1:]
    return pl.pallas_call(
        join_kernel,
        out_shape=jax.ShapeDtypeStruct((rows, 2 * width), jnp.bfloat16),
        compiler_params=pltpu.CompilerParams(vmem_limit_bytes=vmem_limit),
        cost_estimate=small_cost,
        name="join",
    )(keys, values)


def table_kernel(n_z, n_dp, rows_ref, ids_ref, combine_ref, *refs):
    ext_ref, rest_ref = refs[-2:]
    tokens, feat = rows_ref.shape
    lines = 4 * n_dp
    line = lax.broadcasted_iota(jnp.int32, (n_z * lines, tokens), 0)
    kind = line % lines
    member = kind % (2 * n_dp)
    expert = (member // 2) * (2 * n_z) + line // lines * 2 + member % 2
    hits = jnp.zeros((n_z * lines, tokens), jnp.float32)
    weights = jnp.zeros((n_z * lines, tokens), jnp.float32)
    combine = combine_ref[...].astype(jnp.float32)
    for k in range(TOPK):
        hit = ids_ref[k : k + 1, :] == expert
        hits = hits + jnp.where(hit, 1.0, 0.0)
        weights = weights + jnp.where(hit, combine[k : k + 1, :], 0.0)
    before = lax.broadcasted_iota(jnp.int32, (tokens, tokens), 0) < lax.broadcasted_iota(
        jnp.int32, (tokens, tokens), 1
    )
    ranks = mul(hits.astype(jnp.bfloat16), jnp.where(before, 1.0, 0.0).astype(jnp.bfloat16))
    table = jnp.where(kind < 2 * n_dp, jnp.where(hits > 0.0, ranks, -1.0), weights)
    half = feat // 2
    ext_ref[:tokens, :] = rows_ref[:, :half]
    rest_ref[...] = rows_ref[:, half:]
    squares = [table[i * lines : (i + 1) * lines] for i in range(n_z)]
    per_row = half // tokens
    squares += [jnp.zeros((lines, tokens), jnp.float32)] * (-n_z % per_row)
    for i in range(len(squares) // per_row):
        line_of = jnp.concatenate(squares[i * per_row : (i + 1) * per_row], axis=1)
        here = slice(tokens + i * lines, tokens + (i + 1) * lines)
        ext_ref[here, :] = line_of.astype(jnp.bfloat16)


def halves(full_rows, ids, combine, n_z, n_dp, after):
    tokens, feat = full_rows.shape
    return pl.pallas_call(
        functools.partial(table_kernel, n_z, n_dp),
        in_specs=[pl.BlockSpec(memory_space=pltpu.VMEM)] * 3 + [pl.BlockSpec(memory_space=pl.ANY)],
        out_shape=[
            jax.ShapeDtypeStruct(
                (tokens + 4 * n_dp * -(-2 * n_z * tokens // feat), feat // 2), jnp.bfloat16
            ),
            jax.ShapeDtypeStruct((tokens, feat // 2), jnp.bfloat16),
        ],
        compiler_params=pltpu.CompilerParams(vmem_limit_bytes=vmem_limit),
        cost_estimate=small_cost,
        name="slot_table",
    )(full_rows, ids.T, combine.T, after)


def pick_kernel(count, n_dp, capacity, place, *refs):
    table_refs, row_refs = refs[:count], refs[count : 2 * count]
    out_ref, pick_s = refs[-2:]
    tokens = pick_s.shape[2]

    @pl.when(pl.program_id(0) == 0)
    def _():
        for i, ref in enumerate(table_refs):
            table = ref[...].astype(jnp.float32)
            slot = lax.broadcasted_iota(jnp.int32, (capacity, tokens), 0).astype(jnp.float32)
            picks = [
                jnp.where(
                    slot == table[q : q + 1, :], table[2 * n_dp + q : 2 * n_dp + q + 1, :], 0.0
                )
                for q in range(2 * n_dp)
            ]
            pick_s[i] = jnp.concatenate(picks, axis=0).astype(jnp.bfloat16)

    results = [mul(pick_s[i], ref[:tokens, :]) for i, ref in enumerate(row_refs)]
    for q in range(2 * n_dp):
        here = slice(q * capacity, (q + 1) * capacity)
        total = jnp.concatenate([part[here] for part in results], axis=0)
        size = count * capacity
        out_ref[q * size : (q + 1) * size, :] = total.astype(jnp.bfloat16)


def pick_rows(place, table, block_table, array, block, ks, tokens, n_dp, capacity, after=()):
    lines, feat = 4 * n_dp, array.shape[1]
    step = math.gcd(feat, 1024 if len(ks) == 1 else 512)
    out_rows = len(ks) * 2 * n_dp * capacity
    per_row = table.shape[1] // tokens

    def at(place, k, whole, part):
        return (place[0] & (whole.shape[0] // part - 1)) ^ k

    def table_spec(k):
        def index(f, place):
            first = (at(place, k, table, block_table) * block_table + tokens) // lines
            return first + place[0] // per_row, place[0] % per_row

        return pl.BlockSpec((lines, tokens), index)

    def rows_spec(k):
        return pl.BlockSpec((block, step), lambda f, place: (at(place, k, array, block), f))

    return pl.pallas_call(
        functools.partial(pick_kernel, len(ks), n_dp, capacity),
        grid_spec=pltpu.PrefetchScalarGridSpec(
            num_scalar_prefetch=1,
            grid=(feat // step,),
            in_specs=[table_spec(k) for k in ks]
            + [rows_spec(k) for k in ks]
            + [pl.BlockSpec(memory_space=pl.ANY)] * len(after),
            out_specs=pl.BlockSpec((out_rows, step), lambda f, place: (0, f)),
            scratch_shapes=[pltpu.VMEM((len(ks), 2 * n_dp * capacity, tokens), jnp.bfloat16)],
        ),
        out_shape=jax.ShapeDtypeStruct((out_rows, feat), jnp.bfloat16),
        compiler_params=pltpu.CompilerParams(vmem_limit_bytes=vmem_limit),
        cost_estimate=small_cost,
        name="pick_rows",
    )(place, *[table] * len(ks), *[array] * len(ks), *after)


def partial_kernel(rows_ref, w_ref, out_ref):
    out_ref[...] = lax.dot_general(
        rows_ref[...], w_ref[0], (((1,), (1,)), ((), ())), preferred_element_type=jnp.float32
    ).astype(jnp.bfloat16)


def partial_rows(rows, w_down):
    count, half = rows.shape
    hid = w_down.shape[1]
    step = math.gcd(hid, 512)
    return pl.pallas_call(
        partial_kernel,
        grid=(hid // step,),
        in_specs=[
            pl.BlockSpec((count, half), lambda n: (0, 0)),
            pl.BlockSpec((1, step, half), lambda n: (0, n, 0)),
        ],
        out_specs=pl.BlockSpec((count, step), lambda n: (0, n)),
        out_shape=jax.ShapeDtypeStruct((count, hid), jnp.bfloat16),
        compiler_params=pltpu.CompilerParams(vmem_limit_bytes=vmem_limit),
        cost_estimate=small_cost,
        name="partial_rows",
    )(rows, w_down)


def expert_kernel(ks, with_base, n_z, n_dp, capacity, slots, place, rows_ref, w_ref, *refs):
    out_ref, out_s, sem = refs[-3:]
    step, steps = pl.program_id(0), out_s.shape[0]
    width = out_s.shape[-1]
    blocks = [(q, k) for q in range(2 * n_dp) for k in ks]
    result = lax.dot_general(
        rows_ref[...], w_ref[0], (((1,), (1,)), ((), ())), preferred_element_type=jnp.float32
    )
    if with_base:
        result = result + refs[0][...].astype(jnp.float32)
    for i in range(len(blocks)):
        out_s[step, i] = result[i * capacity : i * capacity + slots].astype(jnp.bfloat16)

    def copies(at):
        z = place[0]
        for i, (q, k) in enumerate(blocks):
            source = (q // 2) * (2 * n_z) + (z ^ k) * 2 + q % 2
            lanes = pl.ds(pl.multiple_of(at * width, width), width)
            yield pltpu.make_async_copy(
                out_s.at[at, i], out_ref.at[0, source, :, lanes], sem.at[at, i]
            )

    for copy in copies(step):
        copy.start()

    @pl.when(step == steps - 1)
    def _():
        for at in range(steps):
            for copy in copies(at):
                copy.wait()


def expert_rows(place, rows, ks, w_down, n_z, n_dp, capacity, slots, base, hidden_grad, after=()):
    hid = w_down.shape[1]
    step = math.gcd(hid, 512)
    count = rows.shape[0] // capacity
    part = w_down.shape[2] // rows.shape[1] - 1
    extra = [] if base is None else [base]
    held = [] if hidden_grad is None else [hidden_grad]
    return pl.pallas_call(
        functools.partial(expert_kernel, ks, bool(extra), n_z, n_dp, capacity, slots),
        grid=(hid // step,),
        in_specs=[
            pl.BlockSpec(memory_space=pltpu.SMEM),
            pl.BlockSpec(rows.shape, lambda n: (0, 0)),
            pl.BlockSpec((1, step, rows.shape[1]), lambda n: (0, n, part)),
        ]
        + [pl.BlockSpec((rows.shape[0], step), lambda n: (0, n))] * len(extra)
        + [pl.BlockSpec(memory_space=pl.ANY)] * (len(held) + len(after)),
        out_specs=pl.BlockSpec(memory_space=pl.ANY),
        out_shape=jax.ShapeDtypeStruct((1, n_dp * 2 * n_z, slots, hid), jnp.bfloat16),
        scratch_shapes=[
            pltpu.VMEM((hid // step, count, slots, step), jnp.bfloat16),
            pltpu.SemaphoreType.DMA((hid // step, count)),
        ],
        input_output_aliases={3 + len(extra): 0} if held else {},
        compiler_params=pltpu.CompilerParams(vmem_limit_bytes=vmem_limit),
        cost_estimate=small_cost,
        name="expert_rows",
    )(place, rows, w_down, *extra, *held, *after)


def per_device(queries, keys, values, out_grad, mixed_grad, expert_ids, combine, w_down):
    rows_dev = queries.shape[1]
    kv_local = keys.shape[2] // HEAD_DIM
    n_ctx, n_dp = lax.axis_size("ctx"), lax.axis_size("dp")
    n_z = n_ctx // 2
    position = lax.axis_index("ctx")
    place = jnp.stack([position >> 1, position & 1]).astype(jnp.int32)
    token_rows = expert_ids.shape[0]
    experts_all = n_dp * n_ctx
    slots = min(
        token_rows,
        max(
            2,
            token_rows * TOPK * 5 // (4 * experts_all),
            (token_rows * TOPK + experts_all - 1) // experts_all,
        ),
    )
    capacity = -(-slots // 8) * 8
    full_rows = mixed_grad
    if lax.axis_size("tp") > 1:
        full_rows = lax.all_gather(mixed_grad, "tp", axis=1, tiled=True)
    own = join(keys, values)
    own_halves = list(halves(full_rows, expert_ids, combine, n_z, n_dp, own))

    def along_z(array, targets):
        pairs = [(2 * i + x, 2 * j + x) for i, j in targets for x in range(2)]
        return lax.ppermute(array, "ctx", pairs)

    def pick(table, array, ks, after):
        block = token_rows if array.shape[0] % own_halves[0].shape[0] else own_halves[0].shape[0]
        sizes = (ks, token_rows, n_dp, capacity)
        return pick_rows(place, table, own_halves[0].shape[0], array, block, *sizes, after)

    def across_x(k):
        pairs = [(i, i ^ 1) for i in range(2 * k, n_ctx) if k > 0 or i % 2 == 0]
        return lax.ppermute(columns[k], "ctx", pairs)

    columns, others = [own], []
    for k in range(1, n_z):
        others.append(across_x(k - 1))
        if k == 2:
            columns[-1], own_halves[0] = lax.optimization_barrier((columns[-1], own_halves[0]))
            own_picked = pick(own_halves[0], full_rows, (0,), (columns[1],))
        if k > 2:
            held = lax.optimization_barrier((columns[-1], *others[k - 3 : k - 1]))
            columns[-1], *others[k - 3 : k - 1] = held
        if k == n_z - 1:
            columns[-1], own_picked = lax.optimization_barrier((columns[-1], own_picked))
        columns.append(along_z(columns[-1], [(i, i + 1) for i in range(k - 1, n_z - 1)]))
    columns[-1], others[-1] = lax.optimization_barrier((columns[-1], others[-1]))
    first_half, columns[n_z // 2] = lax.optimization_barrier((own_halves[0], columns[n_z // 2]))
    others.append(across_x(n_z - 1))
    blocks = [block for pair in zip(columns, others) for block in pair]

    plane_groups = [
        [d * n_ctx + 2 * i + j for d in range(n_dp) for j in range(2)] for i in range(n_z)
    ]
    line_groups = [[2 * i + x for i in range(n_z)] for x in range(2)]
    last_half, columns[n_z - 1] = lax.optimization_barrier((own_halves[1], columns[n_z - 1]))
    all_halves = [
        lax.all_gather(half, "ctx", axis=0, tiled=True, axis_index_groups=line_groups)
        for half in (first_half, last_half)
    ]

    def exchange(picked):
        return lax.all_to_all(
            picked,
            ("dp", "ctx"),
            split_axis=0,
            concat_axis=0,
            tiled=True,
            axis_index_groups=plane_groups,
        )

    def cross(array):
        return lax.ppermute(array, "ctx", [(i, i ^ 1) for i in range(n_ctx)])

    counts = [1] if kv_local == 1 else [kv_local // 2, kv_local - kv_local // 2]
    rest = tuple(range(1, n_z))
    own_picked, columns[n_z - 1] = lax.optimization_barrier((own_picked, columns[n_z - 1]))
    got_own = exchange(own_picked)
    query_grad, mine, other = attention(
        place, queries[0], out_grad[0], blocks, 0, counts[0], None, (own_picked,)
    )
    crossed = cross(other)
    picked = pick(all_halves[0], all_halves[0], rest, (query_grad,))
    picked, crossed = lax.optimization_barrier((picked, crossed))
    got_first = exchange(picked)
    others = []
    if len(counts) > 1:
        query_grad, *others = attention(
            place, queries[0], out_grad[0], blocks, counts[0], counts[1], query_grad, (picked,)
        )
    picked = pick(all_halves[0], all_halves[1], rest, (picked,))
    got_last = exchange(picked)
    total = lax.psum_scatter(
        fold(mine, crossed, others),
        "ctx",
        scatter_dimension=0,
        tiled=True,
        axis_index_groups=line_groups,
    )
    sizes = (n_z, n_dp, capacity, slots)
    hidden_grad = expert_rows(place, got_own, (0,), w_down, *sizes, None, None, (picked,))
    base = partial_rows(got_first, w_down)
    total, base, hidden_grad = lax.optimization_barrier((total, base, hidden_grad))
    last = [cross(total[:, -others[1].shape[1] :])] if others else []
    key_grad, value_grad = finish(counts, total, last, base)
    hidden_grad = expert_rows(
        place, got_last, rest, w_down, *sizes, base, hidden_grad, (key_grad,)
    )
    return (query_grad[None], key_grad, value_grad, hidden_grad)


def solution(mesh):
    placed = (
        P("dp", "ctx", "tp"),
        P("dp", "ctx", "tp"),
        P("dp", "ctx", "tp"),
        P("dp", "ctx", "tp"),
        P(("dp", "ctx"), "tp"),
        P(("dp", "ctx"), None),
        P(("dp", "ctx"), None),
        P(("dp", "ctx"), "tp", None),
    )
    return jax.shard_map(
        per_device,
        mesh=mesh,
        in_specs=placed,
        out_specs=(
            P("dp", "ctx", "tp"),
            P("dp", "ctx", "tp"),
            P("dp", "ctx", "tp"),
            P(("dp", "ctx"), None, None, "tp"),
        ),
        check_vma=False,
    )
```
